128 devices in a mesh: fsdp: 128 (over z, x, y, core).
Axes of the slice: x: 4, y: 4, z: 4, core: 2. Of those that a mesh axis runs over, the one named last changes fastest.
Arguments:
- hidden: bfloat16 [16384, 1536], P('fsdp'), may hold values from -6 to 6
- in_weight: bfloat16 [1536, 6448], P('fsdp'), may hold values from -0.15625 to 0.15625
- norm_gain: bfloat16 [1536], P('fsdp'), may hold values from 0.5 to 1.5
- conv_weight: bfloat16 [3328, 4], P('fsdp'), may hold values from -3 to 3
- conv_bias: bfloat16 [3328], P('fsdp'), may hold values from -0.5 to 0.5
- dt_bias: float32 [48], replicated, may hold values from -5 to -2
- a_log: float32 [48], replicated, may hold values from 0 to 2.7
- skip: float32 [48], replicated, may hold values from 0.5 to 1.5
- inner_gain: bfloat16 [3072], P('fsdp'), may hold values from 0.5 to 1.5
- out_weight: bfloat16 [3072, 1536], P('fsdp'), may hold values from -0.109375 to 0.109375
- out_grad: bfloat16 [16384, 1536], P('fsdp'), may hold values from -6 to 6
- seq_lengths: int32 [128], replicated, may hold values from 16 to 128, as said below
- seq_owner: int32 [128], replicated, may hold values from 0 to 127, each once
Outputs:
- mixed: bfloat16 [16384, 1536], P('fsdp')
- in_grad: bfloat16 [16384, 1536], P('fsdp')
- in_weight_grad: float32 [1536, 6448], P('fsdp')
- norm_gain_grad: float32 [1536], P('fsdp')
- conv_weight_grad: float32 [3328, 4], P('fsdp')
- conv_bias_grad: float32 [3328], P('fsdp')
- dt_bias_grad: float32 [48], replicated
- a_log_grad: float32 [48], replicated
- skip_grad: float32 [48], replicated
- inner_gain_grad: float32 [3072], P('fsdp')
- out_weight_grad: float32 [3072, 1536], P('fsdp')
The draws below stay inside these ranges and needn't reach their ends.
Inputs may be any that keep to these rules, and one draw needn't show every extreme that they name: `seq_lengths`: one sequence has exactly 128 tokens. `seq_owner`: each device holds exactly one sequence.
All inputs are finite; a program needn't handle non-finite values.
Results may differ from the reference program's by a relative error of at most 0.007.
Values may be sent and summed in bfloat16 or wider, within the bound.
A program may use at most 192 MiB of HBM per device.

```python
import math
import jax
import jax.numpy as jnp
from jax import lax

D = 1536
NH = 48
TAPS = 4
BLOCK = 128
CAP = 128
INNER = 3072
CONVD = 3328
DIN = 6448
NSEQ = 128
TOKENS = 16384
N_FSDP = 128


def draw_seq_lengths(key, part):
    key = jax.random.fold_in(key, 11)
    first_key, second_key = jax.random.split(key)
    drawn = jax.random.randint(first_key, (NSEQ,), CAP // 8, CAP + 1)
    chosen = jax.random.randint(second_key, (), 0, NSEQ)
    return jnp.where(jnp.arange(NSEQ) == chosen, CAP, drawn).astype(jnp.int32)


def shard_levels(stream_key, dims, cuts, smallest, high):
    level, own = 1.0, jax.random.fold_in(stream_key, 6)
    for axis_at, parts in cuts:
        steps = jnp.exp(jax.random.uniform(jax.random.fold_in(own, axis_at), (parts,), jnp.float32, smallest / len(cuts), high / len(cuts)))
        level = level * jnp.repeat(steps, dims[axis_at] // parts).reshape([-1 if axis == axis_at else 1 for axis in range(len(dims))])
    return level


def centred(own_key, shape, deviation, bound, shards=(), kind=jnp.bfloat16):
    factor_of = shard_levels(own_key, shape, shards, -0.22, 0.18) if shards else 1.0
    values = jax.random.normal(own_key, shape, jnp.float32) * deviation * factor_of
    return jnp.minimum(jnp.maximum(values, -bound), bound).astype(kind)


def setup_inputs(seed: int = 0) -> dict:
    keys = jax.random.split(jax.random.key(seed), 14)
    return {
        "hidden": centred(keys[0], (TOKENS, D), 1.0, 6.0, ((0, 128),)),
        "in_weight": centred(keys[1], (D, DIN), D ** -0.5, 0.15625, ((0, 128),)),
        "norm_gain": jnp.clip(1.0 + 0.1 * jax.random.normal(keys[2], (D,), jnp.float32), 0.5, 1.5).astype(jnp.bfloat16),
        "conv_weight": centred(keys[3], (CONVD, TAPS), TAPS ** -0.5, 3.0, ((0, 128),)),
        "conv_bias": jnp.clip(jax.random.uniform(keys[4], (CONVD,), jnp.float32, -0.5, 0.5) * shard_levels(keys[4], (CONVD,), ((0, 128),), -0.4, 0.0), -0.5, 0.5).astype(jnp.bfloat16),
        "dt_bias": jnp.clip(jax.random.uniform(keys[5], (NH,), jnp.float32, -5.0, -2.0), -5.0, -2.0),
        "a_log": jnp.clip(jax.random.uniform(keys[6], (NH,), jnp.float32, 0.0, 2.7), 0.0, 2.7),
        "skip": jnp.clip(jax.random.uniform(keys[7], (NH,), jnp.float32, 0.5, 1.5), 0.5, 1.5),
        "inner_gain": jnp.clip(1.0 + 0.1 * jax.random.normal(keys[8], (INNER,), jnp.float32), 0.5, 1.5).astype(jnp.bfloat16),
        "out_weight": centred(keys[9], (INNER, D), INNER ** -0.5, 0.109375, ((0, 128),)),
        "out_grad": centred(keys[10], (TOKENS, D), 1.0, 6.0, ((0, 128),)),
        "seq_lengths": draw_seq_lengths(jax.random.fold_in(keys[13], 71), 0),
        "seq_owner": jax.random.permutation(keys[12], NSEQ).astype(jnp.int32),
    }


EPSILON = 1e-05
PRECISE = lax.Precision.HIGHEST

@jax.custom_vjp
def low(v):
    return lax.optimization_barrier(v.astype(jnp.bfloat16)).astype(jnp.float32)

@jax.custom_vjp
def low_back(v):
    return v

def low_keep(v):
    return (low(v), None)

def low_pass(kept, grad):
    return (grad,)

def back_keep(v):
    return (v, None)

def back_low(kept, grad):
    return (low(grad),)
low.defvjp(low_keep, low_pass)
low_back.defvjp(back_keep, back_low)

def scan_block(carry_state, block_items):
    head_values, write_vec, read_vec, step_size, log_decay = block_items
    block_len = log_decay.shape[0]
    positions = jnp.arange(block_len)
    lower_mask = positions[:, None] >= positions[None, :]
    cumulative = jnp.dot(lower_mask.astype(jnp.float32), log_decay, precision=PRECISE)
    across = cumulative.T
    spread = across[:, :, None] - across[:, None, :]
    decays = jnp.exp(jnp.where(lower_mask[None, :, :], spread, -1e+30))
    scores = jnp.dot(read_vec, write_vec.T, precision=PRECISE)
    weights = decays * scores[None, :, :] * step_size.T[:, None, :]
    inside = jnp.einsum('hij,jhp->ihp', weights, head_values, precision=PRECISE)
    carried = jnp.einsum('in,hpn->ihp', read_vec, carry_state, precision=PRECISE) * jnp.exp(cumulative)[:, :, None]
    tail_rates = jnp.exp(cumulative[-1][None, :] - cumulative) * step_size
    scaled = tail_rates[:, :, None] * head_values
    new_state = jnp.exp(cumulative[-1])[:, None, None] * carry_state + jnp.einsum('jhp,jn->hpn', scaled, write_vec, precision=PRECISE)
    return (new_state, inside + carried)

def mixer_layer(projected, conv_weight, conv_bias, dt_bias, a_log, skip, inner_gain):
    row_count = projected.shape[0]
    inner_width = inner_gain.shape[0]
    conv_width = conv_weight.shape[0]
    taps_count = conv_weight.shape[1]
    head_count = dt_bias.shape[0]
    head_width = inner_width // head_count
    state_width = (conv_width - inner_width) // 2
    gate_part = projected[:, :inner_width]
    conv_input = projected[:, inner_width:inner_width + conv_width]
    step_raw = projected[:, inner_width + conv_width:]
    padded = jnp.pad(conv_input, ((taps_count - 1, 0), (0, 0)))
    convolved = jnp.zeros_like(conv_input) + conv_bias[None, :]
    for lag in range(taps_count):
        convolved = convolved + padded[lag:lag + row_count] * conv_weight[:, lag][None, :]
    activated = jax.nn.silu(convolved)
    head_values = activated[:, :inner_width].reshape(row_count, head_count, head_width)
    write_vec = activated[:, inner_width:inner_width + state_width]
    read_vec = activated[:, inner_width + state_width:]
    step_size = jax.nn.softplus(step_raw + dt_bias[None, :])
    log_decay = -jnp.exp(a_log)[None, :] * step_size
    block_count = row_count // BLOCK

    def into_blocks(values_in):
        return values_in.reshape((block_count, BLOCK) + values_in.shape[1:])
    start_state = jnp.zeros((head_count, head_width, state_width), jnp.float32)
    final_state, outputs = lax.scan(jax.checkpoint(scan_block), start_state, (into_blocks(head_values), into_blocks(write_vec), into_blocks(read_vec), into_blocks(step_size), into_blocks(log_decay)))
    heads_out = outputs.reshape(row_count, head_count, head_width) + skip[None, :, None] * head_values
    product = heads_out.reshape(row_count, inner_width) * jax.nn.silu(gate_part)
    factor = lax.rsqrt(lax.optimization_barrier(jnp.mean(product * product, axis=1, keepdims=True)) + EPSILON)
    return product * factor * inner_gain[None, :]

def forward(params, group_rows, group_live):
    in_weight, norm_gain, conv_weight, conv_bias, dt_bias, a_log, skip, inner_gain, out_weight = params
    normed = group_rows * lax.rsqrt(lax.optimization_barrier(jnp.mean(group_rows * group_rows, axis=-1, keepdims=True)) + EPSILON)
    lowered = low(normed * norm_gain)
    projected = low_back(jnp.einsum('gtd,de->gte', lowered, in_weight, precision=PRECISE))

    def one_device(device_rows):
        return mixer_layer(device_rows, conv_weight, conv_bias, dt_bias, a_log, skip, inner_gain)
    gated = low(jax.vmap(one_device)(projected))
    branch = jnp.einsum('gti,id->gtd', gated, out_weight, precision=PRECISE)
    return group_rows + group_live[:, :, None] * branch

def reference(hidden, in_weight, norm_gain, conv_weight, conv_bias, dt_bias, a_log, skip, inner_gain, out_weight, out_grad, seq_lengths, seq_owner):
    devices = N_FSDP
    lengths_dev = jnp.zeros((devices,), jnp.int32).at[seq_owner.astype(jnp.int32)].set(seq_lengths.astype(jnp.int32))
    live = (jnp.arange(CAP, dtype=jnp.int32)[None, :] < lengths_dev[:, None]).astype(jnp.float32)
    group_size = math.gcd(devices, 1 << max(1, 4096 // CAP).bit_length() - 1)
    group_steps = devices // group_size
    params = (in_weight.astype(jnp.float32), norm_gain.astype(jnp.float32), conv_weight.astype(jnp.float32), conv_bias.astype(jnp.float32), dt_bias.astype(jnp.float32), a_log.astype(jnp.float32), skip.astype(jnp.float32), inner_gain.astype(jnp.float32), out_weight.astype(jnp.float32))
    rows_all = hidden.astype(jnp.float32).reshape(group_steps, group_size, CAP, D)
    grads_all = out_grad.astype(jnp.float32).reshape(group_steps, group_size, CAP, D)
    live_all = live.reshape(group_steps, group_size, CAP)

    def one_group(totals, group_items):
        group_rows, group_grads, group_live = group_items

        def run_group(param_set, rows_in):
            return forward(param_set, rows_in, group_live)
        group_out, pull_back = jax.vjp(run_group, params, group_rows)
        param_grads, rows_grad = pull_back(group_grads)
        totals = jax.tree.map(lambda first, second: first + second, totals, param_grads)
        return (totals, (group_out.astype(jnp.bfloat16), rows_grad.astype(jnp.bfloat16)))
    start_totals = jax.tree.map(jnp.zeros_like, params)
    totals, (mixed, in_grad) = lax.scan(one_group, start_totals, (rows_all, grads_all, live_all))
    return (mixed.reshape(TOKENS, D), in_grad.reshape(TOKENS, D), totals[0], totals[1], totals[2], totals[3], totals[4], totals[5], totals[6], totals[7], totals[8])
```

```python
import functools

import jax
import jax.numpy as jnp
from jax import lax
from jax.experimental import pallas as pl
from jax.experimental.pallas import tpu as pltpu
from jax.sharding import PartitionSpec as P

MESH = pl.DeviceIdType.MESH
F32, BF16 = jnp.float32, jnp.bfloat16
HIGHEST = lax.Precision.HIGHEST
EPSILON = 1e-05

D = 1536
INNER = 3072
CONVD = 3328
HEADS = 48
SEQ = 128
GROUP = 8
ROWS = SEQ * GROUP
GW = INNER // GROUP
OWN = HEADS // GROUP
SH = 384
CW = GW + 256
COLS = 2 * GW + SH
KIN = D // 128
KOUT = INNER // 128
FOLD = D + D // 2
VMEM_LIMIT = 60 * 2**20


def iota(shape, dim):
    return lax.broadcasted_iota(jnp.int32, shape, dim)


def ones(condition, kind=BF16):
    return jnp.where(condition, 1.0, 0.0).astype(kind)


def dot(a, b, precision=None):
    return lax.dot_general(a, b, (((1,), (0,)), ((), ())), precision=precision, preferred_element_type=F32)


def dot_nt(a, b, precision=None):
    return lax.dot_general(a, b, (((1,), (1,)), ((), ())), precision=precision, preferred_element_type=F32)


def dot_tn(a, b, precision=None):
    return lax.dot_general(a, b, (((0,), (0,)), ((), ())), precision=precision, preferred_element_type=F32)


def sigmoid(v):
    return 1.0 / (1.0 + jnp.exp(-v))


def softplus(v):
    return jnp.maximum(v, 0.0) + jnp.log1p(jnp.exp(-jnp.abs(v)))


def later(v, k):
    if k == 0:
        return v
    return jnp.where(iota(v.shape, 0) >= k, pltpu.roll(v, k, 0), 0.0)


def earlier(v, k):
    if k == 0:
        return v
    return jnp.where(iota(v.shape, 0) < v.shape[0] - k, pltpu.roll(v, v.shape[0] - k, 0), 0.0)


def place():
    me = lax.axis_index("fsdp")
    return me // 32, (me // 8) % 4, (me // 2) % 4, me % 2


def index(z, x, y, c):
    return ((z * 4 + x) * 4 + y) * 2 + c


def group_partner(k):
    z, x, y, c = place()
    rank = (y * 2 + c + k) % GROUP
    return index(z, x, rank // 2, rank % 2), rank


def on_z(k):
    z, x, y, c = place()
    return index((z + k) % 4, x, y, c)


def on_x(k):
    z, x, y, c = place()
    return index(z, (x + k) % 4, y, c)


def on_y(k):
    z, x, y, c = place()
    return index(z, x, (y + k) % 4, c)


def sibling():
    z, x, y, c = place()
    return index(z, x, y, 1 - c)


def barrier(partners):
    sem = pltpu.get_barrier_semaphore()
    for p in partners:
        pl.semaphore_signal(sem, inc=1, device_id=(p,), device_id_type=MESH)
    pl.semaphore_wait(sem, len(partners))


def remote(src, dst, send, recv, target):
    return pltpu.make_async_remote_copy(
        src_ref=src, dst_ref=dst, send_sem=send, recv_sem=recv, device_id=(target,), device_id_type=MESH
    )


def plane_partners():
    return [on_z(k) for k in (1, 2, 3)] + [on_x(k) for k in (1, 2, 3)]


def group_partners():
    return [group_partner(k)[0] for k in range(1, GROUP)]


class PlaneGather:
    def __init__(self, buf, own, send, recv, halves):
        self.buf, self.own, self.send, self.recv, self.halves = buf, own, send, recv, halves
        self.z, self.x, _, _ = place()

    def slot(self, half, first, second):
        a, b = (first, second) if half == 0 else (second, first)
        return self.buf.at[(self.z + a) % 4, (self.x + b) % 4, half]

    def along(self, half, stage, k):
        return on_z(k) if (half == 0) == (stage == 0) else on_x(k)

    def copy(self, half, first, stage, k):
        src = self.own(half) if first == 0 else self.slot(half, first, 0)
        at = (4 - k, 0) if stage == 0 else (first, 4 - k)
        return remote(
            src,
            self.slot(half, first, 0),
            self.send.at[half, first if stage else 4, k],
            self.recv.at[half, at[0], at[1]],
            self.along(half, stage, k),
        )

    def arrival(self, half, first, second):
        here = self.slot(half, first, second)
        return remote(here, here, self.send.at[half, 4, 0], self.recv.at[half, first, second], on_z(1))

    def start(self):
        for k in (1, 3, 2):
            for half in range(self.halves):
                self.copy(half, 0, 0, k).start()
        for k in (1, 3, 2):
            for half in range(self.halves):
                self.copy(half, 0, 1, k).start()

    def forward(self):
        for first in (1, 3, 2):
            for half in range(self.halves):
                self.arrival(half, first, 0).wait_recv()
                for k in (1, 3, 2):
                    self.copy(half, first, 1, k).start()

    def finish(self):
        for first in range(4):
            for second in (1, 3, 2):
                for half in range(self.halves):
                    self.arrival(half, first, second).wait_recv()
        for half in range(self.halves):
            for k in (1, 2, 3):
                self.copy(half, 0, 0, k).wait_send()
                for first in range(4):
                    self.copy(half, first, 1, k).wait_send()


class GroupGather:
    def __init__(self, buf, own, send, recv):
        self.buf, self.own, self.send, self.recv = buf, own, send, recv
        _, _, self.y, self.c = place()

    def along(self, k):
        return remote(self.own, self.buf.at[self.y, self.c], self.send.at[0, k], self.recv.at[0, 4 - k], on_y(k))

    def across(self, k):
        src = self.own if k == 0 else self.buf.at[(self.y + k) % 4, self.c]
        dst = self.buf.at[(self.y + k) % 4, self.c]
        return remote(src, dst, self.send.at[1, k], self.recv.at[1, k], sibling())

    def arrival(self, hop, k):
        here = self.buf.at[(self.y + k) % 4, self.c if hop == 0 else 1 - self.c]
        return remote(here, here, self.send.at[hop, k], self.recv.at[hop, k], sibling())

    def start(self):
        for k in (1, 3, 2):
            self.along(k).start()
        self.across(0).start()

    def forward(self):
        for k in (1, 3, 2):
            self.arrival(0, k).wait_recv()
            self.across(k).start()

    def finish(self):
        for k in range(4):
            self.arrival(1, k).wait_recv()
        for k in range(4):
            self.across(k).wait_send()
            if k:
                self.along(k).wait_send()


def gather_kernel(
    inw, outl, hid, grd, w_out, p_out, l_out, h_out, g_out,
    split, joined, block, params, plane,
    a2a_sem, w_sem, w_rsem, p_sem, p_rsem, l_sem, l_rsem, h_sem, g_sem, o_sem, local,
):
    z, x, y, c = place()
    rank = y * 2 + c
    barrier(plane_partners() + group_partners())
    hidden = GroupGather(h_out, hid, h_sem.at[0], h_sem.at[1])
    grads = GroupGather(g_out, grd, g_sem.at[0], g_sem.at[1])
    steps = inw[:, 2 * INNER + 256 :]
    for q in range(GROUP):
        split[q] = jnp.zeros((16, COLS), BF16)
        split[q, :, 0:GW] = inw[:, q * GW : (q + 1) * GW]
        split[q, :, GW : 2 * GW] = inw[:, INNER + q * GW : INNER + (q + 1) * GW]
        split[q, :, 2 * GW : 2 * GW + 256] = inw[:, 2 * INNER : 2 * INNER + 256]
        split[q, :, 2 * GW + 256 : 2 * GW + 256 + OWN] = steps[:, q * OWN : (q + 1) * OWN]

    def to_member(k):
        target, q = group_partner(k)
        return remote(split.at[q], joined.at[rank], a2a_sem.at[0, k], a2a_sem.at[1, k], target)

    def from_member(k):
        _, q = group_partner(k)
        return remote(joined.at[q], joined.at[q], a2a_sem.at[0, k], a2a_sem.at[1, GROUP - k], sibling())

    for k in range(1, GROUP):
        to_member(k).start()
    hidden.start()
    joined[rank] = split[rank]
    lines = PlaneGather(l_out_plane := plane, lambda h: outl.at[h], l_sem, l_rsem, 2)
    for k in range(1, GROUP):
        from_member(k).wait_recv()
    row, col = iota((112, 128), 0), iota((112, 128), 1)
    member, line = col // 16, col % 16
    spot = jnp.where(line < KIN, member * KIN + line, jnp.where(line == KIN, 96 + member, -1))
    rows = dot(ones(spot == row), joined[...].reshape(128, COLS)).astype(BF16)
    block[0] = rows[0:48]
    block[1] = rows[48:96]
    params[...] = rows[96:112, 0:256]
    weights = PlaneGather(w_out, lambda h: block.at[h], w_sem, w_rsem, 2)
    small = PlaneGather(p_out, lambda h: params, p_sem, p_rsem, 1)
    small.start()
    weights.start()
    grads.start()
    lines.start()
    own = [
        pltpu.make_async_copy(block, w_out.at[z, x], local.at[0]),
        pltpu.make_async_copy(params, p_out.at[z, x, 0], local.at[1]),
        pltpu.make_async_copy(hid, h_out.at[y, c], local.at[2]),
        pltpu.make_async_copy(grd, g_out.at[y, c], local.at[3]),
        pltpu.make_async_copy(outl, plane.at[z, x], local.at[4]),
    ]
    for copy in own:
        copy.start()
    hidden.forward()
    small.forward()
    weights.forward()
    lines.forward()
    grads.forward()
    hidden.finish()
    small.finish()
    weights.finish()
    lines.finish()
    own[4].wait()

    def slots(q):
        return plane.at[q // 2, pl.ds((q % 2) * 2, 2)]

    def lines_to(k):
        target, q = group_partner(k)
        return remote(slots(q), l_out.at[rank], o_sem.at[0, k], o_sem.at[1, k], target)

    def lines_from(k):
        _, q = group_partner(k)
        return remote(l_out.at[q], l_out.at[q], o_sem.at[0, k], o_sem.at[1, GROUP - k], sibling())

    for k in range(1, GROUP):
        lines_to(k).start()
    mine = pltpu.make_async_copy(slots(rank), l_out.at[rank], local.at[5])
    mine.start()
    for k in range(1, GROUP):
        lines_from(k).wait_recv()
    mine.wait()
    grads.finish()
    for k in range(1, GROUP):
        to_member(k).wait_send()
        lines_to(k).wait_send()
    for copy in own[:4]:
        copy.wait()


def gather(inw, outl, hid, grd):
    vmem, hbm = pl.BlockSpec(memory_space=pltpu.VMEM), pl.BlockSpec(memory_space=pl.ANY)
    dma = pltpu.SemaphoreType.DMA
    return pl.pallas_call(
        gather_kernel,
        name="gather",
        out_shape=(
            jax.ShapeDtypeStruct((4, 4, 2, 48, COLS), BF16),
            jax.ShapeDtypeStruct((4, 4, 1, 16, 256), BF16),
            jax.ShapeDtypeStruct((GROUP, 2, 2, 16, FOLD // 2), BF16),
            jax.ShapeDtypeStruct((4, 2, SEQ, D), BF16),
            jax.ShapeDtypeStruct((4, 2, SEQ, D), BF16),
        ),
        in_specs=[vmem] * 4,
        out_specs=(hbm,) * 5,
        scratch_shapes=[
            pltpu.VMEM((GROUP, 16, COLS), BF16),
            pltpu.VMEM((GROUP, 16, COLS), BF16),
            pltpu.VMEM((2, 48, COLS), BF16),
            pltpu.VMEM((16, 256), BF16),
            pltpu.VMEM((4, 4, 2, 16, FOLD // 2), BF16),
            dma((2, GROUP)),
            dma((2, 5, 4)), dma((2, 4, 4)),
            dma((1, 5, 4)), dma((1, 4, 4)),
            dma((2, 5, 4)), dma((2, 4, 4)),
            dma((2, 2, 4)), dma((2, 2, 4)),
            dma((2, GROUP)), dma((6,)),
        ],
        compiler_params=pltpu.CompilerParams(collective_id=0, has_side_effects=True, vmem_limit_bytes=VMEM_LIMIT),
    )(inw, outl, hid, grd)


def unpack_params(raw, rank, par):
    row = iota((256, 1), 0)
    device = jnp.where(row % 16 < 8, row // 16 * 8 + row % 16, -1).astype(F32)
    values = raw[...]

    def spread(first, count, channel):
        owner = jnp.floor((channel + 0.5) * (1.0 / count))
        lane = channel - owner * count + first
        pick = ones(iota((256, channel.shape[1]), 0).astype(F32) == lane)
        spots = dot(values, pick)
        return jnp.sum(jnp.where(device == owner, spots, 0.0), axis=0, keepdims=True)

    def lanes(n):
        return iota((1, n), 1).astype(F32)

    start = rank.astype(F32) * GW
    conv = lanes(CW)
    conv = jnp.where(conv < GW, conv + start, conv - GW + INNER)
    par[...] = jnp.zeros_like(par)
    par[0:1, :] = spread(0, KIN, lanes(D))
    for k in range(5):
        par[k + 1 : k + 2, 0:CW] = spread(KIN + 26 * k, 26, conv)
    par[6:7, 0:GW] = spread(KIN + 130, KOUT, lanes(GW) + start)


def unfold_out_weight(raw, ow):
    row, col = iota((GW, 256), 0), iota((GW, 256), 1)
    device, line = row // KOUT, row % KOUT
    base = (device % 8) * 32 + (device // 8) * 16
    top = ones(jnp.logical_and(line < 16, col == base + line))
    low_left = ones(jnp.logical_and(line >= 16, col == base + line - 16))
    low_right = ones(jnp.logical_and(line >= 16, col == base + line - 8))
    first = raw[:, :, 0].reshape(256, FOLD // 2)
    second = raw[:, :, 1].reshape(256, FOLD // 2)
    split = FOLD // 2 - D // 2
    left, right_a, right_b, tail = first[:, 0 : D // 2], first[:, D // 2 :], second[:, 0 : D // 2 - split], second[:, D // 2 - split :]
    ow[:, 0 : D // 2] = (dot(top, left) + dot(low_left, tail)).astype(BF16)
    ow[:, D // 2 : D // 2 + split] = (dot(top, right_a) + dot(low_right, tail[:, 0:split])).astype(BF16)
    ow[:, D // 2 + split :] = (dot(top, right_b) + dot(low_right, tail[:, split:])).astype(BF16)


def lower_gain(hid, par, lowered):
    def one(b, carry):
        rows = pl.ds(b * SEQ, SEQ)
        h = hid[rows, :].astype(F32)
        scale = lax.rsqrt(jnp.mean(h * h, axis=1, keepdims=True) + EPSILON)
        lowered[rows, :] = (h * scale * par[0:1, :]).astype(BF16)
        return carry

    lax.fori_loop(0, GROUP, one, 0)


def convolve(raw, par, at, width):
    out = par[5:6, at : at + width] + raw * par[4:5, at : at + width]
    for k in range(3):
        out = out + later(raw, 3 - k) * par[k + 1 : k + 2, at : at + width]
    return out


def steps_of(raw, head):
    step = softplus(raw + head[0:1, :])
    decay = head[1:2, :] * step
    lower = ones(iota((SEQ, SEQ), 0) >= iota((SEQ, SEQ), 1), F32)
    total = dot(lower, decay, HIGHEST)
    return step, decay, total


def forward_mix(proj, par, head, skip, heads_out, dgated, sums):
    row, col = iota((SEQ, SEQ), 0), iota((SEQ, SEQ), 1)
    causal = row >= col
    left = col < 64

    def one(b, acc):
        rows = pl.ds(b * SEQ, SEQ)
        wr = convolve(proj[rows, 2 * GW : 2 * GW + 256], par, GW, 256)
        wr = wr * sigmoid(wr)
        write, read = wr[:, 0:128], wr[:, 128:256]
        step, _, total = steps_of(proj[rows, 2 * GW + 256 : COLS], head)
        total_t, step_t = total.T, step.T
        scores = dot_nt(read, write, HIGHEST)
        squares = jnp.zeros((SEQ, 1), F32)
        crosses = jnp.zeros((SEQ, 1), F32)
        for p in range(3):
            at = p * 128
            values = convolve(proj[rows, GW + at : GW + at + 128], par, at, 128)
            values = values * sigmoid(values)
            values_low = values.astype(BF16)
            parts = []
            for h in (2 * p, 2 * p + 1):
                decays = jnp.exp(jnp.where(causal, total[:, h : h + 1] - total_t[h : h + 1, :], -1e30))
                mix = (decays * scores * step_t[h : h + 1, :]).astype(BF16)
                parts.append(dot(mix, values_low))
            out = jnp.where(left, parts[0], parts[1]) + skip[0:1, at : at + 128] * values
            heads_out[rows, at : at + 128] = out
            gate = proj[rows, at : at + 128]
            product = out * gate * sigmoid(gate)
            w = dgated[rows, at : at + 128] * par[6:7, at : at + 128]
            squares = squares + jnp.sum(product * product, axis=1, keepdims=True)
            crosses = crosses + jnp.sum(product * w, axis=1, keepdims=True)
        return jnp.where(col == b, squares, jnp.where(col == b + 8, crosses, acc))

    acc = lax.fori_loop(0, GROUP, one, jnp.zeros((SEQ, SEQ), F32))
    sums[...] = acc.T[0:16, :]


def forward_kernel(hid, w, praw, oraw, grads, head, skip, proj, lowered, heads_out, dgated, ow, par, sums):
    rank = lax.axis_index("fsdp") % GROUP
    unpack_params(praw, rank, par)
    unfold_out_weight(oraw, ow)
    lower_gain(hid, par, lowered)

    def project(i, carry):
        rows = pl.ds(i * 256, 256)
        proj[rows, :] = dot(lowered[rows, :], w[...])
        dgated[rows, :] = dot_nt(grads[rows, :], ow[...])
        return carry

    lax.fori_loop(0, ROWS // 256, project, 0)
    forward_mix(proj, par, head, skip, heads_out, dgated, sums)


def forward(hid, w, praw, oraw, grads, head, skip):
    vmem = pl.BlockSpec(memory_space=pltpu.VMEM)
    shape = jax.ShapeDtypeStruct
    return pl.pallas_call(
        forward_kernel,
        name="forward",
        out_shape=(
            shape((ROWS, COLS), F32),
            shape((ROWS, D), BF16),
            shape((ROWS, GW), F32),
            shape((ROWS, GW), F32),
            shape((GW, D), BF16),
            shape((8, D), F32),
            shape((16, SEQ), F32),
        ),
        in_specs=[vmem] * 7,
        out_specs=(vmem,) * 7,
        compiler_params=pltpu.CompilerParams(vmem_limit_bytes=VMEM_LIMIT),
    )(hid, w, praw, oraw, grads, head, skip)


def sums_kernel(own, total, slots, send, recv):
    barrier(group_partners())

    def copy(k):
        target, _ = group_partner(k)
        return remote(own, slots.at[k], send.at[k], recv.at[k], target)

    for k in range(1, GROUP):
        copy(k).start()
    out = own[...]
    for k in range(1, GROUP):
        copy(k).wait_recv()
        out = out + slots[k]
    total[...] = out
    for k in range(1, GROUP):
        copy(k).wait_send()


def group_sums(own):
    vmem = pl.BlockSpec(memory_space=pltpu.VMEM)
    return pl.pallas_call(
        sums_kernel,
        name="group_sums",
        out_shape=jax.ShapeDtypeStruct(own.shape, F32),
        in_specs=[vmem],
        out_specs=vmem,
        scratch_shapes=[
            pltpu.VMEM((GROUP,) + own.shape, F32),
            pltpu.SemaphoreType.DMA((GROUP,)),
            pltpu.SemaphoreType.DMA((GROUP,)),
        ],
        compiler_params=pltpu.CompilerParams(collective_id=1, has_side_effects=True),
    )(own)


def backward_mix(proj, par, head, skip, heads_out, dgated, sums, gated, dproj, small):
    row, col = iota((SEQ, SEQ), 0), iota((SEQ, SEQ), 1)
    later_ok = col >= row
    left, right = col < 64, col >= 64
    suffix = ones(row >= col)
    before = row < col
    wide = jnp.concatenate([sums[...], jnp.zeros((SEQ - 16, SEQ), F32)], axis=0).T
    small[...] = jnp.zeros_like(small)

    def conv_back(d_act, raw, at, width):
        v = convolve(raw, par, at, width)
        s = sigmoid(v)
        d_conv = d_act * s * (1.0 + v * (1.0 - s))
        span = slice(at, at + width)
        back = d_conv * par[4:5, span]
        small[3:4, span] += jnp.sum(d_conv * raw, axis=0, keepdims=True)
        for k in range(3):
            back = back + earlier(d_conv, 3 - k) * par[k + 1 : k + 2, span]
            small[k : k + 1, span] += jnp.sum(d_conv * later(raw, 3 - k), axis=0, keepdims=True)
        small[4:5, span] += jnp.sum(d_conv, axis=0, keepdims=True)
        return back

    def one(b, carry):
        rows = pl.ds(b * SEQ, SEQ)
        square = jnp.sum(jnp.where(col == b, wide, 0.0), axis=1, keepdims=True)
        cross = jnp.sum(jnp.where(col == b + 8, wide, 0.0), axis=1, keepdims=True)
        inverse = lax.rsqrt(square * (1.0 / INNER) + EPSILON)
        mean = cross * inverse * (1.0 / INNER)
        raw_wr = proj[rows, 2 * GW : 2 * GW + 256]
        wr = convolve(raw_wr, par, GW, 256)
        wr = wr * sigmoid(wr)
        write, read = wr[:, 0:128], wr[:, 128:256]
        raw_step = proj[rows, 2 * GW + 256 : COLS]
        step, decay, total = steps_of(raw_step, head)
        total_t = total.T
        scores_t = dot_nt(write, read, HIGHEST)
        d_scores = jnp.zeros((SEQ, SEQ), F32)
        direct = jnp.zeros((SEQ, SEQ), F32)
        lines = []
        for p in range(3):
            at = p * 128
            span = slice(at, at + 128)
            out = heads_out[rows, span]
            gate = proj[rows, span]
            s = sigmoid(gate)
            silu = gate * s
            unit = out * silu * inverse
            dg = dgated[rows, span]
            gain = par[6:7, span]
            gated[rows, span] = (unit * gain).astype(BF16)
            small[5:6, span] += jnp.sum(dg * unit, axis=0, keepdims=True)
            d_product = (dg * gain - unit * mean) * inverse
            d_out = d_product * silu
            dproj[rows, span] = (d_product * out * (s * (1.0 + gate * (1.0 - s)))).astype(BF16)
            raw = proj[rows, GW + at : GW + at + 128]
            values = convolve(raw, par, at, 128)
            values = values * sigmoid(values)
            small[6:7, span] += jnp.sum(d_out * values, axis=0, keepdims=True)
            values_low = values.astype(BF16)
            d_low = d_out.astype(BF16)
            parts = []
            for i, h in enumerate((2 * p, 2 * p + 1)):
                decays = jnp.exp(jnp.where(later_ok, total_t[h : h + 1, :] - total[:, h : h + 1], -1e30))
                size = step[:, h : h + 1]
                own = jnp.where(left if i == 0 else right, d_out, 0.0).astype(BF16)
                d_mix = decays * dot_nt(values_low, own)
                d_scores = d_scores + d_mix * size
                per_step = (d_mix * scores_t).astype(BF16)
                tail = dot(per_step, suffix)
                direct = jnp.where(col == h, tail[:, 0:1], direct)
                lines.append(jnp.sum(jnp.where(before, tail * size, 0.0), axis=0, keepdims=True))
                mix = (decays * scores_t * size).astype(BF16)
                parts.append(dot(mix, d_low))
            d_values = jnp.where(left, parts[0], parts[1]) + skip[0:1, span] * d_out
            dproj[rows, GW + at : GW + at + 128] = conv_back(d_values, raw, at, 128).astype(BF16)
        lines = jnp.concatenate(lines + [jnp.zeros((SEQ - OWN, SEQ), F32)], axis=0)
        d_decay = lines.T
        d_step = direct + head[1:2, :] * d_decay
        d_raw = d_step * sigmoid(raw_step + head[0:1, :])
        small[7:8, 0:128] += jnp.sum(d_raw, axis=0, keepdims=True)
        small[7:8, 128:256] += jnp.sum(d_decay * decay, axis=0, keepdims=True)
        d_low = d_scores.astype(BF16)
        d_write = dot(d_low, read.astype(BF16))
        d_read = dot_tn(d_low, write.astype(BF16))
        d_wr = jnp.concatenate([d_write, d_read], axis=1)
        dproj[rows, 2 * GW : 2 * GW + 256] = conv_back(d_wr, raw_wr, GW, 256).astype(BF16)
        dproj[rows, 2 * GW + 256 : COLS] = d_raw.astype(BF16)
        return carry

    lax.fori_loop(0, GROUP, one, 0)


def backward_kernel(
    w, grads, head, skip, proj, lowered, heads_out, dgated, ow, par, sums, branch, d_low, dw, dow, small, gated, dproj
):
    backward_mix(proj, par, head, skip, heads_out, dgated, sums, gated, dproj, small)

    def by_rows(i, carry):
        rows = pl.ds(i * 256, 256)
        branch[rows, :] = dot(gated[rows, :], ow[...]).astype(BF16)
        d_low[rows, :] = dot_nt(dproj[rows, :], w[...]).astype(BF16)
        return carry

    lax.fori_loop(0, ROWS // 256, by_rows, 0)
    for i in range(D // 384):
        span = slice(i * 384, (i + 1) * 384)
        dw[span, :] = dot_tn(lowered[:, span], dproj[...]).astype(BF16)
    out = dot_tn(gated[...], grads[...])
    for j in range(16):
        block = out[j * KOUT : (j + 1) * KOUT]
        tail = jnp.concatenate([block[16:24, 0 : D // 2], block[16:24, D // 2 :]], axis=0)
        fold = jnp.concatenate([block[0:16], tail], axis=1).astype(BF16)
        for half in range(2):
            dow[j % 8, j // 8, half] = fold[:, half * (FOLD // 2) : (half + 1) * (FOLD // 2)]


def backward(w, grads, head, skip, proj, lowered, heads_out, dgated, ow, par, sums):
    vmem = pl.BlockSpec(memory_space=pltpu.VMEM)
    shape = jax.ShapeDtypeStruct
    return pl.pallas_call(
        backward_kernel,
        name="backward",
        out_shape=(
            shape((ROWS, D), BF16),
            shape((ROWS, D), BF16),
            shape((D, COLS), BF16),
            shape((GROUP, 2, 2, 16, FOLD // 2), BF16),
            shape((8, CW), F32),
        ),
        in_specs=[vmem] * 11,
        out_specs=(vmem,) * 5,
        scratch_shapes=[pltpu.VMEM((ROWS, GW), BF16), pltpu.VMEM((ROWS, COLS), BF16)],
        compiler_params=pltpu.CompilerParams(vmem_limit_bytes=VMEM_LIMIT),
    )(w, grads, head, skip, proj, lowered, heads_out, dgated, ow, par, sums)


class PlaneReduce:
    def __init__(self, terms, got, mid, last, out, send, recv):
        self.terms, self.got, self.mid, self.last, self.out = terms, got, mid, last, out
        self.send, self.recv = send, recv
        self.z, self.x, _, _ = place()

    def line(self, half, k):
        return self.terms.at[:, (self.x + k) % 4, 0] if half == 0 else self.terms.at[(self.z + k) % 4, :, 1]

    def first(self, half, k):
        target = on_x(k) if half == 0 else on_z(k)
        return remote(self.line(half, k), self.got.at[half, k - 1], self.send.at[half, 0, k], self.recv.at[half, 0, k], target)

    def second(self, half, k):
        target = on_z(k) if half == 0 else on_x(k)
        return remote(self.mid.at[half, k - 1], self.last.at[half, k - 1], self.send.at[half, 1, k], self.recv.at[half, 1, k], target)

    def start(self):
        for k in (2, 1, 3):
            for half in range(2):
                self.first(half, k).start()

    def middle(self):
        for half in range(2):
            for k in (1, 2, 3):
                self.first(half, k).wait_recv()
            for k in (2, 1, 3, 0):
                if half == 0:
                    at = (self.z + k) % 4
                    total = self.terms[at, self.x, 0].astype(F32)
                else:
                    at = (self.x + k) % 4
                    total = self.terms[self.z, at, 1].astype(F32)
                for j in range(3):
                    total = total + self.got[half, j, at].astype(F32)
                if k:
                    self.mid[half, k - 1] = total.astype(BF16)
                    self.second(half, k).start()
                else:
                    self.out[half] = total

    def end(self):
        for half in range(2):
            for k in (1, 2, 3):
                self.second(half, k).wait_recv()
            total = self.out[half]
            for j in range(3):
                total = total + self.last[half, j].astype(F32)
            self.out[half] = total

    def finish(self):
        for half in range(2):
            for k in (1, 2, 3):
                self.first(half, k).wait_send()
                self.second(half, k).wait_send()


class GroupReduce:
    def __init__(self, terms, got, mid, last, out, send, recv):
        self.terms, self.got, self.mid, self.last, self.out = terms, got, mid, last, out
        self.send, self.recv = send, recv
        _, _, self.y, self.c = place()

    def across(self, k):
        src = self.terms.at[(self.y + k) % 4, 1 - self.c]
        return remote(src, self.got.at[k], self.send.at[0, k], self.recv.at[0, k], sibling())

    def along(self, k):
        return remote(self.mid.at[k - 1], self.last.at[k - 1], self.send.at[1, k], self.recv.at[1, k], on_y(k))

    def start(self):
        for k in (2, 1, 3, 0):
            self.across(k).start()

    def middle(self):
        for k in (2, 1, 3, 0):
            self.across(k).wait_recv()
            total = self.terms[(self.y + k) % 4, self.c].astype(F32) + self.got[k].astype(F32)
            if k:
                self.mid[k - 1] = total.astype(BF16)
                self.along(k).start()
            else:
                self.out[...] = total

    def end(self):
        for k in (1, 2, 3):
            self.along(k).wait_recv()
        total = self.out[...]
        for j in range(3):
            total = total + self.last[j].astype(F32)
        self.out[...] = total

    def finish(self):
        for k in range(4):
            self.across(k).wait_send()
            if k:
                self.along(k).wait_send()


def reduce_kernel(
    branch, d_low, dw, dow, small, branch_out, low_out, rows_out, lines_out, small_out,
    gb, mb, lb, gd, md, ld, gw, mw, lw, fw, tl, gl, ml, ll, cut, zs, xs, part,
    b_sem, b_rsem, d_sem, d_rsem, w_sem, w_rsem, l_sem, l_rsem, o_sem, r_sem, s_sem,
):
    z, x, y, c = place()
    rank = y * 2 + c
    barrier(plane_partners() + group_partners())
    first = GroupReduce(branch, gb, mb, lb, branch_out, b_sem, b_rsem)
    second = GroupReduce(d_low, gd, md, ld, low_out, d_sem, d_rsem)
    weights = PlaneReduce(dw, gw, mw, lw, fw, w_sem, w_rsem)
    lines = PlaneReduce(tl, gl, ml, ll, lines_out, l_sem, l_rsem)

    def to_owner(k):
        target, q = group_partner(k)
        return remote(dow.at[q], tl.at[rank // 2, pl.ds((rank % 2) * 2, 2)], o_sem.at[0, k], o_sem.at[1, k], target)

    def from_member(k):
        _, q = group_partner(k)
        here = tl.at[q // 2, pl.ds((q % 2) * 2, 2)]
        return remote(here, here, o_sem.at[0, k], o_sem.at[1, GROUP - k], sibling())

    def small_z(k):
        return remote(small, zs.at[z], s_sem.at[0, k], s_sem.at[1, k], on_z(k))

    def small_x(k):
        return remote(part, xs.at[x], s_sem.at[2, k], s_sem.at[3, k], on_x(k))

    def small_group(k):
        return remote(small_out.at[rank], small_out.at[rank], s_sem.at[4, k], s_sem.at[5, k], group_partner(k)[0])

    weights.start()
    first.start()
    second.start()
    for k in (1, 2, 3):
        small_z(k).start()
    for k in range(1, GROUP):
        to_owner(k).start()
    tl[rank // 2, pl.ds((rank % 2) * 2, 2)] = dow[rank]
    zs[z] = small[...]
    first.middle()
    second.middle()
    for k in (1, 2, 3):
        small_z(k).wait_recv()
    part[...] = ((zs[0] + zs[1]) + zs[2]) + zs[3]
    xs[x] = part[...]
    for k in (1, 2, 3):
        small_x(k).start()
    weights.middle()
    for k in range(1, GROUP):
        from_member(k).wait_recv()
    lines.start()
    for k in (1, 2, 3):
        small_x(k).wait_recv()
    small_out[rank] = ((xs[0] + xs[1]) + xs[2]) + xs[3]
    for k in range(1, GROUP):
        small_group(k).start()
    weights.end()

    def rows_to(k):
        target, q = group_partner(k)
        return remote(cut.at[q], rows_out.at[rank], r_sem.at[0, k], r_sem.at[1, k], target)

    for q in range(GROUP):
        cut[q] = jnp.zeros((16, COLS), BF16)
        cut[q, 0:KIN, :] = fw[q // 4, q % 4 * KIN : (q % 4 + 1) * KIN, :].astype(BF16)
    for k in range(1, GROUP):
        rows_to(k).start()
    rows_out[rank] = cut[rank]
    lines.middle()
    first.end()
    second.end()
    lines.end()
    for k in range(1, GROUP):
        rows_to(k).wait_recv()
        small_group(k).wait_recv()
    first.finish()
    second.finish()
    weights.finish()
    lines.finish()
    for k in range(1, GROUP):
        to_owner(k).wait_send()
        rows_to(k).wait_send()
        small_group(k).wait_send()
    for k in (1, 2, 3):
        small_z(k).wait_send()
        small_x(k).wait_send()


def reduce_all(branch, d_low, dw, dow, small):
    vmem, vm = pl.BlockSpec(memory_space=pltpu.VMEM), pltpu.VMEM
    dma = pltpu.SemaphoreType.DMA
    shape = jax.ShapeDtypeStruct
    wide = FOLD // 2
    return pl.pallas_call(
        reduce_kernel,
        name="reduce",
        out_shape=(
            shape((SEQ, D), F32),
            shape((SEQ, D), F32),
            shape((GROUP, 16, COLS), BF16),
            shape((2, 16, wide), F32),
            shape((GROUP, 8, CW), F32),
        ),
        in_specs=[vmem] * 5,
        out_specs=(vmem,) * 5,
        scratch_shapes=[
            vm((4, SEQ, D), BF16), vm((3, SEQ, D), BF16), vm((3, SEQ, D), BF16),
            vm((4, SEQ, D), BF16), vm((3, SEQ, D), BF16), vm((3, SEQ, D), BF16),
            vm((2, 3, 4, 48, COLS), BF16), vm((2, 3, 48, COLS), BF16), vm((2, 3, 48, COLS), BF16), vm((2, 48, COLS), F32),
            vm((4, 4, 2, 16, wide), BF16),
            vm((2, 3, 4, 16, wide), BF16), vm((2, 3, 16, wide), BF16), vm((2, 3, 16, wide), BF16),
            vm((GROUP, 16, COLS), BF16),
            vm((4, 8, CW), F32), vm((4, 8, CW), F32), vm((8, CW), F32),
            dma((2, 4)), dma((2, 4)), dma((2, 4)), dma((2, 4)),
            dma((2, 2, 4)), dma((2, 2, 4)), dma((2, 2, 4)), dma((2, 2, 4)),
            dma((2, GROUP)), dma((2, GROUP)), dma((6, GROUP)),
        ],
        compiler_params=pltpu.CompilerParams(collective_id=2, has_side_effects=True, vmem_limit_bytes=VMEM_LIMIT),
    )(branch, d_low, dw, dow, small)


def finish_kernel(
    hid, grd, live, inw, gain_own, par, branch, d_low, rows, lines, small,
    mixed, in_grad, dinw, dgain, dconv, dheads, dinner, doutw,
):
    alive = live[...]
    h = hid[...].astype(F32)
    mixed[...] = (h + alive * branch[...]).astype(BF16)
    scale = lax.rsqrt(jnp.mean(h * h, axis=1, keepdims=True) + EPSILON)
    normed = h * scale
    d_normed = d_low[...] * par[0:1, :]
    through = scale * (d_normed - normed * jnp.mean(d_normed * normed, axis=1, keepdims=True))
    in_grad[...] = (grd[...].astype(F32) + through).astype(BF16)
    shared = jnp.zeros((KIN, 256), F32)
    total = jnp.zeros((KIN, 1), F32)
    for q in range(GROUP):
        block = rows[q].astype(F32)[0:KIN]
        for at, span in ((q * GW, block[:, 0:GW]), (INNER + q * GW, block[:, GW : 2 * GW])):
            dinw[:, at : at + GW] = span
        at = 2 * INNER + 256 + q * OWN
        dinw[:, at : at + OWN] = block[:, 2 * GW + 256 : 2 * GW + 256 + OWN]
        shared = shared + block[:, 2 * GW : 2 * GW + 256]
    dinw[:, 2 * INNER : 2 * INNER + 256] = shared
    total = jnp.sum(dinw[...] * inw[...].astype(F32), axis=1, keepdims=True)
    dgain[...] = total / gain_own[...].astype(F32)
    me = lax.axis_index("fsdp")
    conv = jnp.zeros((32, 8), F32)
    inner = jnp.zeros((32, 8), F32)
    common = jnp.zeros((8, 256), F32)
    line = iota((32, GW), 0)
    heads = ones(iota((GW, 128), 0) // 64 == iota((GW, 128), 1), F32)
    dheads[...] = jnp.zeros_like(dheads)
    for q in range(GROUP):
        part = small[q, :, 0:GW]
        lane = iota((32, GW), 1) + q * GW
        conv = conv + dot_nt(ones(lane == line + 26 * me, F32), part, HIGHEST)
        inner = inner + dot_nt(ones(lane == line + KOUT * me, F32), part, HIGHEST)
        common = common + small[q, :, GW:CW]
        span = slice(q * OWN, (q + 1) * OWN)
        dheads[0:1, span] = small[q, 7:8, 0:OWN]
        dheads[1:2, span] = small[q, 7:8, 128 : 128 + OWN]
        dheads[2:3, span] = dot(part, heads, HIGHEST)[6:7, 0:OWN]
    lane = iota((32, 256), 1) + INNER
    conv = conv + dot_nt(ones(lane == iota((32, 256), 0) + 26 * me, F32), common, HIGHEST)
    dconv[...] = conv
    dinner[...] = inner
    wide = FOLD // 2
    first, second = lines[0], lines[1]
    doutw[0:16, 0:wide] = first
    doutw[0:16, wide:D] = second[:, 0 : D - wide]
    tail = second[:, D - wide :]
    doutw[16:24, 0 : D // 2] = tail[0:8]
    doutw[16:24, D // 2 : D] = tail[8:16]


def finish(*given):
    vmem = pl.BlockSpec(memory_space=pltpu.VMEM)
    shape = jax.ShapeDtypeStruct
    return pl.pallas_call(
        finish_kernel,
        name="finish",
        out_shape=(
            shape((SEQ, D), BF16),
            shape((SEQ, D), BF16),
            shape((KIN, 2 * INNER + 256 + HEADS), F32),
            shape((KIN, 1), F32),
            shape((32, 8), F32),
            shape((8, HEADS), F32),
            shape((32, 8), F32),
            shape((KOUT, D), F32),
        ),
        in_specs=[vmem] * len(given),
        out_specs=(vmem,) * 8,
        compiler_params=pltpu.CompilerParams(vmem_limit_bytes=VMEM_LIMIT),
    )(*given)


def body(
    hidden, in_weight, norm_gain, conv_weight, conv_bias, dt_bias, a_log, skip, inner_gain, out_weight, out_grad,
    seq_lengths, seq_owner,
):
    me = lax.axis_index("fsdp")
    rank = me % GROUP
    length = jnp.sum(jnp.where(seq_owner == me, seq_lengths, 0))
    live = jnp.arange(SEQ)[:, None] < length
    grads = jnp.where(live, out_grad, jnp.zeros_like(out_grad))
    params = jnp.concatenate([norm_gain, conv_weight.T.reshape(-1), conv_bias, inner_gain, jnp.zeros((GW - 166,), BF16)])
    extra = jnp.pad(jnp.tile(params, 8)[None, :], ((0, 3), (0, in_weight.shape[1] - INNER)))
    inw = jnp.concatenate([in_weight, extra], axis=0)
    tail = jnp.concatenate([out_weight[16:, : D // 2], out_weight[16:, D // 2 :]], axis=0)
    fold = jnp.concatenate([out_weight[:16], tail], axis=1)
    outl = jnp.stack([fold[:, : FOLD // 2], fold[:, FOLD // 2 :]])
    mine = lax.dynamic_slice(jnp.stack([dt_bias, -jnp.exp(a_log), skip]), (0, rank * OWN), (3, OWN))
    head = jnp.pad(mine, ((0, 5), (0, 128 - OWN)))
    skip_wide = jnp.broadcast_to(jnp.repeat(mine[2], 64)[None, :], (8, GW))
    w, praw, oraw, hid, grd = gather(inw, outl, hidden, grads)
    w = w.reshape(D, COLS)
    hid, grd = hid.reshape(ROWS, D), grd.reshape(ROWS, D)
    proj, lowered, heads_out, dgated, ow, par, sums = forward(hid, w, praw.reshape(256, 256), oraw, grd, head, skip_wide)
    sums = group_sums(sums)
    branch, d_low, dw, dow, small = backward(w, grd, head, skip_wide, proj, lowered, heads_out, dgated, ow, par, sums)
    branch, d_low, rows, lines, small = reduce_all(
        branch.reshape(4, 2, SEQ, D), d_low.reshape(4, 2, SEQ, D), dw.reshape(4, 4, 2, 48, COLS), dow, small
    )
    mixed, in_grad, dinw, dgain, dconv, dheads, dinner, doutw = finish(
        hidden, out_grad, live.astype(F32), in_weight, norm_gain[:, None], par, branch, d_low, rows, lines, small
    )
    return (
        mixed,
        in_grad,
        dinw,
        dgain[:, 0],
        dconv[:26, :4],
        dconv[:26, 4],
        dheads[0],
        dheads[1],
        dheads[2],
        dinner[:KOUT, 5],
        doutw,
    )


def solution(mesh):
    rows, line, whole = P("fsdp", None), P("fsdp"), P()
    return jax.shard_map(
        body,
        mesh=mesh,
        in_specs=(rows, rows, line, rows, line, whole, whole, whole, line, rows, rows, whole, whole),
        out_specs=(rows, rows, rows, line, rows, line, whole, whole, whole, line, rows),
        check_vma=False,
    )
```

```python
import functools

import jax
import jax.numpy as jnp
from jax import lax
from jax.experimental import pallas as pl
from jax.experimental.pallas import tpu as pltpu
from jax.sharding import PartitionSpec as P

MESH = pl.DeviceIdType.MESH
F32, BF16 = jnp.float32, jnp.bfloat16
HIGHEST = lax.Precision.HIGHEST
EPSILON = 1e-05

D = 1536
INNER = 3072
CONVD = 3328
HEADS = 48
SEQ = 128
GROUP = 8
ROWS = SEQ * GROUP
GW = INNER // GROUP
OWN = HEADS // GROUP
SH = 384
CW = GW + 256
COLS = 2 * GW + SH
WR, ST, GA = GW, GW + 256, GW + SH
KIN = D // 128
KOUT = INNER // 128
FOLD = D + D // 2
WIDE = FOLD // 2
VMEM_LIMIT = 60 * 2**20


def iota(shape, dim):
    return lax.broadcasted_iota(jnp.int32, shape, dim)


def ones(condition, kind=BF16):
    return jnp.where(condition, 1.0, 0.0).astype(kind)


def dot(a, b, precision=None):
    return lax.dot_general(a, b, (((1,), (0,)), ((), ())), precision=precision, preferred_element_type=F32)


def dot_nt(a, b, precision=None):
    return lax.dot_general(a, b, (((1,), (1,)), ((), ())), precision=precision, preferred_element_type=F32)


def dot_tn(a, b, precision=None):
    return lax.dot_general(a, b, (((0,), (0,)), ((), ())), precision=precision, preferred_element_type=F32)


def sigmoid(v):
    return 1.0 / (1.0 + jnp.exp(-v))


def softplus(v):
    return jnp.maximum(v, 0.0) + jnp.log1p(jnp.exp(-jnp.abs(v)))


def later(v, k):
    if k == 0:
        return v
    return jnp.where(iota(v.shape, 0) >= k, pltpu.roll(v, k, 0), 0.0)


def earlier(v, k):
    if k == 0:
        return v
    return jnp.where(iota(v.shape, 0) < v.shape[0] - k, pltpu.roll(v, v.shape[0] - k, 0), 0.0)


def place():
    me = lax.axis_index("fsdp")
    return me // 32, (me // 8) % 4, (me // 2) % 4, me % 2


def index(z, x, y, c):
    return ((z * 4 + x) * 4 + y) * 2 + c


def group_partner(k):
    z, x, y, c = place()
    rank = (y * 2 + c + k) % GROUP
    return index(z, x, rank // 2, rank % 2), rank


def on_z(k):
    z, x, y, c = place()
    return index((z + k) % 4, x, y, c)


def on_x(k):
    z, x, y, c = place()
    return index(z, (x + k) % 4, y, c)


def on_y(k):
    z, x, y, c = place()
    return index(z, x, (y + k) % 4, c)


def sibling():
    z, x, y, c = place()
    return index(z, x, y, 1 - c)


def barrier(partners):
    sem = pltpu.get_barrier_semaphore()
    for p in partners:
        pl.semaphore_signal(sem, inc=1, device_id=(p,), device_id_type=MESH)
    pl.semaphore_wait(sem, len(partners))


def remote(src, dst, send, recv, target):
    return pltpu.make_async_remote_copy(
        src_ref=src, dst_ref=dst, send_sem=send, recv_sem=recv, device_id=(target,), device_id_type=MESH
    )


def plane_partners():
    return [on_z(k) for k in (1, 2, 3)] + [on_x(k) for k in (1, 2, 3)]


def group_partners():
    return [group_partner(k)[0] for k in range(1, GROUP)]


class PlaneGather:
    def __init__(self, buf, own, send, recv, halves):
        self.buf, self.own, self.send, self.recv, self.halves = buf, own, send, recv, halves
        self.z, self.x, _, _ = place()

    def slot(self, half, first, second):
        a, b = (first, second) if half == 0 else (second, first)
        return self.buf.at[(self.z + a) % 4, (self.x + b) % 4, half]

    def along(self, half, stage, k):
        return on_z(k) if (half == 0) == (stage == 0) else on_x(k)

    def copy(self, half, first, stage, k):
        src = self.own(half) if first == 0 else self.slot(half, first, 0)
        at = (4 - k, 0) if stage == 0 else (first, 4 - k)
        return remote(
            src,
            self.slot(half, first, 0),
            self.send.at[half, first if stage else 4, k],
            self.recv.at[half, at[0], at[1]],
            self.along(half, stage, k),
        )

    def arrival(self, half, first, second):
        here = self.slot(half, first, second)
        return remote(here, here, self.send.at[half, 4, 0], self.recv.at[half, first, second], on_z(1))

    def start(self):
        for k in (1, 3, 2):
            for half in range(self.halves):
                self.copy(half, 0, 0, k).start()
        for k in (1, 3, 2):
            for half in range(self.halves):
                self.copy(half, 0, 1, k).start()

    def forward(self):
        for first in (1, 3, 2):
            for half in range(self.halves):
                self.arrival(half, first, 0).wait_recv()
                for k in (1, 3, 2):
                    self.copy(half, first, 1, k).start()

    def finish(self):
        for first in range(4):
            for second in (1, 3, 2):
                for half in range(self.halves):
                    self.arrival(half, first, second).wait_recv()

    def sent(self):
        for half in range(self.halves):
            for k in (1, 2, 3):
                self.copy(half, 0, 0, k).wait_send()
                for first in range(4):
                    self.copy(half, first, 1, k).wait_send()


class GroupGather:
    def __init__(self, buf, own, send, recv):
        self.buf, self.own, self.send, self.recv = buf, own, send, recv
        _, _, self.y, self.c = place()

    def along(self, k):
        return remote(self.own, self.buf.at[self.y, self.c], self.send.at[0, k], self.recv.at[0, 4 - k], on_y(k))

    def across(self, k):
        src = self.own if k == 0 else self.buf.at[(self.y + k) % 4, self.c]
        dst = self.buf.at[(self.y + k) % 4, self.c]
        return remote(src, dst, self.send.at[1, k], self.recv.at[1, k], sibling())

    def arrival(self, hop, k):
        here = self.buf.at[(self.y + k) % 4, self.c if hop == 0 else 1 - self.c]
        return remote(here, here, self.send.at[hop, k], self.recv.at[hop, k], sibling())

    def start(self):
        for k in (1, 3, 2):
            self.along(k).start()
        self.across(0).start()

    def forward(self):
        for k in (1, 3, 2):
            self.arrival(0, k).wait_recv()
            self.across(k).start()

    def finish(self):
        for k in range(4):
            self.arrival(1, k).wait_recv()

    def sent(self):
        for k in range(4):
            self.across(k).wait_send()
            if k:
                self.along(k).wait_send()


def unpack_params(raw, rank, par):
    row = iota((512, 1), 0)
    device = (row // 4).astype(F32)
    tap = row % 4
    values = raw[...].reshape(512, 256)

    def spots(span, first, count, channel):
        owner = jnp.floor((channel + 0.5) * (1.0 / count))
        lane = channel - owner * count + first
        pick = ones(iota((128, channel.shape[1]), 0).astype(F32) == lane)
        return jnp.where(device == owner, dot(values[:, span], pick), 0.0)

    def only(k, at):
        return jnp.sum(jnp.where(tap == k, at, 0.0), axis=0, keepdims=True)

    def lanes(n):
        return iota((1, n), 1).astype(F32)

    start = rank.astype(F32) * GW
    conv = lanes(CW)
    conv = jnp.where(conv < GW, conv + start, conv - GW + INNER)
    low, high = slice(0, 128), slice(128, 256)
    par[...] = jnp.zeros_like(par)
    par[0:1, :] = only(0, spots(high, 0, KIN, lanes(D)))
    taps = spots(low, 0, 26, conv)
    for k in range(4):
        par[k + 1 : k + 2, 0:CW] = only(k, taps)
    par[5:6, 0:CW] = only(0, spots(high, KIN, 26, conv))
    par[6:7, 0:GW] = only(0, spots(high, KIN + 26, KOUT, lanes(GW) + start))


def own_heads(raw, rank, head, skip):
    row = iota((128, 128), 0)
    col = iota((128, 128), 1)
    given = raw[...]
    mine = dot(given, ones(jnp.logical_and(row == col + OWN * rank, col < OWN), F32), HIGHEST)
    head[...] = jnp.where(iota((8, 128), 0) == 1, -jnp.exp(mine), mine)
    wide = iota((128, GW), 0) == iota((128, GW), 1) // 64 + OWN * rank
    skip[...] = dot(given, ones(wide, F32), HIGHEST)[2:3]


def unfold_out_weight(raw, ow):
    row, col = iota((GW, 256), 0), iota((GW, 256), 1)
    device, line = row // KOUT, row % KOUT
    base = (device % 8) * 32 + (device // 8) * 16
    top = ones(jnp.logical_and(line < 16, col == base + line))
    low_left = ones(jnp.logical_and(line >= 16, col == base + line - 16))
    low_right = ones(jnp.logical_and(line >= 16, col == base + line - 8))
    first = raw[:, :, 0].reshape(256, WIDE)
    second = raw[:, :, 1].reshape(256, WIDE)
    half, split = D // 2, WIDE - D // 2
    left, right_a = first[:, 0:half], first[:, half:]
    right_b, tail = second[:, 0 : half - split], second[:, half - split :]
    ow[:, 0:half] = (dot(top, left) + dot(low_left, tail)).astype(BF16)
    ow[:, half : half + split] = (dot(top, right_a) + dot(low_right, tail[:, 0:split])).astype(BF16)
    ow[:, half + split :] = (dot(top, right_b) + dot(low_right, tail[:, split:])).astype(BF16)


def convolve(raw, par, at, width):
    out = par[5:6, at : at + width] + raw * par[4:5, at : at + width]
    for k in range(3):
        out = out + later(raw, 3 - k) * par[k + 1 : k + 2, at : at + width]
    return out


def steps_of(raw, head):
    step = softplus(raw + head[0:1, :])
    decay = head[1:2, :] * step
    lower = ones(iota((SEQ, SEQ), 0) >= iota((SEQ, SEQ), 1), F32)
    total = dot(lower, decay, HIGHEST)
    return step, decay, total


def mix_forward(b, proj, par, head, skip, heads_out):
    row, col = iota((SEQ, SEQ), 0), iota((SEQ, SEQ), 1)
    causal = row >= col
    rows = pl.ds(pl.multiple_of(b * SEQ, SEQ), SEQ)
    wr = convolve(proj[rows, WR:ST], par, GW, 256)
    wr = wr * sigmoid(wr)
    write, read = wr[:, 0:128], wr[:, 128:256]
    step, _, total = steps_of(proj[rows, ST:GA], head)
    total_t, step_t = total.T, step.T
    scores = dot_nt(read, write, HIGHEST)
    for p in range(3):
        at = p * 128
        values = convolve(proj[rows, at : at + 128], par, at, 128)
        values = values * sigmoid(values)
        values_low = values.astype(BF16)
        parts = []
        for h in (2 * p, 2 * p + 1):
            decays = jnp.exp(jnp.where(causal, total[:, h : h + 1] - total_t[h : h + 1, :], -1e30))
            mix = (decays * scores * step_t[h : h + 1, :]).astype(BF16)
            parts.append(dot(mix, values_low))
        heads_out[rows, at : at + 128] = jnp.where(col < 64, parts[0], parts[1]) + skip[0:1, at : at + 128] * values


def norm_sums(b, proj, par, heads_out, dgated, acc):
    rows = pl.ds(pl.multiple_of(b * SEQ, SEQ), SEQ)
    gate = proj[rows, GA:COLS]
    product = heads_out[rows, :] * gate * sigmoid(gate)
    squares = jnp.sum(product * product, axis=1, keepdims=True)
    crosses = jnp.sum(product * dgated[rows, :] * par[6:7, 0:GW], axis=1, keepdims=True)
    col = iota((SEQ, SEQ), 1)
    return jnp.where(col == b, squares, jnp.where(col == b + 8, crosses, acc))


def norm_back(b, proj, par, wide, heads_out, dgated, gated, dproj, small):
    rows = pl.ds(pl.multiple_of(b * SEQ, SEQ), SEQ)
    col = iota((SEQ, SEQ), 1)
    square = jnp.sum(jnp.where(col == b, wide[...], 0.0), axis=1, keepdims=True)
    cross = jnp.sum(jnp.where(col == b + 8, wide[...], 0.0), axis=1, keepdims=True)
    inverse = lax.rsqrt(square * (1.0 / INNER) + EPSILON)
    mean = cross * inverse * (1.0 / INNER)
    out = heads_out[rows, :]
    gate = proj[rows, GA:COLS]
    s = sigmoid(gate)
    silu = gate * s
    unit = out * silu * inverse
    dg = dgated[rows, :]
    gain = par[6:7, 0:GW]
    gated[rows, :] = (unit * gain).astype(BF16)
    small[5:6, 0:GW] += jnp.sum(dg * unit, axis=0, keepdims=True)
    d_product = (dg * gain - unit * mean) * inverse
    dproj[rows, GA:COLS] = (d_product * out * (s * (1.0 + gate * (1.0 - s)))).astype(BF16)
    dgated[rows, :] = d_product * silu


def mix_back(b, proj, par, head, skip, d_heads, dproj, small):
    row, col = iota((SEQ, SEQ), 0), iota((SEQ, SEQ), 1)
    later_ok = col >= row
    left, right = col < 64, col >= 64
    suffix = ones(row >= col)
    before = row < col
    rows = pl.ds(pl.multiple_of(b * SEQ, SEQ), SEQ)

    def conv_back(d_act, raw, v, s, at, width):
        d_conv = d_act * s * (1.0 + v * (1.0 - s))
        span = slice(at, at + width)
        back = d_conv * par[4:5, span]
        small[3:4, span] += jnp.sum(d_conv * raw, axis=0, keepdims=True)
        for k in range(3):
            back = back + earlier(d_conv, 3 - k) * par[k + 1 : k + 2, span]
            small[k : k + 1, span] += jnp.sum(d_conv * later(raw, 3 - k), axis=0, keepdims=True)
        small[4:5, span] += jnp.sum(d_conv, axis=0, keepdims=True)
        return back

    raw_wr = proj[rows, WR:ST]
    pre_wr = convolve(raw_wr, par, GW, 256)
    sig_wr = sigmoid(pre_wr)
    wr = pre_wr * sig_wr
    write, read = wr[:, 0:128], wr[:, 128:256]
    raw_step = proj[rows, ST:GA]
    step, decay, total = steps_of(raw_step, head)
    total_t = total.T
    scores_t = dot_nt(write, read, HIGHEST)
    d_scores = jnp.zeros((SEQ, SEQ), F32)
    direct = jnp.zeros((SEQ, SEQ), F32)
    lines = []
    for p in range(3):
        at = p * 128
        span = slice(at, at + 128)
        d_out = d_heads[rows, span]
        raw = proj[rows, span]
        pre = convolve(raw, par, at, 128)
        sig = sigmoid(pre)
        values = pre * sig
        small[6:7, span] += jnp.sum(d_out * values, axis=0, keepdims=True)
        values_low = values.astype(BF16)
        d_low = d_out.astype(BF16)
        parts = []
        for i, h in enumerate((2 * p, 2 * p + 1)):
            decays = jnp.exp(jnp.where(later_ok, total_t[h : h + 1, :] - total[:, h : h + 1], -1e30))
            size = step[:, h : h + 1]
            own = jnp.where(left if i == 0 else right, d_out, 0.0).astype(BF16)
            d_mix = decays * dot_nt(values_low, own)
            d_scores = d_scores + d_mix * size
            per_step = (d_mix * scores_t).astype(BF16)
            tail = dot(per_step, suffix)
            direct = jnp.where(col == h, tail[:, 0:1], direct)
            lines.append(jnp.sum(jnp.where(before, tail * size, 0.0), axis=0, keepdims=True))
            mix = (decays * scores_t * size).astype(BF16)
            parts.append(dot(mix, d_low))
        d_values = jnp.where(left, parts[0], parts[1]) + skip[0:1, span] * d_out
        dproj[rows, span] = conv_back(d_values, raw, pre, sig, at, 128).astype(BF16)
    d_decay = jnp.concatenate(lines + [jnp.zeros((SEQ - OWN, SEQ), F32)], axis=0).T
    d_step = direct + head[1:2, :] * d_decay
    d_raw = d_step * sigmoid(raw_step + head[0:1, :])
    small[7:8, 0:128] += jnp.sum(d_raw, axis=0, keepdims=True)
    small[7:8, 128:256] += jnp.sum(d_decay * decay, axis=0, keepdims=True)
    d_low = d_scores.astype(BF16)
    d_write = dot(d_low, read.astype(BF16))
    d_read = dot_tn(d_low, write.astype(BF16))
    d_wr = jnp.concatenate([d_write, d_read], axis=1)
    dproj[rows, WR:ST] = conv_back(d_wr, raw_wr, pre_wr, sig_wr, GW, 256).astype(BF16)
    dproj[rows, ST:GA] = d_raw.astype(BF16)


class PlaneReduce:
    def __init__(self, terms, got, mid, last, out, send, recv):
        self.terms, self.got, self.mid, self.last, self.out = terms, got, mid, last, out
        self.send, self.recv = send, recv
        self.z, self.x, _, _ = place()

    def line(self, half, k):
        return self.terms.at[:, (self.x + k) % 4, 0] if half == 0 else self.terms.at[(self.z + k) % 4, :, 1]

    def first(self, half, k):
        target = on_x(k) if half == 0 else on_z(k)
        return remote(self.line(half, k), self.got.at[half, k - 1], self.send.at[half, 0, k], self.recv.at[half, 0, k], target)

    def second(self, half, k):
        target = on_z(k) if half == 0 else on_x(k)
        return remote(self.mid.at[half, k - 1], self.last.at[half, k - 1], self.send.at[half, 1, k], self.recv.at[half, 1, k], target)

    def start(self):
        for k in (2, 1, 3):
            for half in range(2):
                self.first(half, k).start()

    def middle(self):
        for half in range(2):
            for k in (1, 2, 3):
                self.first(half, k).wait_recv()
            for k in (2, 1, 3, 0):
                if half == 0:
                    at = (self.z + k) % 4
                    total = self.terms[at, self.x, 0].astype(F32)
                else:
                    at = (self.x + k) % 4
                    total = self.terms[self.z, at, 1].astype(F32)
                for j in range(3):
                    total = total + self.got[half, j, at].astype(F32)
                if k:
                    self.mid[half, k - 1] = total.astype(BF16)
                    self.second(half, k).start()
                else:
                    self.out[half] = total

    def end(self):
        for half in range(2):
            for k in (1, 2, 3):
                self.second(half, k).wait_recv()
            total = self.out[half]
            for j in range(3):
                total = total + self.last[half, j].astype(F32)
            self.out[half] = total

    def finish(self):
        for half in range(2):
            for k in (1, 2, 3):
                self.first(half, k).wait_send()
                self.second(half, k).wait_send()


class GroupReduce:
    def __init__(self, terms, got, mid, last, out, send, recv):
        self.terms, self.got, self.mid, self.last, self.out = terms, got, mid, last, out
        self.send, self.recv = send, recv
        _, _, self.y, self.c = place()

    def across(self, k):
        src = self.terms.at[(self.y + k) % 4, 1 - self.c]
        return remote(src, self.got.at[k], self.send.at[0, k], self.recv.at[0, k], sibling())

    def along(self, k):
        return remote(self.mid.at[k - 1], self.last.at[k - 1], self.send.at[1, k], self.recv.at[1, k], on_y(k))

    def start(self):
        for k in (2, 1, 3, 0):
            self.across(k).start()

    def middle(self):
        for k in (2, 1, 3, 0):
            self.across(k).wait_recv()
            total = self.terms[(self.y + k) % 4, self.c].astype(F32) + self.got[k].astype(F32)
            if k:
                self.mid[k - 1] = total.astype(BF16)
                self.along(k).start()
            else:
                self.out[...] = total

    def end(self):
        for k in (1, 2, 3):
            self.along(k).wait_recv()
        total = self.out[...]
        for j in range(3):
            total = total + self.last[j].astype(F32)
        self.out[...] = total

    def finish(self):
        for k in range(4):
            self.across(k).wait_send()
            if k:
                self.along(k).wait_send()


class Members:
    def __init__(self, src, dst, send, recv):
        self.src, self.dst, self.send, self.recv = src, dst, send, recv
        _, _, y, c = place()
        self.rank = y * 2 + c

    def copy(self, k):
        target, q = group_partner(k)
        return remote(self.src(q), self.dst(self.rank), self.send.at[k], self.recv.at[k], target)

    def arrival(self, k):
        _, q = group_partner(k)
        return remote(self.dst(q), self.dst(q), self.send.at[k], self.recv.at[GROUP - k], sibling())

    def start(self):
        for k in range(1, GROUP):
            self.copy(k).start()

    def finish(self):
        for k in range(1, GROUP):
            self.arrival(k).wait_recv()

    def sent(self):
        for k in range(1, GROUP):
            self.copy(k).wait_send()


def layer_kernel(
    hid, inw, vectors, taps, heads_in, outw, grd, lengths, owners,
    mixed, in_grad, dinw, dgain, dconv, dheads, dinner, doutw,
    split, joined, block, gblock, params, outl, live_grd,
    wx, wg, praw, plane, oraw, hall, gall, low, proj, heads_out, dgated, ow, par, head, skip, sums, slots, wide,
    gated, dproj, d_low, dw, dow, small,
    gb, mb, lb, fb, gd, md, ld, fd, gw, mw, lw, fw, tl, gl, ml, ll, fl, cut, rows_in, zs, xs, part, small_all,
    a_s, a_r, wx_s, wx_r, wg_s, wg_r, p_s, p_r, l_s, l_r, h_s, h_r, g_s, g_r, o_s, o_r, n_s, n_r,
    b_s, b_r, d_s, d_r, rw_s, rw_r, rl_s, rl_r, ro_s, ro_r, rr_s, rr_r, sz_s, sz_r, sx_s, sx_r, sg_s, sg_r, local,
):
    z, x, y, c = place()
    rank = y * 2 + c
    barrier(plane_partners() + group_partners())

    tap_rows = dot_tn(taps[...], ones(iota((26, 128), 0) == iota((26, 128), 1)))
    top = iota((4, 128), 0) == 0
    lines = [tap_rows, jnp.where(top, vectors[...].astype(F32), 0.0), jnp.zeros((4, 128), F32)]

    def padded(span, extra):
        return jnp.concatenate([inw[:, span].astype(F32), extra], axis=0).astype(BF16)

    extra = jnp.concatenate(lines, axis=1)
    rest, few = jnp.zeros((4, 256), F32), jnp.zeros((4, HEADS), F32)
    shared = padded(slice(2 * INNER, 2 * INNER + 256), rest)
    steps = padded(slice(2 * INNER + 256, 2 * INNER + 256 + HEADS), few)
    for q in range(GROUP):
        split[q, :, 0:GW] = padded(slice(INNER + q * GW, INNER + (q + 1) * GW), extra)
        split[q, :, WR:ST] = shared
        split[q, :, ST:GA] = jnp.zeros((16, 128), BF16)
        split[q, :, ST : ST + OWN] = steps[:, q * OWN : (q + 1) * OWN]
        split[q, :, GA:COLS] = padded(slice(q * GW, (q + 1) * GW), extra)
    cuts = Members(lambda q: split.at[q], lambda q: joined.at[q], a_s, a_r)
    cuts.start()
    joined[rank] = split[rank]
    length = jnp.sum(jnp.where(owners[...] == lax.axis_index("fsdp"), lengths[...], 0), axis=1, keepdims=True)
    live = iota((SEQ, 1), 0) < length
    live_grd[...] = jnp.where(live, grd[...].astype(F32), 0.0).astype(BF16)
    end = outw[16:24, :].astype(F32)
    tail = jnp.concatenate([end[:, 0 : D // 2], end[:, D // 2 :]], axis=0).astype(BF16)
    outl[0] = outw[0:16, 0:WIDE]
    outl[1, :, 0 : D - WIDE] = outw[0:16, WIDE:D]
    outl[1, :, D - WIDE :] = tail
    own_heads(heads_in, rank, head, skip)

    hidden = GroupGather(hall, hid, h_s, h_r)
    grads = GroupGather(gall, live_grd, g_s, g_r)
    first_w = PlaneGather(wx, lambda h: block.at[h], wx_s, wx_r, 2)
    gate_w = PlaneGather(wg, lambda h: gblock.at[h], wg_s, wg_r, 2)
    vecs = PlaneGather(praw, lambda h: params, p_s, p_r, 1)
    out_lines = PlaneGather(plane, lambda h: outl.at[h], l_s, l_r, 2)
    out_rows = Members(lambda q: plane.at[q // 2, pl.ds((q % 2) * 2, 2)], lambda q: oraw.at[q], o_s, o_r)

    cuts.finish()
    hidden.start()
    row, col = iota((128, 128), 0), iota((128, 128), 1)
    member, line = col // 16, col % 16
    spot = jnp.where(line < KIN, member * KIN + line, 96 + member * 4 + line - KIN)
    both = dot(ones(spot == row), joined[...].reshape(128, COLS)).astype(BF16)
    for h in range(2):
        block[h] = both[48 * h : 48 * h + 48, 0:GA]
        gblock[h] = both[48 * h : 48 * h + 48, GA:COLS]
    params[...] = both[96:128, 0:256]
    vecs.start()
    first_w.start()
    wx[z, x] = block[...]
    wg[z, x] = gblock[...]
    praw[z, x, 0] = params[...]
    hall[y, c] = hid[...]
    gall[y, c] = live_grd[...]
    plane[z, x] = outl[...]
    vecs.forward()
    first_w.forward()
    vecs.finish()
    unpack_params(praw, rank, par)
    hidden.forward()
    hidden.finish()

    def lower(b, carry):
        h = hall[b // 2, b % 2].astype(F32)
        scale = lax.rsqrt(jnp.mean(h * h, axis=1, keepdims=True) + EPSILON)
        low[pl.ds(pl.multiple_of(b * SEQ, SEQ), SEQ), :] = (h * scale * par[0:1, :]).astype(BF16)
        return carry

    lax.fori_loop(0, GROUP, lower, 0)
    grads.start()
    first_w.finish()
    gate_w.start()
    out_lines.start()

    def chunk(i):
        return pl.ds(pl.multiple_of(i * 256, 256), 256)

    def project(i, carry):
        proj[chunk(i), 0:GA] = dot(low[chunk(i), :], wx[...].reshape(D, GA))
        return carry

    lax.fori_loop(0, ROWS // 256, project, 0)
    gate_w.forward()
    out_lines.forward()

    def forward(b, carry):
        @pl.when(b == 4)
        def _():
            out_lines.finish()
            out_rows.start()
            oraw[rank] = plane[rank // 2, pl.ds((rank % 2) * 2, 2)]

        mix_forward(b, proj, par, head, skip, heads_out)
        return carry

    lax.fori_loop(0, GROUP, forward, 0)
    gate_w.finish()

    def project_gate(i, carry):
        proj[chunk(i), GA:COLS] = dot(low[chunk(i), :], wg[...].reshape(D, GW))
        return carry

    lax.fori_loop(0, ROWS // 256, project_gate, 0)
    grads.forward()
    out_rows.finish()
    unfold_out_weight(oraw, ow)
    grads.finish()

    def pull(i, carry):
        dgated[chunk(i), :] = dot_nt(gall[i].reshape(256, D), ow[...])
        return carry

    lax.fori_loop(0, ROWS // 256, pull, 0)
    acc = lax.fori_loop(
        0, GROUP, lambda b, acc: norm_sums(b, proj, par, heads_out, dgated, acc), jnp.zeros((SEQ, SEQ), F32)
    )
    sums[...] = acc.T[0:16, :]
    norms = Members(lambda q: sums, lambda q: slots.at[q], n_s, n_r)
    norms.start()
    slots[rank] = sums[...]
    small[...] = jnp.zeros_like(small)
    norms.finish()
    total = slots[0]
    for q in range(1, GROUP):
        total = total + slots[q]
    wide[...] = jnp.concatenate([total, jnp.zeros((SEQ - 16, SEQ), F32)], axis=0).T

    def norms_back(b, carry):
        norm_back(b, proj, par, wide, heads_out, dgated, gated, dproj, small)
        return carry

    lax.fori_loop(0, GROUP, norms_back, 0)

    branches = GroupReduce(hall, gb, mb, lb, fb, b_s, b_r)
    lowers = GroupReduce(d_low, gd, md, ld, fd, d_s, d_r)
    weights = PlaneReduce(dw, gw, mw, lw, fw, rw_s, rw_r)
    out_sums = PlaneReduce(tl, gl, ml, ll, fl, rl_s, rl_r)
    to_plane = Members(lambda q: dow.at[q], lambda q: tl.at[q // 2, pl.ds((q % 2) * 2, 2)], ro_s, ro_r)
    cut_rows = Members(lambda q: cut.at[q], lambda q: rows_in.at[q], rr_s, rr_r)
    all_small = Members(lambda q: small_all.at[rank], lambda q: small_all.at[q], sg_s, sg_r)

    def small_z(k):
        return remote(small, zs.at[z], sz_s.at[k], sz_r.at[k], on_z(k))

    def small_x(k):
        return remote(part, xs.at[x], sx_s.at[k], sx_r.at[k], on_x(k))

    hidden.sent()
    branch = hall

    def out_term(i, carry):
        branch[i] = dot(gated[chunk(i), :], ow[...]).astype(BF16).reshape(2, SEQ, D)
        return carry

    lax.fori_loop(0, ROWS // 256, out_term, 0)
    branches.start()
    out = dot_tn(gated[...], gall[...].reshape(ROWS, D))
    for j in range(16):
        piece = out[j * KOUT : (j + 1) * KOUT]
        tail = jnp.concatenate([piece[16:24, 0 : D // 2], piece[16:24, D // 2 :]], axis=0)
        fold = jnp.concatenate([piece[0:16], tail], axis=1).astype(BF16)
        for h in range(2):
            dow[j % 8, j // 8, h] = fold[:, h * WIDE : (h + 1) * WIDE]
    to_plane.start()
    tl[rank // 2, pl.ds((rank % 2) * 2, 2)] = dow[rank]

    def backward(b, carry):
        @pl.when(b == 2)
        def _():
            branches.middle()

        @pl.when(b == 6)
        def _():
            to_plane.finish()
            out_sums.start()

        mix_back(b, proj, par, head, skip, dgated, dproj, small)
        return carry

    lax.fori_loop(0, GROUP, backward, 0)
    for k in (1, 2, 3):
        small_z(k).start()
    zs[z] = small[...]

    def slab(k):
        at = (z + k) % 4
        rows = dot_tn(low[:, pl.ds(pl.multiple_of(at * GW, GW), GW)], dproj[...]).astype(BF16)
        dw[at] = rows.reshape(4, 2, 48, COLS)

    for k in (2, 1, 3, 0):
        slab(k)
        if k:
            weights.first(1, k).start()
    for k in (2, 1, 3):
        weights.first(0, k).start()
    out_sums.middle()

    def lower_back(i, carry):
        back = dot_nt(dproj[chunk(i), 0:GA], wx[...].reshape(D, GA))
        back = back + dot_nt(dproj[chunk(i), GA:COLS], wg[...].reshape(D, GW))
        d_low[i] = back.astype(BF16).reshape(2, SEQ, D)
        return carry

    lax.fori_loop(0, ROWS // 256, lower_back, 0)
    lowers.start()
    for k in (1, 2, 3):
        small_z(k).wait_recv()
    part[...] = ((zs[0] + zs[1]) + zs[2]) + zs[3]
    xs[x] = part[...]
    for k in (1, 2, 3):
        small_x(k).start()
    branches.end()
    h32 = hid[...].astype(F32)
    mixed[...] = (h32 + jnp.where(live, fb[...], 0.0)).astype(BF16)
    weights.middle()
    lowers.middle()
    for k in (1, 2, 3):
        small_x(k).wait_recv()
    small_all[rank] = ((xs[0] + xs[1]) + xs[2]) + xs[3]
    all_small.start()
    out_sums.end()
    doutw[0:16, 0:WIDE] = fl[0]
    doutw[0:16, WIDE:D] = fl[1, :, 0 : D - WIDE]
    doutw[16:24, 0 : D // 2] = fl[1, 0:8, D - WIDE :]
    doutw[16:24, D // 2 : D] = fl[1, 8:16, D - WIDE :]
    weights.end()
    for q in range(GROUP):
        cut[q] = jnp.zeros((16, COLS), BF16)
        cut[q, 0:KIN, :] = fw[q // 4, q % 4 * KIN : (q % 4 + 1) * KIN, :].astype(BF16)
    cut_rows.start()
    rows_in[rank] = cut[rank]
    all_small.finish()
    finish_small(small_all, dconv, dheads, dinner)
    lowers.end()
    scale = lax.rsqrt(jnp.mean(h32 * h32, axis=1, keepdims=True) + EPSILON)
    normed = h32 * scale
    d_normed = fd[...] * par[0:1, :]
    through = scale * (d_normed - normed * jnp.mean(d_normed * normed, axis=1, keepdims=True))
    in_grad[...] = (grd[...].astype(F32) + through).astype(BF16)
    cut_rows.finish()
    finish_rows(rows_in, inw, vectors, dinw, dgain)
    for gone in (grads, first_w, gate_w, vecs, out_lines, cuts, out_rows, norms, to_plane, cut_rows, all_small):
        gone.sent()
    for gone in (branches, lowers, weights, out_sums):
        gone.finish()
    for k in (1, 2, 3):
        small_z(k).wait_send()
        small_x(k).wait_send()


def finish_small(small, dconv, dheads, dinner):
    me = lax.axis_index("fsdp")
    conv = jnp.zeros((32, 8), F32)
    inner = jnp.zeros((32, 8), F32)
    common = jnp.zeros((8, 256), F32)
    line = iota((32, GW), 0)
    heads = ones(iota((GW, 128), 0) // 64 == iota((GW, 128), 1), F32)
    dheads[...] = jnp.zeros_like(dheads)
    for q in range(GROUP):
        part = small[q, :, 0:GW]
        lane = iota((32, GW), 1) + q * GW
        conv = conv + dot_nt(ones(lane == line + 26 * me, F32), part, HIGHEST)
        inner = inner + dot_nt(ones(lane == line + KOUT * me, F32), part, HIGHEST)
        common = common + small[q, :, GW:CW]
        span = slice(q * OWN, (q + 1) * OWN)
        dheads[0:1, span] = small[q, 7:8, 0:OWN]
        dheads[1:2, span] = small[q, 7:8, 128 : 128 + OWN]
        dheads[2:3, span] = dot(part, heads, HIGHEST)[6:7, 0:OWN]
    lane = iota((32, 256), 1) + INNER
    dconv[...] = conv + dot_nt(ones(lane == iota((32, 256), 0) + 26 * me, F32), common, HIGHEST)
    dinner[...] = inner


def finish_rows(rows, inw, vectors, dinw, dgain):
    shared = jnp.zeros((KIN, 256), F32)
    for q in range(GROUP):
        own = rows[q].astype(F32)[0:KIN]
        dinw[:, INNER + q * GW : INNER + (q + 1) * GW] = own[:, 0:GW]
        dinw[:, q * GW : (q + 1) * GW] = own[:, GA:COLS]
        at = 2 * INNER + 256 + q * OWN
        dinw[:, at : at + OWN] = own[:, ST : ST + OWN]
        shared = shared + own[:, WR:ST]
    dinw[:, 2 * INNER : 2 * INNER + 256] = shared
    total = jnp.sum(dinw[...] * inw[...].astype(F32), axis=1, keepdims=True)
    gain = jnp.where(iota((KIN, 128), 0) == iota((KIN, 128), 1), vectors[...].astype(F32), 0.0)
    dgain[...] = total / jnp.sum(gain, axis=1, keepdims=True)


def layer(*given):
    vmem, vm = pl.BlockSpec(memory_space=pltpu.VMEM), pltpu.VMEM
    shape = jax.ShapeDtypeStruct

    def dma(*dims):
        return pltpu.SemaphoreType.DMA(dims)

    seven, pair = [dma(GROUP)] * 2, [dma(2, 4)] * 2
    return pl.pallas_call(
        layer_kernel,
        name="layer",
        out_shape=OUT_SHAPES,
        in_specs=[vmem] * len(given),
        out_specs=(vmem,) * len(OUT_SHAPES),
        scratch_shapes=[
            vm((GROUP, 16, COLS), BF16), vm((GROUP, 16, COLS), BF16), vm((2, 48, GA), BF16), vm((2, 48, GW), BF16),
            vm((32, 256), BF16), vm((2, 16, WIDE), BF16), vm((SEQ, D), BF16),
            vm((4, 4, 2, 48, GA), BF16), vm((4, 4, 2, 48, GW), BF16), vm((4, 4, 1, 32, 256), BF16),
            vm((4, 4, 2, 16, WIDE), BF16), vm((GROUP, 2, 2, 16, WIDE), BF16),
            vm((4, 2, SEQ, D), BF16), vm((4, 2, SEQ, D), BF16),
            vm((ROWS, D), BF16), vm((ROWS, COLS), F32), vm((ROWS, GW), F32), vm((ROWS, GW), F32), vm((GW, D), BF16),
            vm((8, D), F32), vm((8, 128), F32), vm((1, GW), F32),
            vm((16, SEQ), F32), vm((GROUP, 16, SEQ), F32), vm((SEQ, SEQ), F32),
            vm((ROWS, GW), BF16), vm((ROWS, COLS), BF16), vm((4, 2, SEQ, D), BF16),
            vm((4, 4, 2, 48, COLS), BF16), vm((GROUP, 2, 2, 16, WIDE), BF16), vm((8, CW), F32),
            vm((4, SEQ, D), BF16), vm((3, SEQ, D), BF16), vm((3, SEQ, D), BF16), vm((SEQ, D), F32),
            vm((4, SEQ, D), BF16), vm((3, SEQ, D), BF16), vm((3, SEQ, D), BF16), vm((SEQ, D), F32),
            vm((2, 3, 4, 48, COLS), BF16), vm((2, 3, 48, COLS), BF16), vm((2, 3, 48, COLS), BF16), vm((2, 48, COLS), F32),
            vm((4, 4, 2, 16, WIDE), BF16),
            vm((2, 3, 4, 16, WIDE), BF16), vm((2, 3, 16, WIDE), BF16), vm((2, 3, 16, WIDE), BF16), vm((2, 16, WIDE), F32),
            vm((GROUP, 16, COLS), BF16), vm((GROUP, 16, COLS), BF16),
            vm((4, 8, CW), F32), vm((4, 8, CW), F32), vm((8, CW), F32), vm((GROUP, 8, CW), F32),
            *seven,
            dma(2, 5, 4), dma(2, 4, 4), dma(2, 5, 4), dma(2, 4, 4), dma(1, 5, 4), dma(1, 4, 4), dma(2, 5, 4), dma(2, 4, 4),
            *pair, *pair, *seven, *seven,
            *pair, *pair, *[dma(2, 2, 4)] * 4, *seven, *seven, *[dma(4)] * 4, *seven, dma(8),
        ],
        compiler_params=pltpu.CompilerParams(collective_id=0, has_side_effects=True, vmem_limit_bytes=VMEM_LIMIT),
    )(*given)


OUT_SHAPES = (
    jax.ShapeDtypeStruct((SEQ, D), BF16),
    jax.ShapeDtypeStruct((SEQ, D), BF16),
    jax.ShapeDtypeStruct((KIN, 2 * INNER + 256 + HEADS), F32),
    jax.ShapeDtypeStruct((KIN, 1), F32),
    jax.ShapeDtypeStruct((32, 8), F32),
    jax.ShapeDtypeStruct((8, HEADS), F32),
    jax.ShapeDtypeStruct((32, 8), F32),
    jax.ShapeDtypeStruct((KOUT, D), F32),
)


def body(
    hidden, in_weight, norm_gain, conv_weight, conv_bias, dt_bias, a_log, skip, inner_gain, out_weight, out_grad,
    seq_lengths, seq_owner,
):
    vectors = jnp.concatenate([norm_gain, conv_bias, inner_gain, jnp.zeros((66,), BF16)])[None, :]
    heads = jnp.pad(jnp.stack([dt_bias, a_log, skip]), ((0, 5), (0, 128 - HEADS)))
    mixed, in_grad, dinw, dgain, dconv, dheads, dinner, doutw = layer(
        hidden, in_weight, vectors, conv_weight, heads, out_weight, out_grad, seq_lengths[None, :], seq_owner[None, :]
    )
    return (
        mixed,
        in_grad,
        dinw,
        dgain[:, 0],
        dconv[:26, :4],
        dconv[:26, 4],
        dheads[0],
        dheads[1],
        dheads[2],
        dinner[:KOUT, 5],
        doutw,
    )


def solution(mesh):
    rows, line, whole = P("fsdp", None), P("fsdp"), P()
    return jax.shard_map(
        body,
        mesh=mesh,
        in_specs=(rows, rows, line, rows, line, whole, whole, whole, line, rows, rows, whole, whole),
        out_specs=(rows, rows, rows, line, rows, line, whole, whole, whole, line, rows),
        check_vma=False,
    )
```

```python
import functools

import jax
import jax.numpy as jnp
from jax import lax
from jax.experimental import pallas as pl
from jax.experimental.pallas import tpu as pltpu
from jax.sharding import PartitionSpec as P

MESH = pl.DeviceIdType.MESH
F32, BF16 = jnp.float32, jnp.bfloat16
HIGHEST = lax.Precision.HIGHEST
EPSILON = 1e-05

D = 1536
INNER = 3072
CONVD = 3328
HEADS = 48
SEQ = 128
GROUP = 8
ROWS = SEQ * GROUP
GW = INNER // GROUP
OWN = HEADS // GROUP
CW = GW + 128
GA, COLS = CW, CW + GW
ST = COLS
KIN = D // 128
KOUT = INNER // 128
STEP = 2 * INNER + 256
FOLD = D + D // 2
WIDE = FOLD // 2
VMEM_LIMIT = 60 * 2**20


def iota(shape, dim):
    return lax.broadcasted_iota(jnp.int32, shape, dim)


def ones(condition, kind=BF16):
    return jnp.where(condition, 1.0, 0.0).astype(kind)


def dot(a, b, precision=None):
    return lax.dot_general(a, b, (((1,), (0,)), ((), ())), precision=precision, preferred_element_type=F32)


def dot_nt(a, b, precision=None):
    return lax.dot_general(a, b, (((1,), (1,)), ((), ())), precision=precision, preferred_element_type=F32)


def dot_tn(a, b, precision=None):
    return lax.dot_general(a, b, (((0,), (0,)), ((), ())), precision=precision, preferred_element_type=F32)


def sigmoid(v):
    return 1.0 / (1.0 + jnp.exp(-v))


def softplus(v):
    return jnp.maximum(v, 0.0) + jnp.log1p(jnp.exp(-jnp.abs(v)))


def later(v, k):
    if k == 0:
        return v
    return jnp.where(iota(v.shape, 0) >= k, pltpu.roll(v, k, 0), 0.0)


def earlier(v, k):
    if k == 0:
        return v
    return jnp.where(iota(v.shape, 0) < v.shape[0] - k, pltpu.roll(v, v.shape[0] - k, 0), 0.0)


def place():
    me = lax.axis_index("fsdp")
    return me // 32, (me // 8) % 4, (me // 2) % 4, me % 2


def index(z, x, y, c):
    return ((z * 4 + x) * 4 + y) * 2 + c


def group_partner(k):
    z, x, y, c = place()
    rank = (y * 2 + c + k) % GROUP
    return index(z, x, rank // 2, rank % 2), rank


def on_z(k):
    z, x, y, c = place()
    return index((z + k) % 4, x, y, c)


def on_x(k):
    z, x, y, c = place()
    return index(z, (x + k) % 4, y, c)


def on_y(k):
    z, x, y, c = place()
    return index(z, x, (y + k) % 4, c)


def sibling():
    z, x, y, c = place()
    return index(z, x, y, 1 - c)


def swap_to():
    z, x, y, c = place()
    return index(y, x % 2 * 2 + c, z, x // 2)


def swap_from():
    z, x, y, c = place()
    return index(y, c * 2 + x // 2, z, x % 2)


def signal(target):
    pl.semaphore_signal(pltpu.get_barrier_semaphore(), inc=1, device_id=(target,), device_id_type=MESH)


def remote(src, dst, send, recv, target):
    return pltpu.make_async_remote_copy(
        src_ref=src, dst_ref=dst, send_sem=send, recv_sem=recv, device_id=(target,), device_id_type=MESH
    )


def plane_partners():
    return [on_z(k) for k in (1, 2, 3)] + [on_x(k) for k in (1, 2, 3)]


def group_partners():
    return [group_partner(k)[0] for k in range(1, GROUP)]


class PlaneGather:
    def __init__(self, buf, own, send, recv, halves):
        self.buf, self.own, self.send, self.recv, self.halves = buf, own, send, recv, halves
        self.z, self.x, _, _ = place()

    def slot(self, half, first, second):
        a, b = (first, second) if half == 0 else (second, first)
        return self.buf.at[(self.z + a) % 4, (self.x + b) % 4, half]

    def along(self, half, stage, k):
        return on_z(k) if (half == 0) == (stage == 0) else on_x(k)

    def copy(self, half, first, stage, k):
        src = self.own(half) if first == 0 else self.slot(half, first, 0)
        at = (4 - k, 0) if stage == 0 else (first, 4 - k)
        return remote(
            src,
            self.slot(half, first, 0),
            self.send.at[half, first if stage else 4, k],
            self.recv.at[half, at[0], at[1]],
            self.along(half, stage, k),
        )

    def relayed(self, half, first):
        came, k = (3, 1) if first < 2 else (1, 3)
        here = self.slot(half, first, came)
        return remote(here, here, self.send.at[half, first, 2], self.recv.at[half, first, 2], self.along(half, 1, k))

    def arrival(self, half, first, second):
        here = self.slot(half, first, second)
        return remote(here, here, self.send.at[half, 4, 0], self.recv.at[half, first, second], on_z(1))

    def start(self):
        for k in (1, 3, 2):
            for half in range(self.halves):
                self.copy(half, 0, 0, k).start()
        for k in (1, 3):
            for half in range(self.halves):
                self.copy(half, 0, 1, k).start()

    def forward(self):
        for first in (1, 3, 2):
            for half in range(self.halves):
                self.arrival(half, first, 0).wait_recv()
                for k in (1, 3):
                    self.copy(half, first, 1, k).start()

    def relay(self):
        for first in (0, 3, 1, 2):
            for half in range(self.halves):
                self.arrival(half, first, 3 if first < 2 else 1).wait_recv()
                self.relayed(half, first).start()

    def finish(self):
        for first in range(4):
            for half in range(self.halves):
                self.arrival(half, first, 1 if first < 2 else 3).wait_recv()
        for first in range(4):
            for half in range(self.halves):
                self.arrival(half, first, 2).wait_recv()

    def sent(self):
        for half in range(self.halves):
            for k in (1, 2, 3):
                self.copy(half, 0, 0, k).wait_send()
            for first in range(4):
                for k in (1, 3):
                    self.copy(half, first, 1, k).wait_send()
                self.relayed(half, first).wait_send()


class GroupGather:
    def __init__(self, buf, own, send, recv):
        self.buf, self.own, self.send, self.recv = buf, own, send, recv
        _, _, self.y, self.c = place()

    def along(self, k):
        return remote(self.own, self.buf.at[self.y, self.c], self.send.at[0, k], self.recv.at[0, 4 - k], on_y(k))

    def half(self, k):
        return pl.ds(0, SEQ // 2) if k == 3 else pl.ds(SEQ // 2, SEQ // 2)

    def relayed(self, k):
        here = self.buf.at[(self.y + k) % 4, self.c, self.half(k)]
        at = 2 if k == 3 else 0
        return remote(here, here, self.send.at[0, at], self.recv.at[0, at], on_y(4 - k))

    def across(self, k):
        src = self.own if k == 0 else self.buf.at[(self.y + k) % 4, self.c]
        dst = self.buf.at[(self.y + k) % 4, self.c]
        return remote(src, dst, self.send.at[1, k], self.recv.at[1, k], sibling())

    def start(self):
        for k in (1, 3):
            self.along(k).start()
        self.across(0).start()

    def forward(self, k):
        if k == 2:
            for came in (3, 1):
                here = self.buf.at[(self.y + 2) % 4, self.c, self.half(came)]
                at = 2 if came == 3 else 0
                remote(here, here, self.send.at[0, at], self.recv.at[0, at], sibling()).wait_recv()
        else:
            here = self.buf.at[(self.y + k) % 4, self.c]
            remote(here, here, self.send.at[0, k], self.recv.at[0, k], sibling()).wait_recv()
            self.relayed(k).start()
        self.across(k).start()

    def arrived(self, k):
        here = self.buf.at[(self.y + k) % 4, 1 - self.c]
        remote(here, here, self.send.at[1, k], self.recv.at[1, k], sibling()).wait_recv()

    def sent(self):
        for k in (1, 3):
            self.along(k).wait_send()
            self.relayed(k).wait_send()
        for k in range(4):
            self.across(k).wait_send()


def unpack_params(raw, rank, core, par, step_rows):
    row = iota((512, 1), 0)
    device = (row // 4).astype(F32)
    tap = row % 4
    values = raw[...].reshape(512, 384)

    def spots(span, first, count, channel):
        owner = jnp.floor((channel + 0.5) * (1.0 / count))
        lane = channel - owner * count + first
        pick = ones(iota((128, channel.shape[1]), 0).astype(F32) == lane)
        return jnp.where(device == owner, dot(values[:, span], pick), 0.0)

    def only(k, at):
        return jnp.sum(jnp.where(tap == k, at, 0.0), axis=0, keepdims=True)

    def lanes(n):
        return iota((1, n), 1).astype(F32)

    start = rank.astype(F32) * GW
    conv = lanes(CW)
    conv = jnp.where(conv < GW, conv + start, conv - GW + INNER + 128 * core.astype(F32))
    low, high, last = slice(0, 128), slice(128, 256), slice(256, 384)
    par[...] = jnp.zeros_like(par)
    par[0:1, :] = only(0, spots(high, 0, KIN, lanes(D)))
    taps = spots(low, 0, 26, conv)
    for k in range(4):
        par[k + 1 : k + 2, 0:CW] = only(k, taps)
    par[5:6, 0:CW] = only(0, spots(high, KIN, 26, conv))
    par[6:7, 0:GW] = only(0, spots(high, KIN + 26, KOUT, lanes(GW) + start))
    four, two = spots(last, 0, KIN, lanes(D)), spots(last, 16, KIN, lanes(D))
    rows = [only(k, four) for k in range(4)] + [only(k, two) for k in range(2)] + [jnp.zeros((122, D), F32)]
    step_rows[...] = jnp.concatenate(rows, axis=0).astype(BF16)


def own_heads(raw, rank, head, skip):
    row = iota((128, 128), 0)
    col = iota((128, 128), 1)
    given = raw[...]
    mine = dot(given, ones(jnp.logical_and(row == col + OWN * rank, col < OWN), F32), HIGHEST)
    head[...] = jnp.where(iota((8, 128), 0) == 1, -jnp.exp(mine), mine)
    wide = iota((128, GW), 0) == iota((128, GW), 1) // 64 + OWN * rank
    skip[...] = dot(given, ones(wide, F32), HIGHEST)[2:3]


def unfold_out_weight(raw, ow):
    row, col = iota((GW, 256), 0), iota((GW, 256), 1)
    device, line = row // KOUT, row % KOUT
    base = (device % 8 // 2 * 4 + device // 8 * 2 + device % 2) * 16
    top = ones(jnp.logical_and(line < 16, col == base + line))
    low_left = ones(jnp.logical_and(line >= 16, col == base + line - 16))
    low_right = ones(jnp.logical_and(line >= 16, col == base + line - 8))
    first = raw[:, :, 0].reshape(256, WIDE)
    second = raw[:, :, 1].reshape(256, WIDE)
    half, split = D // 2, WIDE - D // 2
    left, right_a = first[:, 0:half], first[:, half:]
    right_b, tail = second[:, 0 : half - split], second[:, half - split :]
    ow[:, 0:half] = (dot(top, left) + dot(low_left, tail)).astype(BF16)
    ow[:, half : half + split] = (dot(top, right_a) + dot(low_right, tail[:, 0:split])).astype(BF16)
    ow[:, half + split :] = (dot(top, right_b) + dot(low_right, tail[:, split:])).astype(BF16)


def convolve(raw, par, at, width):
    out = par[5:6, at : at + width] + raw * par[4:5, at : at + width]
    for k in range(3):
        out = out + later(raw, 3 - k) * par[k + 1 : k + 2, at : at + width]
    return out


def steps_of(raw, head):
    step = softplus(raw + head[0:1, :])
    decay = head[1:2, :] * step
    lower = ones(iota((SEQ, SEQ), 0) >= iota((SEQ, SEQ), 1), F32)
    total = dot(lower, decay, HIGHEST)
    return step, decay, total


def mix_forward(b, proj, act, par, head, skip, heads_out):
    row, col = iota((SEQ, SEQ), 0), iota((SEQ, SEQ), 1)
    causal = row >= col
    rows = pl.ds(pl.multiple_of(b * SEQ, SEQ), SEQ)
    write, read = act[0, rows, :], act[1, rows, :]
    step, _, total = steps_of(proj[rows, ST:], head)
    total_t, step_t = total.T, step.T
    scores = dot_nt(read, write, HIGHEST)
    for p in range(3):
        at = p * 128
        values = convolve(proj[rows, at : at + 128], par, at, 128)
        values = values * sigmoid(values)
        values_low = values.astype(BF16)
        parts = []
        for h in (2 * p, 2 * p + 1):
            decays = jnp.exp(jnp.where(causal, total[:, h : h + 1] - total_t[h : h + 1, :], -1e30))
            mix = (decays * scores * step_t[h : h + 1, :]).astype(BF16)
            parts.append(dot(mix, values_low))
        heads_out[rows, at : at + 128] = jnp.where(col < 64, parts[0], parts[1]) + skip[0:1, at : at + 128] * values


def norm_sums(b, proj, par, heads_out, dgated, acc):
    rows = pl.ds(pl.multiple_of(b * SEQ, SEQ), SEQ)
    gate = proj[rows, GA:COLS]
    product = heads_out[rows, :] * gate * sigmoid(gate)
    squares = jnp.sum(product * product, axis=1, keepdims=True)
    crosses = jnp.sum(product * dgated[rows, :] * par[6:7, 0:GW], axis=1, keepdims=True)
    col = iota((SEQ, SEQ), 1)
    return jnp.where(col == b, squares, jnp.where(col == b + 8, crosses, acc))


def norm_back(b, proj, par, wide, heads_out, dgated, gated, dproj, small):
    rows = pl.ds(pl.multiple_of(b * SEQ, SEQ), SEQ)
    col = iota((SEQ, SEQ), 1)
    square = jnp.sum(jnp.where(col == b, wide[...], 0.0), axis=1, keepdims=True)
    cross = jnp.sum(jnp.where(col == b + 8, wide[...], 0.0), axis=1, keepdims=True)
    inverse = lax.rsqrt(square * (1.0 / INNER) + EPSILON)
    mean = cross * inverse * (1.0 / INNER)
    out = heads_out[rows, :]
    gate = proj[rows, GA:COLS]
    s = sigmoid(gate)
    silu = gate * s
    unit = out * silu * inverse
    dg = dgated[rows, :]
    gain = par[6:7, 0:GW]
    gated[rows, :] = (unit * gain).astype(BF16)
    small[5:6, 0:GW] += jnp.sum(dg * unit, axis=0, keepdims=True)
    d_product = (dg * gain - unit * mean) * inverse
    dproj[rows, GA:COLS] = (d_product * out * (s * (1.0 + gate * (1.0 - s)))).astype(BF16)
    dgated[rows, :] = d_product * silu


def conv_back(d_act, raw, v, s, par, small, at):
    d_conv = d_act * s * (1.0 + v * (1.0 - s))
    span = slice(at, at + 128)
    back = d_conv * par[4:5, span]
    small[3:4, span] += jnp.sum(d_conv * raw, axis=0, keepdims=True)
    for k in range(3):
        back = back + earlier(d_conv, 3 - k) * par[k + 1 : k + 2, span]
        small[k : k + 1, span] += jnp.sum(d_conv * later(raw, 3 - k), axis=0, keepdims=True)
    small[4:5, span] += jnp.sum(d_conv, axis=0, keepdims=True)
    return back


def mix_back(b, core, proj, act, par, head, skip, d_heads, dproj, d_steps, small, d_mine, d_other):
    row, col = iota((SEQ, SEQ), 0), iota((SEQ, SEQ), 1)
    later_ok = col >= row
    left, right = col < 64, col >= 64
    suffix = ones(row >= col)
    before = row < col
    rows = pl.ds(pl.multiple_of(b * SEQ, SEQ), SEQ)

    write, read = act[0, rows, :], act[1, rows, :]
    raw_step = proj[rows, ST:]
    step, decay, total = steps_of(raw_step, head)
    total_t = total.T
    scores_t = dot_nt(write, read, HIGHEST)
    d_scores = jnp.zeros((SEQ, SEQ), F32)
    direct = jnp.zeros((SEQ, SEQ), F32)
    lines = []
    for p in range(3):
        at = p * 128
        span = slice(at, at + 128)
        d_out = d_heads[rows, span]
        raw = proj[rows, span]
        pre = convolve(raw, par, at, 128)
        sig = sigmoid(pre)
        values = pre * sig
        small[6:7, span] += jnp.sum(d_out * values, axis=0, keepdims=True)
        values_low = values.astype(BF16)
        d_low = d_out.astype(BF16)
        parts = []
        for i, h in enumerate((2 * p, 2 * p + 1)):
            decays = jnp.exp(jnp.where(later_ok, total_t[h : h + 1, :] - total[:, h : h + 1], -1e30))
            size = step[:, h : h + 1]
            own = jnp.where(left if i == 0 else right, d_out, 0.0).astype(BF16)
            d_mix = decays * dot_nt(values_low, own)
            d_scores = d_scores + d_mix * size
            per_step = (d_mix * scores_t).astype(BF16)
            tail = dot(per_step, suffix)
            direct = jnp.where(col == h, tail[:, 0:1], direct)
            lines.append(jnp.sum(jnp.where(before, tail * size, 0.0), axis=0, keepdims=True))
            mix = (decays * scores_t * size).astype(BF16)
            parts.append(dot(mix, d_low))
        d_values = jnp.where(left, parts[0], parts[1]) + skip[0:1, span] * d_out
        dproj[rows, span] = conv_back(d_values, raw, pre, sig, par, small, at).astype(BF16)
    d_decay = jnp.concatenate(lines + [jnp.zeros((SEQ - OWN, SEQ), F32)], axis=0).T
    d_step = direct + head[1:2, :] * d_decay
    d_raw = d_step * sigmoid(raw_step + head[0:1, :])
    small[7:8, 0:128] += jnp.sum(d_raw, axis=0, keepdims=True)
    small[7:8, 128:256] += jnp.sum(d_decay * decay, axis=0, keepdims=True)
    d_low = d_scores.astype(BF16)
    d_write = dot(d_low, read.astype(BF16))
    d_read = dot_tn(d_low, write.astype(BF16))
    d_mine[rows, :] = jnp.where(core == 0, d_write, d_read)
    d_other[rows, :] = jnp.where(core == 0, d_read, d_write)
    d_steps[rows, :] = d_raw.astype(BF16)


def vector_forward(b, core, proj, act, par):
    rows = pl.ds(pl.multiple_of(b * SEQ, SEQ), SEQ)
    v = convolve(proj[rows, GW:CW], par, GW, 128)
    act[core, rows, :] = v * sigmoid(v)


def vector_back(b, proj, par, d_mine, d_in, dproj, small):
    rows = pl.ds(pl.multiple_of(b * SEQ, SEQ), SEQ)
    raw = proj[rows, GW:CW]
    v = convolve(raw, par, GW, 128)
    d = d_mine[rows, :] + d_in[rows, :]
    dproj[rows, GW:CW] = conv_back(d, raw, v, sigmoid(v), par, small, GW).astype(BF16)


class PlaneReduce:
    def __init__(self, terms, got, mid, last, out, send, recv, halves=2):
        self.terms, self.got, self.mid, self.last, self.out = terms, got, mid, last, out
        self.send, self.recv, self.halves = send, recv, halves
        self.z, self.x, _, _ = place()

    def line(self, half, k):
        return self.terms.at[:, (self.x + k) % 4, 0] if half == 0 else self.terms.at[(self.z + k) % 4, :, 1]

    def first(self, half, k):
        target = on_x(k) if half == 0 else on_z(k)
        return remote(self.line(half, k), self.got.at[half, k - 1], self.send.at[half, 0, k], self.recv.at[half, 0, k], target)

    def second(self, half, k):
        target = on_z(k) if half == 0 else on_x(k)
        return remote(self.mid.at[half, k - 1], self.last.at[half, k - 1], self.send.at[half, 1, k], self.recv.at[half, 1, k], target)

    def start(self):
        for k in (2, 1, 3):
            for half in range(self.halves):
                self.first(half, k).start()

    def middle(self):
        for half in range(self.halves):
            for k in (1, 2, 3):
                self.first(half, k).wait_recv()
            for k in (2, 1, 3, 0):
                if half == 0:
                    at = (self.z + k) % 4
                    total = self.terms[at, self.x, 0].astype(F32)
                else:
                    at = (self.x + k) % 4
                    total = self.terms[self.z, at, 1].astype(F32)
                for j in range(3):
                    total = total + self.got[half, j, at].astype(F32)
                if k:
                    self.mid[half, k - 1] = total.astype(BF16)
                    self.second(half, k).start()
                else:
                    self.out[half] = total

    def end(self):
        for half in range(self.halves):
            for k in (1, 2, 3):
                self.second(half, k).wait_recv()
            total = self.out[half]
            for j in range(3):
                total = total + self.last[half, j].astype(F32)
            self.out[half] = total

    def finish(self):
        for half in range(self.halves):
            for k in (1, 2, 3):
                self.first(half, k).wait_send()
                self.second(half, k).wait_send()


class GroupReduce:
    def __init__(self, terms, got, mid, last, out, send, recv):
        self.terms, self.got, self.mid, self.last, self.out = terms, got, mid, last, out
        self.send, self.recv = send, recv
        _, _, self.y, self.c = place()

    def across(self, k):
        src = self.terms.at[(self.y + k) % 4, 1 - self.c]
        return remote(src, self.got.at[k], self.send.at[0, k], self.recv.at[0, k], sibling())

    def along(self, k):
        return remote(self.mid.at[k - 1], self.last.at[k - 1], self.send.at[1, k], self.recv.at[1, k], on_y(k))

    def half(self, k):
        self.across(k).wait_recv()
        return self.terms[(self.y + k) % 4, self.c].astype(F32) + self.got[k].astype(F32)

    def pass_on(self, k):
        self.mid[k - 1] = self.half(k).astype(BF16)
        self.along(k).start()

    def keep(self):
        self.out[...] = self.half(0)

    def end(self):
        for k in (1, 2, 3):
            self.along(k).wait_recv()
        total = self.out[...]
        for j in range(3):
            total = total + self.last[j].astype(F32)
        self.out[...] = total

    def finish(self):
        for k in range(4):
            self.across(k).wait_send()
            if k:
                self.along(k).wait_send()


class Members:
    def __init__(self, src, dst, send, recv):
        self.src, self.dst, self.send, self.recv = src, dst, send, recv
        _, _, y, c = place()
        self.rank = y * 2 + c

    def copy(self, k):
        target, q = group_partner(k)
        return remote(self.src(q), self.dst(self.rank), self.send.at[k], self.recv.at[k], target)

    def arrival(self, k):
        _, q = group_partner(k)
        return remote(self.dst(q), self.dst(q), self.send.at[k], self.recv.at[GROUP - k], sibling())

    def start(self):
        for k in range(1, GROUP):
            self.copy(k).start()

    def finish(self):
        for k in range(1, GROUP):
            self.arrival(k).wait_recv()

    def sent(self):
        for k in range(1, GROUP):
            self.copy(k).wait_send()


def layer_kernel(
    hid, inw, gain_in, taps, bias_in, dt_in, a_in, skip_in, inner_in, outw, grd, lengths, owners,
    mixed, in_grad, dinw, dvecs, doutw,
    vectors, heads_in, tap_rows,
    split, joined, block, gblock, params, outl, placed, live_grd,
    wx, wg, praw, plane, hall, gall, low, proj, act, step_rows, heads_out, dgated, ow, par, head, skip, sums, slots, wide,
    gated, dproj, d_steps, d_mine, d_other, d_in, d_low, dwx, dwg, dow, dws, small,
    gb, mb, lb, fb, gd, md, ld, fd, gx, mx, lx, fx, gg, mg, lg, fg, gl, ml, ll, fl, gs, ms, ls, fs,
    swapped, cut, rows_in, gcut, grows_in, zs, xs, part, small_all,
    a_s, a_r, wx_s, wx_r, wg_s, wg_r, p_s, p_r, l_s, l_r, h_s, h_r, g_s, g_r, n_s, n_r, v_s, v_r, u_s, u_r,
    b_s, b_r, d_s, d_r, rx_s, rx_r, rg_s, rg_r, rl_s, rl_r, rs_s, rs_r, rr_s, rr_r, rq_s, rq_r,
    sz_s, sz_r, sx_s, sx_r, sg_s, sg_r, swap_s, swap_r,
):
    z, x, y, c = place()
    rank = y * 2 + c
    me = lax.axis_index("fsdp")
    partners = plane_partners() + group_partners()
    moves = swap_to() != me
    for p in partners:
        signal(p)

    @pl.when(moves)
    def _():
        signal(swap_to())
        signal(swap_from())

    vectors[...] = jnp.zeros_like(vectors)
    heads_in[...] = jnp.zeros_like(heads_in)
    tap_rows[...] = jnp.zeros_like(tap_rows)
    vectors[0:1, 0:KIN] = gain_in[...].astype(F32)[None, :]
    vectors[0:1, KIN : KIN + 26] = bias_in[...].astype(F32)[None, :]
    vectors[0:1, KIN + 26 : KIN + 26 + KOUT] = inner_in[...].astype(F32)[None, :]
    for i, line in enumerate((dt_in, a_in, skip_in)):
        heads_in[i : i + 1, 0:HEADS] = line[...][None, :]
    tap_rows[0:4, 0:26] = taps[...].astype(F32)
    col_steps = inw[:, STEP : STEP + HEADS]
    steps_low = dot_tn(col_steps, ones(iota((KIN, 128), 0) == iota((KIN, 128), 1)))
    steps_high = dot_tn(col_steps, ones(iota((KIN, 128), 0) + 16 == iota((KIN, 128), 1)))
    rest = jnp.zeros((4, 128), F32)

    def padded(span, extra):
        return jnp.concatenate([inw[:, span].astype(F32), extra], axis=0).astype(BF16)

    vector_cols = [padded(slice(2 * INNER + 128 * i, 2 * INNER + 128 * (i + 1)), rest) for i in range(2)]
    for q in range(GROUP):
        at = q * OWN
        two = jnp.concatenate([steps_high[at + 4 : at + OWN], jnp.zeros((2, 128), F32)], axis=0)
        extra = jnp.concatenate([tap_rows[0:4], vectors[0:4], steps_low[at : at + 4] + two], axis=1)
        split[q, :, 0:GW] = padded(slice(INNER + q * GW, INNER + (q + 1) * GW), extra)
        split[q, :, GW:CW] = vector_cols[q % 2]
        split[q, :, GA:COLS] = padded(slice(q * GW, (q + 1) * GW), jnp.zeros((4, GW), F32))
    end = outw[16:24, :].astype(F32)
    tail = jnp.concatenate([end[:, 0 : D // 2], end[:, D // 2 :]], axis=0).astype(BF16)
    outl[0] = outw[0:16, 0:WIDE]
    outl[1, :, 0 : D - WIDE] = outw[0:16, WIDE:D]
    outl[1, :, D - WIDE :] = tail

    @pl.when(moves)
    def _():
        pl.semaphore_wait(pltpu.get_barrier_semaphore(), len(partners) + 2)

    @pl.when(jnp.logical_not(moves))
    def _():
        pl.semaphore_wait(pltpu.get_barrier_semaphore(), len(partners))

    cuts = Members(lambda q: split.at[q], lambda q: joined.at[q], a_s, a_r)
    cuts.start()
    swap = remote(outl, placed, swap_s.at[0], swap_r.at[0], swap_to())
    swap_back = remote(fl, swapped, swap_s.at[1], swap_r.at[1], swap_from())

    @pl.when(moves)
    def _():
        swap.start()

    joined[rank] = split[rank]
    length = jnp.sum(jnp.where(owners[...][None, :] == me, lengths[...][None, :], 0), axis=1, keepdims=True)
    live = iota((SEQ, 1), 0) < length
    live_grd[...] = jnp.where(live, grd[...].astype(F32), 0.0).astype(BF16)
    own_heads(heads_in, rank, head, skip)

    hidden = GroupGather(hall, hid, h_s, h_r)
    grads = GroupGather(gall, live_grd, g_s, g_r)
    first_w = PlaneGather(wx, lambda h: block.at[h], wx_s, wx_r, 2)
    gate_w = PlaneGather(wg, lambda h: gblock.at[h], wg_s, wg_r, 2)
    vecs = PlaneGather(praw, lambda h: params, p_s, p_r, 1)
    lines = PlaneGather(plane, lambda h: placed.at[h], l_s, l_r, 2)

    cuts.finish()
    hidden.start()
    row, col = iota((128, 128), 0), iota((128, 128), 1)
    member, line = col // 16, col % 16
    spot = jnp.where(line < KIN, member * KIN + line, 96 + member * 4 + line - KIN)
    both = dot(ones(spot == row), joined[...].reshape(128, COLS)).astype(BF16)
    for h in range(2):
        block[h] = both[48 * h : 48 * h + 48, 0:GA]
        gblock[h] = both[48 * h : 48 * h + 48, GA:COLS]
    params[...] = both[96:128, 0:384]
    vecs.start()
    first_w.start()
    wx[z, x] = block[...]
    wg[z, x] = gblock[...]
    praw[z, x, 0] = params[...]
    hall[y, c] = hid[...]
    gall[y, c] = live_grd[...]
    vecs.forward()
    first_w.forward()
    vecs.relay()
    first_w.relay()
    gate_w.start()

    @pl.when(moves)
    def _():
        swap.wait_recv()

    @pl.when(jnp.logical_not(moves))
    def _():
        placed[...] = outl[...]

    lines.start()
    plane[z, x] = placed[...]
    vecs.finish()
    unpack_params(praw, rank, c, par, step_rows)
    gate_w.forward()
    lines.forward()
    hidden.forward(1)
    hidden.forward(3)
    grads.start()
    first_w.finish()
    gate_w.relay()
    lines.relay()

    def chunk(i):
        return pl.ds(pl.multiple_of(i * 256, 256), 256)

    def in_turn(i):
        return (y + i + i // 2 * (5 - 2 * i)) % 4

    def vector_copy(i):
        here = act.at[c, chunk(in_turn(i))]
        return remote(here, here, v_s.at[i], v_r.at[i], sibling())

    def vector_arrival(i):
        here = act.at[1 - c, chunk(in_turn(i))]
        return remote(here, here, v_s.at[i], v_r.at[i], sibling())

    def forward(i, carry):
        @pl.when(i == 0)
        def _():
            hidden.arrived(0)

        @pl.when(i == 1)
        def _():
            hidden.arrived(1)

        @pl.when(i == 2)
        def _():
            hidden.arrived(3)
            hidden.forward(2)

        @pl.when(i == 3)
        def _():
            hidden.arrived(2)

        @pl.when(i < 4)
        def _():
            at = in_turn(i)
            for core in range(2):
                h = hall[at, core].astype(F32)
                scale = lax.rsqrt(jnp.mean(h * h, axis=1, keepdims=True) + EPSILON)
                rows = pl.ds(pl.multiple_of(at * 256 + core * SEQ, SEQ), SEQ)
                low[rows, :] = (h * scale * par[0:1, :]).astype(BF16)
            rows = chunk(at)
            proj[rows, 0:GA] = dot(low[rows, :], wx[...].reshape(D, GA))
            proj[rows, ST:] = dot_nt(low[rows, :], step_rows[...])
            for core in range(2):
                vector_forward(at * 2 + core, c, proj, act, par)
            vector_copy(i).start()

        @pl.when(i > 0)
        def _():
            vector_arrival(i - 1).wait_recv()
            at = in_turn(i - 1)
            for core in range(2):
                mix_forward(at * 2 + core, proj, act, par, head, skip, heads_out)

        return carry

    lax.fori_loop(0, 5, forward, 0)
    gate_w.finish()

    def project_gate(i, carry):
        proj[chunk(i), GA:COLS] = dot(low[chunk(i), :], wg[...].reshape(D, GW))
        return carry

    lax.fori_loop(0, ROWS // 256, project_gate, 0)
    grads.forward(1)
    grads.forward(3)
    lines.finish()
    unfold_out_weight(plane, ow)
    grads.arrived(0)

    def pull(i, carry):
        @pl.when(i == 1)
        def _():
            grads.arrived(1)

        @pl.when(i == 2)
        def _():
            grads.arrived(3)
            grads.forward(2)

        @pl.when(i == 3)
        def _():
            grads.arrived(2)

        at = in_turn(i)
        dgated[chunk(at), :] = dot_nt(gall[at].reshape(256, D), ow[...])
        return carry

    lax.fori_loop(0, 4, pull, 0)
    acc = lax.fori_loop(
        0, GROUP, lambda b, acc: norm_sums(b, proj, par, heads_out, dgated, acc), jnp.zeros((SEQ, SEQ), F32)
    )
    sums[...] = acc.T[0:16, :]
    norms = Members(lambda q: sums, lambda q: slots.at[q], n_s, n_r)
    norms.start()
    slots[rank] = sums[...]
    small[...] = jnp.zeros_like(small)
    norms.finish()
    total = slots[0]
    for q in range(1, GROUP):
        total = total + slots[q]
    wide[...] = jnp.concatenate([total, jnp.zeros((SEQ - 16, SEQ), F32)], axis=0).T

    def norms_back(b, carry):
        norm_back(b, proj, par, wide, heads_out, dgated, gated, dproj, small)
        return carry

    lax.fori_loop(0, GROUP, norms_back, 0)

    hidden.sent()
    branch = hall
    branches = GroupReduce(branch, gb, mb, lb, fb, b_s, b_r)
    lowers = GroupReduce(d_low, gd, md, ld, fd, d_s, d_r)
    sums_x = PlaneReduce(dwx, gx, mx, lx, fx, rx_s, rx_r)
    sums_g = PlaneReduce(dwg, gg, mg, lg, fg, rg_s, rg_r)
    sums_l = PlaneReduce(dow, gl, ml, ll, fl, rl_s, rl_r)
    sums_s = PlaneReduce(dws, gs, ms, ls, fs, rs_s, rs_r, 1)
    cut_rows = Members(lambda q: cut.at[q], lambda q: rows_in.at[q], rr_s, rr_r)
    gate_rows = Members(lambda q: gcut.at[q], lambda q: grows_in.at[q], rq_s, rq_r)
    all_small = Members(lambda q: small_all.at[rank], lambda q: small_all.at[q], sg_s, sg_r)

    def small_z(k):
        return remote(small, zs.at[z], sz_s.at[k], sz_r.at[k], on_z(k))

    def small_x(k):
        return remote(part, xs.at[x], sx_s.at[k], sx_r.at[k], on_x(k))

    def slab(k, span):
        at = (z + k) % 4
        own = low[:, pl.ds(pl.multiple_of(at * GW, GW), GW)]
        return at, dot_tn(own, dproj[:, span]).astype(BF16).reshape(4, 2, 48, span.stop - span.start)

    def out_term(i, carry):
        at = (y + 3 - i) % 4
        branch[at] = dot(gated[chunk(at), :], ow[...]).astype(BF16).reshape(2, SEQ, D)
        branches.across((3 - i) % 4).start()
        return carry

    lax.fori_loop(0, 4, out_term, 0)
    for k in (2, 1, 3, 0):
        at, rows = slab(k, slice(GA, COLS))
        dwg[at] = rows
        if k:
            sums_g.first(1, k).start()
    for k in (2, 1, 3):
        sums_g.first(0, k).start()
    out = dot_tn(gated[...], gall[...].reshape(ROWS, D))
    for j in range(16):
        piece = out[j * KOUT : (j + 1) * KOUT]
        tail = jnp.concatenate([piece[16:24, 0 : D // 2], piece[16:24, D // 2 :]], axis=0)
        fold = jnp.concatenate([piece[0:16], tail], axis=1).astype(BF16)
        for h in range(2):
            dow[j % 8 // 2, j // 8 * 2 + j % 2, h] = fold[:, h * WIDE : (h + 1) * WIDE]
    sums_l.start()

    def other_copy(i):
        rows = chunk((y + i + 1) % 4)
        return remote(d_other.at[rows], d_in.at[rows], u_s.at[i], u_r.at[i], sibling())

    def backward(i, carry):
        @pl.when(i < 4)
        def _():
            at = (y + i + 1) % 4
            for core in range(2):
                mix_back(at * 2 + core, c, proj, act, par, head, skip, dgated, dproj, d_steps, small, d_mine, d_other)
            other_copy(i).start()

        @pl.when(i == 0)
        def _():
            for k in (3, 2, 1):
                branches.pass_on(k)
            branches.keep()

        @pl.when(i == 1)
        def _():
            sums_g.middle()

        @pl.when(i == 2)
        def _():
            sums_l.middle()

        @pl.when(jnp.logical_and(i > 0, i < 5))
        def _():
            other_copy(i - 1).wait_recv()
            at = (y + i) % 4
            for core in range(2):
                vector_back(at * 2 + core, proj, par, d_mine, d_in, dproj, small)
            rows = chunk(at)
            back = dot_nt(dproj[rows, 0:GA], wx[...].reshape(D, GA))
            back = back + dot_nt(dproj[rows, GA:COLS], wg[...].reshape(D, GW))
            back = back + dot(d_steps[rows, :], step_rows[...])
            d_low[at] = back.astype(BF16).reshape(2, SEQ, D)
            lowers.across(i % 4).start()

        @pl.when(jnp.logical_and(i > 1, i < 5))
        def _():
            lowers.pass_on(i - 1)

        return carry

    lax.fori_loop(0, 5, backward, 0)
    for k in (1, 2, 3):
        small_z(k).start()
    zs[z] = small[...]
    for k in (2, 1, 3, 0):
        at, rows = slab(k, slice(0, GA))
        dwx[at] = rows
        if k:
            sums_x.first(1, k).start()
    for k in (2, 1, 3):
        sums_x.first(0, k).start()
    steps_back = dot_tn(d_steps[...], low[...])
    for r in range(16):
        own = jnp.concatenate([steps_back[0:16, r * 96 : (r + 1) * 96], jnp.zeros((16, 32), F32)], axis=1)
        dws[r // 4, r % 4, 0] = own.astype(BF16)
    sums_s.start()
    for k in (1, 2, 3):
        small_z(k).wait_recv()
    part[...] = ((zs[0] + zs[1]) + zs[2]) + zs[3]
    xs[x] = part[...]
    for k in (1, 2, 3):
        small_x(k).start()
    sums_x.middle()
    sums_s.middle()
    lowers.keep()
    sums_g.end()
    for q in range(GROUP):
        gcut[q] = jnp.zeros((16, GW), BF16)
        gcut[q, 0:KIN, :] = fg[q // 4, q % 4 * KIN : (q % 4 + 1) * KIN, :].astype(BF16)
    gate_rows.start()
    grows_in[rank] = gcut[rank]
    sums_l.end()

    @pl.when(moves)
    def _():
        swap_back.start()

    for k in (1, 2, 3):
        small_x(k).wait_recv()
    small_all[rank] = ((xs[0] + xs[1]) + xs[2]) + xs[3]
    all_small.start()
    branches.end()
    h32 = hid[...].astype(F32)
    mixed[...] = (h32 + jnp.where(live, fb[...], 0.0)).astype(BF16)
    sums_s.end()
    sums_x.end()
    step_cols = dot_tn(fs[0, 0:8], ones(iota((8, 128), 0) == iota((8, 128), 1), F32), HIGHEST)
    for q in range(GROUP):
        at = q % 4 * KIN
        cut[q] = jnp.zeros((16, CW + 128), BF16)
        cut[q, 0:KIN, 0:CW] = fx[q // 4, at : at + KIN, :].astype(BF16)
        cut[q, 0:KIN, CW:] = step_cols[q * KIN : (q + 1) * KIN].astype(BF16)
    cut_rows.start()
    rows_in[rank] = cut[rank]
    all_small.finish()
    finish_small(small_all, dvecs)

    @pl.when(moves)
    def _():
        swap_back.wait_recv()

    @pl.when(jnp.logical_not(moves))
    def _():
        swapped[...] = fl[...]

    doutw[0:16, 0:WIDE] = swapped[0]
    doutw[0:16, WIDE:D] = swapped[1, :, 0 : D - WIDE]
    doutw[16:24, 0 : D // 2] = swapped[1, 0:8, D - WIDE :]
    doutw[16:24, D // 2 : D] = swapped[1, 8:16, D - WIDE :]
    lowers.end()
    scale = lax.rsqrt(jnp.mean(h32 * h32, axis=1, keepdims=True) + EPSILON)
    normed = h32 * scale
    d_normed = fd[...] * par[0:1, :]
    through = scale * (d_normed - normed * jnp.mean(d_normed * normed, axis=1, keepdims=True))
    in_grad[...] = (grd[...].astype(F32) + through).astype(BF16)
    gate_rows.finish()
    cut_rows.finish()
    finish_rows(rows_in, grows_in, inw, vectors, dinw, dvecs)
    for gone in (grads, first_w, gate_w, vecs, lines, cuts, norms, cut_rows, gate_rows, all_small):
        gone.sent()
    for gone in (branches, lowers, sums_x, sums_g, sums_l, sums_s):
        gone.finish()
    for k in (1, 2, 3):
        small_z(k).wait_send()
        small_x(k).wait_send()
    for i in range(4):
        vector_copy(i).wait_send()
        other_copy(i).wait_send()

    @pl.when(moves)
    def _():
        swap.wait_send()
        swap_back.wait_send()


def finish_small(small, dvecs):
    me = lax.axis_index("fsdp")
    conv = jnp.zeros((8, 128), F32)
    inner = jnp.zeros((8, 128), F32)
    common = [jnp.zeros((8, 128), F32), jnp.zeros((8, 128), F32)]
    row, col = iota((GW, 128), 0), iota((GW, 128), 1)
    heads = ones(row // 64 == col, F32)
    dvecs[...] = jnp.zeros_like(dvecs)
    for q in range(GROUP):
        part = small[q, :, 0:GW]
        conv = conv + dot(part, ones(row + q * GW == col + 26 * me, F32), HIGHEST)
        inner = inner + dot(part, ones(row + q * GW == col + KOUT * me, F32), HIGHEST)
        common[q % 2] = common[q % 2] + small[q, :, GW:CW]
        span = slice(q * OWN, (q + 1) * OWN)
        dvecs[3:4, span] = small[q, 7:8, 0:OWN]
        dvecs[4:5, span] = small[q, 7:8, 128 : 128 + OWN]
        dvecs[5:6, span] = dot(part, heads, HIGHEST)[6:7, 0:OWN]
    row, col = iota((256, 128), 0), iota((256, 128), 1)
    conv = conv + dot(jnp.concatenate(common, axis=1), ones(row + INNER == col + 26 * me, F32), HIGHEST)
    dvecs[1:2] = conv[4:5]
    dvecs[2:3] = inner[5:6]
    dvecs[8:12] = conv[0:4]


def finish_rows(rows, gate_rows, inw, vectors, dinw, dvecs):
    shared = [jnp.zeros((KIN, 128), F32), jnp.zeros((KIN, 128), F32)]
    for q in range(GROUP):
        own = rows[q].astype(F32)[0:KIN]
        dinw[:, INNER + q * GW : INNER + (q + 1) * GW] = own[:, 0:GW]
        dinw[:, q * GW : (q + 1) * GW] = gate_rows[q].astype(F32)[0:KIN]
        dinw[:, STEP + q * OWN : STEP + (q + 1) * OWN] = own[:, CW : CW + OWN]
        shared[q % 2] = shared[q % 2] + own[:, GW:CW]
    dinw[:, 2 * INNER : 2 * INNER + 128] = shared[0]
    dinw[:, 2 * INNER + 128 : STEP] = shared[1]
    total = jnp.sum(dinw[...] * inw[...].astype(F32), axis=1, keepdims=True)
    spread = jnp.where(iota((KIN, 128), 0) == iota((KIN, 128), 1), total, 0.0)
    gain = jnp.where(iota((1, 128), 1) < KIN, vectors[0:1], 1.0)
    dvecs[0:1] = jnp.sum(spread, axis=0, keepdims=True) / gain


def emit_kernel(mixed, in_grad, dinw, doutw, dvecs, *outs):
    (mixed_out, grad_out, dinw_out, dgain, conv_out, dbias, ddt, da_log, dskip, dinner, doutw_out) = outs
    for given, out in ((mixed, mixed_out), (in_grad, grad_out), (dinw, dinw_out), (doutw, doutw_out)):
        out[...] = given[...]
    for i, line in enumerate((dgain, dbias, dinner, ddt, da_log, dskip)):
        line[...] = dvecs[i, 0 : line.shape[0]]
    conv_out[...] = dvecs[8:12, 0:26]


def emit(*given):
    vmem = pl.BlockSpec(memory_space=pltpu.VMEM)
    shape = jax.ShapeDtypeStruct
    line = [shape((n,), F32) for n in (KIN, 26, HEADS, HEADS, HEADS, KOUT)]
    return pl.pallas_call(
        emit_kernel,
        name="emit",
        out_shape=(*OUT_SHAPES[0:3], line[0], shape((4, 26), F32), *line[1:], OUT_SHAPES[4]),
        in_specs=[vmem] * 5,
        out_specs=(vmem,) * 11,
        compiler_params=pltpu.CompilerParams(vmem_limit_bytes=VMEM_LIMIT),
    )(*given)


def layer(*given):
    vmem, vm = pl.BlockSpec(memory_space=pltpu.VMEM), pltpu.VMEM

    def dma(*dims):
        return pltpu.SemaphoreType.DMA(dims)

    def plane_reduce(halves, rows, cols):
        block = (rows, cols)
        return [
            vm((halves, 3, 4) + block, BF16), vm((halves, 3) + block, BF16), vm((halves, 3) + block, BF16),
            vm((halves,) + block, F32),
        ]

    seven, pair, four = [dma(GROUP)] * 2, [dma(2, 4)] * 2, [dma(4)] * 2
    group_reduce = [vm((4, SEQ, D), BF16), vm((3, SEQ, D), BF16), vm((3, SEQ, D), BF16), vm((SEQ, D), F32)]
    gather = [dma(2, 5, 4), dma(2, 4, 4)]
    return pl.pallas_call(
        layer_kernel,
        name="layer",
        out_shape=OUT_SHAPES,
        in_specs=[vmem] * len(given),
        out_specs=(vmem,) * len(OUT_SHAPES),
        scratch_shapes=[
            vm((8, 128), F32), vm((8, 128), F32), vm((8, 128), F32),
            vm((GROUP, 16, COLS), BF16), vm((GROUP, 16, COLS), BF16), vm((2, 48, GA), BF16), vm((2, 48, GW), BF16),
            vm((32, 384), BF16), vm((2, 16, WIDE), BF16), vm((2, 16, WIDE), BF16), vm((SEQ, D), BF16),
            vm((4, 4, 2, 48, GA), BF16), vm((4, 4, 2, 48, GW), BF16), vm((4, 4, 1, 32, 384), BF16),
            vm((4, 4, 2, 16, WIDE), BF16), vm((4, 2, SEQ, D), BF16), vm((4, 2, SEQ, D), BF16),
            vm((ROWS, D), BF16), vm((ROWS, COLS + 128), F32), vm((2, ROWS, 128), F32), vm((128, D), BF16),
            vm((ROWS, GW), F32), vm((ROWS, GW), F32), vm((GW, D), BF16),
            vm((8, D), F32), vm((8, 128), F32), vm((1, GW), F32),
            vm((16, SEQ), F32), vm((GROUP, 16, SEQ), F32), vm((SEQ, SEQ), F32),
            vm((ROWS, GW), BF16), vm((ROWS, COLS), BF16), vm((ROWS, 128), BF16),
            vm((ROWS, 128), F32), vm((ROWS, 128), F32), vm((ROWS, 128), F32), vm((4, 2, SEQ, D), BF16),
            vm((4, 4, 2, 48, GA), BF16), vm((4, 4, 2, 48, GW), BF16), vm((4, 4, 2, 16, WIDE), BF16),
            vm((4, 4, 1, 16, 128), BF16), vm((8, CW), F32),
            *group_reduce, *group_reduce, *plane_reduce(2, 48, GA), *plane_reduce(2, 48, GW),
            *plane_reduce(2, 16, WIDE), *plane_reduce(1, 16, 128),
            vm((2, 16, WIDE), F32), vm((GROUP, 16, CW + 128), BF16), vm((GROUP, 16, CW + 128), BF16),
            vm((GROUP, 16, GW), BF16), vm((GROUP, 16, GW), BF16),
            vm((4, 8, CW), F32), vm((4, 8, CW), F32), vm((8, CW), F32), vm((GROUP, 8, CW), F32),
            *seven, *gather, *gather, dma(1, 5, 4), dma(1, 4, 4), *gather,
            *pair, *pair, *seven, *four, *four,
            *pair, *pair, *[dma(2, 2, 4)] * 6, *[dma(1, 2, 4)] * 2, *seven, *seven,
            *four, *four, *seven, dma(2), dma(2),
        ],
        compiler_params=pltpu.CompilerParams(collective_id=0, has_side_effects=True, vmem_limit_bytes=VMEM_LIMIT),
    )(*given)


OUT_SHAPES = (
    jax.ShapeDtypeStruct((SEQ, D), BF16),
    jax.ShapeDtypeStruct((SEQ, D), BF16),
    jax.ShapeDtypeStruct((KIN, STEP + HEADS), F32),
    jax.ShapeDtypeStruct((16, 128), F32),
    jax.ShapeDtypeStruct((KOUT, D), F32),
)


def body(
    hidden, in_weight, norm_gain, conv_weight, conv_bias, dt_bias, a_log, skip, inner_gain, out_weight, out_grad,
    seq_lengths, seq_owner,
):
    mixed, in_grad, dinw, dvecs, doutw = layer(
        hidden, in_weight, norm_gain, conv_weight.T, conv_bias, dt_bias, a_log, skip, inner_gain, out_weight, out_grad,
        seq_lengths, seq_owner,
    )
    outs = list(emit(mixed, in_grad, dinw, doutw, dvecs))
    outs[4] = outs[4].T
    return tuple(outs)


def solution(mesh):
    rows, line, whole = P("fsdp", None), P("fsdp"), P()
    return jax.shard_map(
        body,
        mesh=mesh,
        in_specs=(rows, rows, line, rows, line, whole, whole, whole, line, rows, rows, whole, whole),
        out_specs=(rows, rows, rows, line, rows, line, whole, whole, whole, line, rows),
        check_vma=False,
    )
```

```python
import functools

import jax
import jax.numpy as jnp
from jax import lax
from jax.experimental import pallas as pl
from jax.experimental.pallas import tpu as pltpu
from jax.sharding import PartitionSpec as P

MESH = pl.DeviceIdType.MESH
F32, BF16 = jnp.float32, jnp.bfloat16
HIGHEST = lax.Precision.HIGHEST
EPSILON = 1e-05

D = 1536
INNER = 3072
CONVD = 3328
HEADS = 48
SEQ = 128
GROUP = 8
ROWS = SEQ * GROUP
GW = INNER // GROUP
OWN = HEADS // GROUP
CW = GW + 128
GA, COLS = CW, CW + GW
ST = COLS
KIN = D // 128
KOUT = INNER // 128
STEP = 2 * INNER + 256
FOLD = D + D // 2
WIDE = FOLD // 2
VMEM_LIMIT = 60 * 2**20


def iota(shape, dim):
    return lax.broadcasted_iota(jnp.int32, shape, dim)


def ones(condition, kind=BF16):
    return jnp.where(condition, 1.0, 0.0).astype(kind)


def dot(a, b, precision=None):
    return lax.dot_general(a, b, (((1,), (0,)), ((), ())), precision=precision, preferred_element_type=F32)


def dot_nt(a, b, precision=None):
    return lax.dot_general(a, b, (((1,), (1,)), ((), ())), precision=precision, preferred_element_type=F32)


def dot_tn(a, b, precision=None):
    return lax.dot_general(a, b, (((0,), (0,)), ((), ())), precision=precision, preferred_element_type=F32)


def sigmoid(v):
    return 1.0 / (1.0 + jnp.exp(-v))


def softplus(v):
    return jnp.maximum(v, 0.0) + jnp.log1p(jnp.exp(-jnp.abs(v)))


def later(v, k):
    if k == 0:
        return v
    return jnp.where(iota(v.shape, 0) >= k, pltpu.roll(v, k, 0), 0.0)


def earlier(v, k):
    if k == 0:
        return v
    return jnp.where(iota(v.shape, 0) < v.shape[0] - k, pltpu.roll(v, v.shape[0] - k, 0), 0.0)


def place():
    me = lax.axis_index("fsdp")
    return me // 32, (me // 8) % 4, (me // 2) % 4, me % 2


def index(z, x, y, c):
    return ((z * 4 + x) * 4 + y) * 2 + c


def group_partner(k):
    z, x, y, c = place()
    rank = (y * 2 + c + k) % GROUP
    return index(z, x, rank // 2, rank % 2), rank


def on_z(k):
    z, x, y, c = place()
    return index((z + k) % 4, x, y, c)


def on_x(k):
    z, x, y, c = place()
    return index(z, (x + k) % 4, y, c)


def on_y(k):
    z, x, y, c = place()
    return index(z, x, (y + k) % 4, c)


def sibling():
    z, x, y, c = place()
    return index(z, x, y, 1 - c)


def swap_to():
    z, x, y, c = place()
    return index(y, x % 2 * 2 + c, z, x // 2)


def swap_from():
    z, x, y, c = place()
    return index(y, c * 2 + x // 2, z, x % 2)


def signal(target):
    pl.semaphore_signal(pltpu.get_barrier_semaphore(), inc=1, device_id=(target,), device_id_type=MESH)


def remote(src, dst, send, recv, target):
    return pltpu.make_async_remote_copy(
        src_ref=src, dst_ref=dst, send_sem=send, recv_sem=recv, device_id=(target,), device_id_type=MESH
    )


def plane_partners():
    return [on_z(k) for k in (1, 2, 3)] + [on_x(k) for k in (1, 2, 3)]


def group_partners():
    return [group_partner(k)[0] for k in range(1, GROUP)]


class PlaneGather:
    def __init__(self, buf, own, send, recv, halves):
        self.buf, self.own, self.send, self.recv, self.halves = buf, own, send, recv, halves
        self.z, self.x, _, _ = place()

    def slot(self, half, first, second):
        a, b = (first, second) if half == 0 else (second, first)
        return self.buf.at[(self.z + a) % 4, (self.x + b) % 4, half]

    def along(self, half, stage, k):
        return on_z(k) if (half == 0) == (stage == 0) else on_x(k)

    def came(self, first):
        return 3 if first < 2 else 1

    def mark(self, half, first, second):
        if second == 0:
            return self.recv.at[half, first - 1]
        return self.recv.at[half, 3 + first if second == self.came(first) else 7]

    def copy(self, half, first, stage, k):
        src = self.own(half) if first == 0 else self.slot(half, first, 0)
        at = (4 - k, 0) if stage == 0 else (first, 4 - k)
        return remote(
            src, self.slot(half, first, 0), self.send.at[half, stage], self.mark(half, *at), self.along(half, stage, k)
        )

    def relayed(self, half, first):
        came = self.came(first)
        here = self.slot(half, first, came)
        return remote(here, here, self.send.at[half, 1], self.mark(half, first, 2), self.along(half, 1, 4 - came))

    def arrival(self, half, first, second):
        here = self.slot(half, first, second)
        return remote(here, here, self.send.at[half, 0], self.mark(half, first, second), on_z(1))

    def some(self, rows, count, half):
        return self.buf.at[pl.ds(0, rows), pl.ds(0, count), half]

    def start(self):
        for k in (1, 3, 2):
            for half in range(self.halves):
                self.copy(half, 0, 0, k).start()
        for k in (1, 3):
            for half in range(self.halves):
                self.copy(half, 0, 1, k).start()

    def forward(self):
        for first in (1, 3, 2):
            for half in range(self.halves):
                self.arrival(half, first, 0).wait_recv()
                for k in (1, 3):
                    self.copy(half, first, 1, k).start()

    def relay(self):
        for first in (0, 3, 1, 2):
            for half in range(self.halves):
                self.arrival(half, first, self.came(first)).wait_recv()
                self.relayed(half, first).start()

    def finish(self):
        for half in range(self.halves):
            here = self.some(4, 2, half)
            remote(here, here, self.send.at[half, 0], self.recv.at[half, 7], on_z(1)).wait_recv()

    def sent(self):
        for half in range(self.halves):
            for stage, here in ((0, self.some(1, 3, half)), (1, self.some(4, 3, half))):
                remote(here, here, self.send.at[half, stage], self.recv.at[half, 7], on_z(1)).wait_send()


class GroupGather:
    def __init__(self, buf, own, send, recv):
        self.buf, self.own, self.send, self.recv = buf, own, send, recv
        _, _, self.y, self.c = place()

    def along(self, k):
        return remote(self.own, self.buf.at[self.y, self.c], self.send.at[0], self.recv.at[4 - k], on_y(k))

    def half(self, k):
        return pl.ds(0, SEQ // 2) if k == 3 else pl.ds(SEQ // 2, SEQ // 2)

    def relayed(self, k):
        here = self.buf.at[(self.y + k) % 4, self.c, self.half(k)]
        return remote(here, here, self.send.at[0], self.recv.at[2], on_y(4 - k))

    def across(self, k):
        src = self.own if k == 0 else self.buf.at[(self.y + k) % 4, self.c]
        dst = self.buf.at[(self.y + k) % 4, self.c]
        return remote(src, dst, self.send.at[1], self.recv.at[4 + k], sibling())

    def start(self):
        for k in (1, 3):
            self.along(k).start()
        self.across(0).start()

    def forward(self, k):
        here = self.buf.at[(self.y + k) % 4, self.c]
        remote(here, here, self.send.at[0], self.recv.at[k], sibling()).wait_recv()
        if k != 2:
            self.relayed(k).start()
        self.across(k).start()

    def arrived(self, k):
        here = self.buf.at[(self.y + k) % 4, 1 - self.c]
        remote(here, here, self.send.at[0], self.recv.at[4 + k], sibling()).wait_recv()

    def sent(self):
        for at, here in ((0, self.buf.at[pl.ds(0, 3), 0]), (1, self.buf.at[:, 0])):
            remote(here, here, self.send.at[at], self.recv.at[0], sibling()).wait_send()


def unpack_params(raw, rank, core, par, step_rows):
    row = iota((512, 1), 0)
    device = (row // 4).astype(F32)
    tap = row % 4
    values = raw[...].reshape(512, 384)

    def spots(span, first, count, channel):
        owner = jnp.floor((channel + 0.5) * (1.0 / count))
        lane = channel - owner * count + first
        pick = ones(iota((128, channel.shape[1]), 0).astype(F32) == lane)
        return jnp.where(device == owner, dot(values[:, span], pick), 0.0)

    def only(k, at):
        return jnp.sum(jnp.where(tap == k, at, 0.0), axis=0, keepdims=True)

    def lanes(n):
        return iota((1, n), 1).astype(F32)

    start = rank.astype(F32) * GW
    conv = lanes(CW)
    conv = jnp.where(conv < GW, conv + start, conv - GW + INNER + 128 * core.astype(F32))
    low, high, last = slice(0, 128), slice(128, 256), slice(256, 384)
    par[...] = jnp.zeros_like(par)
    par[0:1, :] = only(0, spots(high, 0, KIN, lanes(D)))
    taps = spots(low, 0, 26, conv)
    for k in range(4):
        par[k + 1 : k + 2, 0:CW] = only(k, taps)
    par[5:6, 0:CW] = only(0, spots(high, KIN, 26, conv))
    par[6:7, 0:GW] = only(0, spots(high, KIN + 26, KOUT, lanes(GW) + start))
    four, two = spots(last, 0, KIN, lanes(D)), spots(last, 16, KIN, lanes(D))
    rows = [only(k, four) for k in range(4)] + [only(k, two) for k in range(2)] + [jnp.zeros((122, D), F32)]
    step_rows[...] = jnp.concatenate(rows, axis=0).astype(BF16)


def own_heads(raw, rank, head, skip):
    row = iota((128, 128), 0)
    col = iota((128, 128), 1)
    given = raw[...]
    mine = dot(given, ones(jnp.logical_and(row == col + OWN * rank, col < OWN), F32), HIGHEST)
    head[...] = jnp.where(iota((8, 128), 0) == 1, -jnp.exp(mine), mine)
    wide = iota((128, GW), 0) == iota((128, GW), 1) // 64 + OWN * rank
    skip[...] = dot(given, ones(wide, F32), HIGHEST)[2:3]


def unfold_out_weight(raw, ow):
    row, col = iota((GW, 256), 0), iota((GW, 256), 1)
    device, line = row // KOUT, row % KOUT
    base = (device % 8 // 2 * 4 + device // 8 * 2 + device % 2) * 16
    top = ones(jnp.logical_and(line < 16, col == base + line))
    low_left = ones(jnp.logical_and(line >= 16, col == base + line - 16))
    low_right = ones(jnp.logical_and(line >= 16, col == base + line - 8))
    first = raw[:, :, 0].reshape(256, WIDE)
    second = raw[:, :, 1].reshape(256, WIDE)
    half, split = D // 2, WIDE - D // 2
    left, right_a = first[:, 0:half], first[:, half:]
    right_b, tail = second[:, 0 : half - split], second[:, half - split :]
    ow[:, 0:half] = (dot(top, left) + dot(low_left, tail)).astype(BF16)
    ow[:, half : half + split] = (dot(top, right_a) + dot(low_right, tail[:, 0:split])).astype(BF16)
    ow[:, half + split :] = (dot(top, right_b) + dot(low_right, tail[:, split:])).astype(BF16)


def convolve(raw, par, at, width):
    out = par[5:6, at : at + width] + raw * par[4:5, at : at + width]
    for k in range(3):
        out = out + later(raw, 3 - k) * par[k + 1 : k + 2, at : at + width]
    return out


def steps_of(raw, head):
    step = softplus(raw + head[0:1, :])
    decay = head[1:2, :] * step
    lower = ones(iota((SEQ, SEQ), 0) >= iota((SEQ, SEQ), 1), F32)
    total = dot(lower, decay, HIGHEST)
    return step, decay, total


def mix_forward(b, proj, act, par, head, skip, heads_out):
    row, col = iota((SEQ, SEQ), 0), iota((SEQ, SEQ), 1)
    causal = row >= col
    rows = pl.ds(pl.multiple_of(b * SEQ, SEQ), SEQ)
    write, read = act[0, rows, :], act[1, rows, :]
    step, _, total = steps_of(proj[rows, ST:], head)
    total_t, step_t = total.T, step.T
    scores = dot_nt(read, write, HIGHEST)
    for p in range(3):
        at = p * 128
        values = convolve(proj[rows, at : at + 128], par, at, 128)
        values = values * sigmoid(values)
        values_low = values.astype(BF16)
        parts = []
        for h in (2 * p, 2 * p + 1):
            decays = jnp.exp(jnp.where(causal, total[:, h : h + 1] - total_t[h : h + 1, :], -1e30))
            mix = (decays * scores * step_t[h : h + 1, :]).astype(BF16)
            parts.append(dot(mix, values_low))
        heads_out[rows, at : at + 128] = jnp.where(col < 64, parts[0], parts[1]) + skip[0:1, at : at + 128] * values


def weigh(b, proj, par, heads_out, gated):
    rows = pl.ds(pl.multiple_of(b * SEQ, SEQ), SEQ)
    gate = proj[rows, GA:COLS]
    gated[rows, :] = (heads_out[rows, :] * gate * sigmoid(gate) * par[6:7, 0:GW]).astype(BF16)


def column(at, values):
    return jnp.sum(jnp.where(iota((SEQ, SEQ), 1) == at, values, 0.0), axis=1, keepdims=True)


def norm_sums(b, proj, par, heads_out, dgated, acc):
    rows = pl.ds(pl.multiple_of(b * SEQ, SEQ), SEQ)
    gate = proj[rows, GA:COLS]
    product = heads_out[rows, :] * gate * sigmoid(gate)
    squares = jnp.sum(product * product, axis=1, keepdims=True)
    crosses = jnp.sum(product * dgated[rows, :] * par[6:7, 0:GW], axis=1, keepdims=True)
    col = iota((SEQ, SEQ), 1)
    return jnp.where(col == b, squares, jnp.where(col == b + 8, crosses, acc))


def norm_back(b, proj, par, wide, heads_out, dgated, gated, dproj, small):
    rows = pl.ds(pl.multiple_of(b * SEQ, SEQ), SEQ)
    cross = column(b + 8, wide[...])
    inverse = lax.rsqrt(column(b, wide[...]) * (1.0 / INNER) + EPSILON)
    mean = cross * inverse * (1.0 / INNER)
    out = heads_out[rows, :]
    gate = proj[rows, GA:COLS]
    s = sigmoid(gate)
    silu = gate * s
    unit = out * silu * inverse
    dg = dgated[rows, :]
    gain = par[6:7, 0:GW]
    gated[rows, :] = (unit * gain).astype(BF16)
    small[5:6, 0:GW] += jnp.sum(dg * unit, axis=0, keepdims=True)
    d_product = (dg * gain - unit * mean) * inverse
    dproj[rows, GA:COLS] = (d_product * out * (s * (1.0 + gate * (1.0 - s)))).astype(BF16)
    dgated[rows, :] = d_product * silu


def conv_back(d_act, raw, v, s, par, small, at):
    d_conv = d_act * s * (1.0 + v * (1.0 - s))
    span = slice(at, at + 128)
    back = d_conv * par[4:5, span]
    small[3:4, span] += jnp.sum(d_conv * raw, axis=0, keepdims=True)
    for k in range(3):
        back = back + earlier(d_conv, 3 - k) * par[k + 1 : k + 2, span]
        small[k : k + 1, span] += jnp.sum(d_conv * later(raw, 3 - k), axis=0, keepdims=True)
    small[4:5, span] += jnp.sum(d_conv, axis=0, keepdims=True)
    return back


def mix_back(b, core, proj, act, par, head, skip, d_heads, dproj, d_steps, small, d_mine, d_other):
    row, col = iota((SEQ, SEQ), 0), iota((SEQ, SEQ), 1)
    later_ok = col >= row
    left, right = col < 64, col >= 64
    suffix = ones(row >= col)
    before = row < col
    rows = pl.ds(pl.multiple_of(b * SEQ, SEQ), SEQ)

    write, read = act[0, rows, :], act[1, rows, :]
    raw_step = proj[rows, ST:]
    step, decay, total = steps_of(raw_step, head)
    total_t = total.T
    scores_t = dot_nt(write, read, HIGHEST)
    d_scores = jnp.zeros((SEQ, SEQ), F32)
    direct = jnp.zeros((SEQ, SEQ), F32)
    lines = []
    for p in range(3):
        at = p * 128
        span = slice(at, at + 128)
        d_out = d_heads[rows, span]
        raw = proj[rows, span]
        pre = convolve(raw, par, at, 128)
        sig = sigmoid(pre)
        values = pre * sig
        small[6:7, span] += jnp.sum(d_out * values, axis=0, keepdims=True)
        values_low = values.astype(BF16)
        d_low = d_out.astype(BF16)
        parts = []
        for i, h in enumerate((2 * p, 2 * p + 1)):
            decays = jnp.exp(jnp.where(later_ok, total_t[h : h + 1, :] - total[:, h : h + 1], -1e30))
            size = step[:, h : h + 1]
            own = jnp.where(left if i == 0 else right, d_out, 0.0).astype(BF16)
            d_mix = decays * dot_nt(values_low, own)
            d_scores = d_scores + d_mix * size
            per_step = (d_mix * scores_t).astype(BF16)
            tail = dot(per_step, suffix)
            direct = jnp.where(col == h, tail[:, 0:1], direct)
            lines.append(jnp.sum(jnp.where(before, tail * size, 0.0), axis=0, keepdims=True))
            mix = (decays * scores_t * size).astype(BF16)
            parts.append(dot(mix, d_low))
        d_values = jnp.where(left, parts[0], parts[1]) + skip[0:1, span] * d_out
        dproj[rows, span] = conv_back(d_values, raw, pre, sig, par, small, at).astype(BF16)
    d_decay = jnp.concatenate(lines + [jnp.zeros((SEQ - OWN, SEQ), F32)], axis=0).T
    d_step = direct + head[1:2, :] * d_decay
    d_raw = d_step * sigmoid(raw_step + head[0:1, :])
    small[7:8, 0:128] += jnp.sum(d_raw, axis=0, keepdims=True)
    small[7:8, 128:256] += jnp.sum(d_decay * decay, axis=0, keepdims=True)
    d_low = d_scores.astype(BF16)
    d_write = dot(d_low, read.astype(BF16))
    d_read = dot_tn(d_low, write.astype(BF16))
    d_mine[rows, :] = jnp.where(core == 0, d_write, d_read)
    d_other[rows, :] = jnp.where(core == 0, d_read, d_write)
    d_steps[rows, :] = d_raw.astype(BF16)


def vector_forward(b, core, proj, act, par):
    rows = pl.ds(pl.multiple_of(b * SEQ, SEQ), SEQ)
    v = convolve(proj[rows, GW:CW], par, GW, 128)
    act[core, rows, :] = v * sigmoid(v)


def vector_back(b, proj, par, d_mine, d_in, dproj, small):
    rows = pl.ds(pl.multiple_of(b * SEQ, SEQ), SEQ)
    raw = proj[rows, GW:CW]
    v = convolve(raw, par, GW, 128)
    d = d_mine[rows, :] + d_in[rows, :]
    dproj[rows, GW:CW] = conv_back(d, raw, v, sigmoid(v), par, small, GW).astype(BF16)


class PlaneReduce:
    def __init__(self, terms, got, mid, last, out, send, recv, halves=2):
        self.terms, self.got, self.mid, self.last, self.out = terms, got, mid, last, out
        self.send, self.recv, self.halves = send, recv, halves
        self.z, self.x, _, _ = place()

    def line(self, half, k):
        return self.terms.at[:, (self.x + k) % 4, 0] if half == 0 else self.terms.at[(self.z + k) % 4, :, 1]

    def first(self, half, k):
        target = on_x(k) if half == 0 else on_z(k)
        return remote(self.line(half, k), self.got.at[half, k - 1], self.send.at[half, 0], self.recv.at[half, 0], target)

    def second(self, half, k):
        target = on_z(k) if half == 0 else on_x(k)
        return remote(self.mid.at[half, k - 1], self.last.at[half, k - 1], self.send.at[half, 1], self.recv.at[half, 1], target)

    def stage(self, half, at, like):
        return remote(like.at[half], like.at[half], self.send.at[half, at], self.recv.at[half, at], on_z(1))

    def start(self):
        for k in (2, 1, 3):
            for half in reversed(range(self.halves)):
                self.first(half, k).start()

    def middle(self):
        for half in reversed(range(self.halves)):
            self.stage(half, 0, self.got).wait_recv()
            for k in (2, 1, 3, 0):
                if half == 0:
                    at = (self.z + k) % 4
                    total = self.terms[at, self.x, 0].astype(F32)
                else:
                    at = (self.x + k) % 4
                    total = self.terms[self.z, at, 1].astype(F32)
                for j in range(3):
                    total = total + self.got[half, j, at].astype(F32)
                if k:
                    self.mid[half, k - 1] = total.astype(BF16)
                    self.second(half, k).start()
                else:
                    self.out[half] = total

    def end(self):
        for half in reversed(range(self.halves)):
            self.stage(half, 1, self.last).wait_recv()
            total = self.out[half]
            for j in range(3):
                total = total + self.last[half, j].astype(F32)
            self.out[half] = total

    def finish(self):
        for half in reversed(range(self.halves)):
            self.stage(half, 0, self.got).wait_send()
            self.stage(half, 1, self.mid).wait_send()


class GroupReduce:
    def __init__(self, terms, got, mid, relay, last, out, send, recv):
        self.terms, self.got, self.mid, self.relay, self.last, self.out = terms, got, mid, relay, last, out
        self.send, self.recv = send, recv
        _, _, self.y, self.c = place()

    def across(self, k):
        src = self.terms.at[(self.y + k) % 4, 1 - self.c]
        return remote(src, self.got.at[k], self.send.at[0], self.recv.at[k], sibling())

    def along(self, k):
        at = (k - 1) // 2
        return remote(self.mid.at[k - 1], self.last.at[at], self.send.at[1], self.recv.at[6], on_y(k))

    def far(self, at):
        src = self.mid.at[1, pl.ds(at * (SEQ // 2), SEQ // 2)]
        return remote(src, self.relay.at[at], self.send.at[1], self.recv.at[4 + at], on_y(3 if at else 1))

    def half(self, k):
        self.across(k).wait_recv()
        return self.terms[(self.y + k) % 4, self.c].astype(F32) + self.got[k].astype(F32)

    def pass_far(self):
        self.mid[1] = self.half(2).astype(BF16)
        for at in range(2):
            self.far(at).start()

    def pass_on(self, k):
        at = (k - 1) // 2
        total = self.half(k)
        self.far(at).wait_recv()
        came = self.relay[at].astype(F32)
        upper, lower = total[0 : SEQ // 2], total[SEQ // 2 :]
        if at == 0:
            upper = upper + came
        else:
            lower = lower + came
        self.mid[k - 1, 0 : SEQ // 2] = upper.astype(BF16)
        self.mid[k - 1, SEQ // 2 :] = lower.astype(BF16)
        self.along(k).start()

    def keep(self):
        self.out[...] = self.half(0)

    def end(self):
        total = self.out[...]
        remote(self.last, self.last, self.send.at[1], self.recv.at[6], sibling()).wait_recv()
        self.out[...] = total + self.last[0].astype(F32) + self.last[1].astype(F32)

    def finish(self):
        for at, here in ((0, self.got), (1, self.mid)):
            remote(here, here, self.send.at[at], self.recv.at[6], sibling()).wait_send()


class Members:
    def __init__(self, src, buf, send, recv):
        self.src, self.buf, self.send, self.recv = src, buf, send.at[0], recv.at[0]
        _, _, y, c = place()
        self.rank = y * 2 + c

    def start(self):
        for k in range(1, GROUP):
            target, q = group_partner(k)
            remote(self.src(q), self.buf.at[self.rank], self.send, self.recv, target).start()

    def others(self):
        here = self.buf.at[pl.ds(0, GROUP - 1)]
        return remote(here, here, self.send, self.recv, sibling())

    def finish(self):
        self.others().wait_recv()

    def sent(self):
        self.others().wait_send()


def layer_kernel(
    hid, inw, gain_in, taps, bias_in, dt_in, a_in, skip_in, inner_in, outw, grd, lengths, owners,
    mixed, in_grad, dinw, dvecs, doutw,
    vectors, heads_in, tap_rows,
    split, joined, block, gblock, params, outl, placed, live_grd,
    wx, wg, praw, plane, hall, gall, low, proj, act, step_rows, heads_out, dgated, ow, par, head, skip, sums, slots, wide,
    gated, dproj, d_steps, d_mine, d_other, d_in, d_low, dwx, dwg, dow, dws, small,
    gb, mb, tb, lb, fb, gd, md, td, ld, fd, gx, mx, lx, fx, gg, mg, lg, fg, gl, ml, ll, fl, gs, ms, ls, fs,
    swapped, cut, rows_in, gcut, grows_in, zs, xs, part, small_all,
    a_s, a_r, wx_s, wx_r, wg_s, wg_r, p_s, p_r, l_s, l_r, h_s, h_r, g_s, g_r, n_s, n_r, v_s, v_r, u_s, u_r,
    b_s, b_r, d_s, d_r, rx_s, rx_r, rg_s, rg_r, rl_s, rl_r, rs_s, rs_r, rr_s, rr_r, rq_s, rq_r,
    sz_s, sz_r, sx_s, sx_r, sg_s, sg_r, swap_s, swap_r,
):
    z, x, y, c = place()
    rank = y * 2 + c
    me = lax.axis_index("fsdp")
    partners = plane_partners() + group_partners()
    moves = swap_to() != me
    for p in partners:
        signal(p)

    @pl.when(moves)
    def _():
        signal(swap_to())
        signal(swap_from())

    vectors[...] = jnp.zeros_like(vectors)
    heads_in[...] = jnp.zeros_like(heads_in)
    tap_rows[...] = jnp.zeros_like(tap_rows)
    vectors[0:1, 0:KIN] = gain_in[...].astype(F32)[None, :]
    vectors[0:1, KIN : KIN + 26] = bias_in[...].astype(F32)[None, :]
    vectors[0:1, KIN + 26 : KIN + 26 + KOUT] = inner_in[...].astype(F32)[None, :]
    for i, line in enumerate((dt_in, a_in, skip_in)):
        heads_in[i : i + 1, 0:HEADS] = line[...][None, :]
    tap_rows[0:4, 0:26] = taps[...].astype(F32)
    col_steps = inw[:, STEP : STEP + HEADS]
    steps_low = dot_tn(col_steps, ones(iota((KIN, 128), 0) == iota((KIN, 128), 1)))
    steps_high = dot_tn(col_steps, ones(iota((KIN, 128), 0) + 16 == iota((KIN, 128), 1)))
    rest = jnp.zeros((4, 128), F32)

    def padded(span, extra):
        return jnp.concatenate([inw[:, span].astype(F32), extra], axis=0).astype(BF16)

    vector_cols = [padded(slice(2 * INNER + 128 * i, 2 * INNER + 128 * (i + 1)), rest) for i in range(2)]
    for q in range(GROUP):
        at = q * OWN
        two = jnp.concatenate([steps_high[at + 4 : at + OWN], jnp.zeros((2, 128), F32)], axis=0)
        extra = jnp.concatenate([tap_rows[0:4], vectors[0:4], steps_low[at : at + 4] + two], axis=1)
        split[q, :, 0:GW] = padded(slice(INNER + q * GW, INNER + (q + 1) * GW), extra)
        split[q, :, GW:CW] = vector_cols[q % 2]
        split[q, :, GA:COLS] = padded(slice(q * GW, (q + 1) * GW), jnp.zeros((4, GW), F32))
    end = outw[16:24, :].astype(F32)
    tail = jnp.concatenate([end[:, 0 : D // 2], end[:, D // 2 :]], axis=0).astype(BF16)
    outl[0] = outw[0:16, 0:WIDE]
    outl[1, :, 0 : D - WIDE] = outw[0:16, WIDE:D]
    outl[1, :, D - WIDE :] = tail

    @pl.when(moves)
    def _():
        pl.semaphore_wait(pltpu.get_barrier_semaphore(), len(partners) + 2)

    @pl.when(jnp.logical_not(moves))
    def _():
        pl.semaphore_wait(pltpu.get_barrier_semaphore(), len(partners))

    cuts = Members(lambda q: split.at[q], joined, a_s, a_r)
    cuts.start()
    swap = remote(outl, placed, swap_s.at[0], swap_r.at[0], swap_to())
    swap_back = remote(fl, swapped, swap_s.at[1], swap_r.at[1], swap_from())

    @pl.when(moves)
    def _():
        swap.start()

    joined[rank] = split[rank]
    length = jnp.sum(jnp.where(owners[...][None, :] == me, lengths[...][None, :], 0), axis=1, keepdims=True)
    live = iota((SEQ, 1), 0) < length
    live_grd[...] = jnp.where(live, grd[...].astype(F32), 0.0).astype(BF16)
    own_heads(heads_in, rank, head, skip)

    hidden = GroupGather(hall, hid, h_s, h_r)
    grads = GroupGather(gall, live_grd, g_s, g_r)
    first_w = PlaneGather(wx, lambda h: block.at[h], wx_s, wx_r, 2)
    gate_w = PlaneGather(wg, lambda h: gblock.at[h], wg_s, wg_r, 2)
    vecs = PlaneGather(praw, lambda h: params, p_s, p_r, 1)
    lines = PlaneGather(plane, lambda h: placed.at[h], l_s, l_r, 2)

    hidden.start()
    cuts.finish()
    row, col = iota((128, 128), 0), iota((128, 128), 1)
    member, line = col // 16, col % 16
    spot = jnp.where(line < KIN, member * KIN + line, 96 + member * 4 + line - KIN)
    both = dot(ones(spot == row), joined[...].reshape(128, COLS)).astype(BF16)
    for h in range(2):
        block[h] = both[48 * h : 48 * h + 48, 0:GA]
        gblock[h] = both[48 * h : 48 * h + 48, GA:COLS]
    params[...] = both[96:128, 0:384]
    vecs.start()
    first_w.start()
    wx[z, x] = block[...]
    wg[z, x] = gblock[...]
    praw[z, x, 0] = params[...]
    hall[y, c] = hid[...]
    gall[y, c] = live_grd[...]
    vecs.forward()
    first_w.forward()
    gate_w.start()

    @pl.when(moves)
    def _():
        swap.wait_recv()

    @pl.when(jnp.logical_not(moves))
    def _():
        placed[...] = outl[...]

    lines.start()
    plane[z, x] = placed[...]
    hidden.forward(1)
    hidden.forward(3)
    grads.start()
    vecs.relay()
    first_w.relay()
    vecs.finish()
    unpack_params(praw, rank, c, par, step_rows)
    gate_w.forward()
    lines.forward()
    first_w.finish()

    def chunk(i):
        return pl.ds(pl.multiple_of(i * 256, 256), 256)

    def turn(i):
        return i + i // 2 * (5 - 2 * i)

    def in_turn(i):
        return (y + turn(i)) % 4

    def vector_copy(i):
        here = act.at[c, chunk(in_turn(i))]
        return remote(here, here, v_s.at[0], v_r.at[i], sibling())

    def vector_arrival(i):
        here = act.at[1 - c, chunk(in_turn(i))]
        return remote(here, here, v_s.at[0], v_r.at[i], sibling())

    def forward(i, carry):
        @pl.when(i == 0)
        def _():
            hidden.arrived(0)

        @pl.when(i == 1)
        def _():
            hidden.arrived(1)
            hidden.forward(2)

        @pl.when(i == 2)
        def _():
            hidden.arrived(3)
            gate_w.relay()

        @pl.when(i == 3)
        def _():
            hidden.arrived(2)
            lines.relay()

        @pl.when(i == 4)
        def _():
            grads.forward(1)
            grads.forward(3)

        @pl.when(i < 4)
        def _():
            at = in_turn(i)
            for core in range(2):
                h = hall[at, core].astype(F32)
                scale = lax.rsqrt(jnp.mean(h * h, axis=1, keepdims=True) + EPSILON)
                rows = pl.ds(pl.multiple_of(at * 256 + core * SEQ, SEQ), SEQ)
                low[rows, :] = (h * scale * par[0:1, :]).astype(BF16)
            rows = chunk(at)
            proj[rows, 0:GA] = dot(low[rows, :], wx[...].reshape(D, GA))
            proj[rows, ST:] = dot_nt(low[rows, :], step_rows[...])
            for core in range(2):
                vector_forward(at * 2 + core, c, proj, act, par)
            vector_copy(i).start()

        @pl.when(i > 0)
        def _():
            vector_arrival(i - 1).wait_recv()
            at = in_turn(i - 1)
            for core in range(2):
                mix_forward(at * 2 + core, proj, act, par, head, skip, heads_out)

        return carry

    lax.fori_loop(0, 5, forward, 0)
    gate_w.finish()

    def project_gate(i, carry):
        proj[chunk(i), GA:COLS] = dot(low[chunk(i), :], wg[...].reshape(D, GW))
        return carry

    lax.fori_loop(0, ROWS // 256, project_gate, 0)

    def weighed(b, carry):
        weigh(b, proj, par, heads_out, gated)
        return carry

    lax.fori_loop(0, GROUP, weighed, 0)
    lines.finish()
    unfold_out_weight(plane, ow)
    hidden.sent()
    branch = hall
    branches = GroupReduce(branch, gb, mb, tb, lb, fb, b_s, b_r)

    def out_term(i, carry):
        at = in_turn(3 - i)
        branch[at] = dot(gated[chunk(at), :], ow[...]).astype(BF16).reshape(2, SEQ, D)
        branches.across(turn(3 - i)).start()
        return carry

    lax.fori_loop(0, 4, out_term, 0)
    grads.forward(2)
    grads.arrived(0)

    def pull(i, carry):
        @pl.when(i == 1)
        def _():
            grads.arrived(1)

        @pl.when(i == 2)
        def _():
            grads.arrived(3)

        @pl.when(i == 3)
        def _():
            grads.arrived(2)

        at = in_turn(i)
        dgated[chunk(at), :] = dot_nt(gall[at].reshape(256, D), ow[...])
        return carry

    lax.fori_loop(0, 4, pull, 0)
    acc = lax.fori_loop(
        0, GROUP, lambda b, acc: norm_sums(b, proj, par, heads_out, dgated, acc), jnp.zeros((SEQ, SEQ), F32)
    )
    sums[...] = acc.T[0:16, :]
    norms = Members(lambda q: sums, slots, n_s, n_r)
    norms.start()
    slots[rank] = sums[...]
    small[...] = jnp.zeros_like(small)
    branches.pass_far()
    norms.finish()
    total = slots[0]
    for q in range(1, GROUP):
        total = total + slots[q]
    wide[...] = jnp.concatenate([total, jnp.zeros((SEQ - 16, SEQ), F32)], axis=0).T

    def norms_back(b, carry):
        norm_back(b, proj, par, wide, heads_out, dgated, gated, dproj, small)
        return carry

    lax.fori_loop(0, GROUP, norms_back, 0)

    lowers = GroupReduce(d_low, gd, md, td, ld, fd, d_s, d_r)
    sums_x = PlaneReduce(dwx, gx, mx, lx, fx, rx_s, rx_r)
    sums_g = PlaneReduce(dwg, gg, mg, lg, fg, rg_s, rg_r)
    sums_l = PlaneReduce(dow, gl, ml, ll, fl, rl_s, rl_r)
    sums_s = PlaneReduce(dws, gs, ms, ls, fs, rs_s, rs_r, 1)
    cut_rows = Members(lambda q: cut.at[q], rows_in, rr_s, rr_r)
    gate_rows = Members(lambda q: gcut.at[q], grows_in, rq_s, rq_r)
    all_small = Members(lambda q: small_all.at[rank], small_all, sg_s, sg_r)

    def small_z(k):
        return remote(small, zs.at[z], sz_s.at[0], sz_r.at[0], on_z(k))

    def small_x(k):
        return remote(part, xs.at[x], sx_s.at[0], sx_r.at[0], on_x(k))

    def small_all_of(buf, send, recv):
        here = buf.at[pl.ds(0, 3)]
        return remote(here, here, send.at[0], recv.at[0], on_z(1))


    def slab(k, span):
        at = (z + k) % 4
        own = low[:, pl.ds(pl.multiple_of(at * GW, GW), GW)]
        return at, dot_tn(own, dproj[:, span]).astype(BF16).reshape(4, 2, 48, span.stop - span.start)

    for k in (2, 1, 3, 0):
        at, rows = slab(k, slice(GA, COLS))
        dwg[at] = rows
        if k:
            sums_g.first(1, k).start()
    for k in (2, 1, 3):
        sums_g.first(0, k).start()
    out = dot_tn(gated[...], gall[...].reshape(ROWS, D))
    for j in range(16):
        piece = out[j * KOUT : (j + 1) * KOUT]
        tail = jnp.concatenate([piece[16:24, 0 : D // 2], piece[16:24, D // 2 :]], axis=0)
        fold = jnp.concatenate([piece[0:16], tail], axis=1).astype(BF16)
        for h in range(2):
            dow[j % 8 // 2, j // 8 * 2 + j % 2, h] = fold[:, h * WIDE : (h + 1) * WIDE]
    sums_l.start()

    def other_copy(i):
        rows = chunk(in_turn(3 - i))
        return remote(d_other.at[rows], d_in.at[rows], u_s.at[0], u_r.at[i], sibling())

    def lower_back(k):
        at = (y + k) % 4
        rows = chunk(at)
        back = dot_nt(dproj[rows, 0:GA], wx[...].reshape(D, GA))
        back = back + dot_nt(dproj[rows, GA:COLS], wg[...].reshape(D, GW))
        back = back + dot(d_steps[rows, :], step_rows[...])
        d_low[at] = back.astype(BF16).reshape(2, SEQ, D)
        lowers.across(k).start()

    def backward(i, carry):
        @pl.when(i < 4)
        def _():
            at = in_turn(3 - i)
            for core in range(2):
                mix_back(at * 2 + core, c, proj, act, par, head, skip, dgated, dproj, d_steps, small, d_mine, d_other)
            other_copy(i).start()

        @pl.when(i == 0)
        def _():
            branches.pass_on(3)
            branches.pass_on(1)
            branches.keep()

        @pl.when(i == 3)
        def _():
            sums_g.middle()

        @pl.when(i == 4)
        def _():
            sums_l.middle()

        @pl.when(i > 0)
        def _():
            other_copy(i - 1).wait_recv()
            at = in_turn(4 - i)
            for core in range(2):
                vector_back(at * 2 + core, proj, par, d_mine, d_in, dproj, small)

        @pl.when(jnp.logical_and(i > 0, i < 3))
        def _():
            lower_back(turn(4 - i))

        @pl.when(i == 2)
        def _():
            lowers.pass_far()

        @pl.when(i == 4)
        def _():
            lowers.pass_on(3)

        return carry

    lax.fori_loop(0, 5, backward, 0)
    for k in (1, 2, 3):
        small_z(k).start()
    zs[z] = small[...]
    for k in (2, 1, 3, 0):
        at, rows = slab(k, slice(0, GA))
        dwx[at] = rows
        if k:
            sums_x.first(1, k).start()
    for k in (2, 1, 3):
        sums_x.first(0, k).start()
    steps_back = dot_tn(d_steps[...], low[...])
    for r in range(16):
        own = jnp.concatenate([steps_back[0:16, r * 96 : (r + 1) * 96], jnp.zeros((16, 32), F32)], axis=1)
        dws[r // 4, r % 4, 0] = own.astype(BF16)
    sums_s.start()
    lax.fori_loop(0, 2, lambda i, carry: (lower_back(1 - i), carry)[1], 0)
    small_all_of(zs, sz_s, sz_r).wait_recv()
    part[...] = ((zs[0] + zs[1]) + zs[2]) + zs[3]
    xs[x] = part[...]
    for k in (1, 2, 3):
        small_x(k).start()
    lowers.pass_on(1)
    sums_x.middle()
    sums_s.middle()
    lowers.keep()
    sums_g.end()
    for q in range(GROUP):
        gcut[q] = jnp.zeros((16, GW), BF16)
        gcut[q, 0:KIN, :] = fg[q // 4, q % 4 * KIN : (q % 4 + 1) * KIN, :].astype(BF16)
    gate_rows.start()
    grows_in[rank] = gcut[rank]
    sums_l.end()

    @pl.when(moves)
    def _():
        swap_back.start()

    small_all_of(xs, sx_s, sx_r).wait_recv()
    small_all[rank] = ((xs[0] + xs[1]) + xs[2]) + xs[3]
    all_small.start()
    branches.end()
    h32 = hid[...].astype(F32)
    inverse = lax.rsqrt(column(rank, wide[...]) * (1.0 / INNER) + EPSILON)
    mixed[...] = (h32 + jnp.where(live, inverse * fb[...], 0.0)).astype(BF16)
    sums_s.end()
    sums_x.end()
    step_cols = dot_tn(fs[0, 0:8], ones(iota((8, 128), 0) == iota((8, 128), 1), F32), HIGHEST)
    for q in range(GROUP):
        at = q % 4 * KIN
        cut[q] = jnp.zeros((16, CW + 128), BF16)
        cut[q, 0:KIN, 0:CW] = fx[q // 4, at : at + KIN, :].astype(BF16)
        cut[q, 0:KIN, CW:] = step_cols[q * KIN : (q + 1) * KIN].astype(BF16)
    cut_rows.start()
    rows_in[rank] = cut[rank]
    all_small.finish()
    finish_small(small_all, dvecs)

    @pl.when(moves)
    def _():
        swap_back.wait_recv()

    @pl.when(jnp.logical_not(moves))
    def _():
        swapped[...] = fl[...]

    doutw[0:16, 0:WIDE] = swapped[0]
    doutw[0:16, WIDE:D] = swapped[1, :, 0 : D - WIDE]
    doutw[16:24, 0 : D // 2] = swapped[1, 0:8, D - WIDE :]
    doutw[16:24, D // 2 : D] = swapped[1, 8:16, D - WIDE :]
    lowers.end()
    scale = lax.rsqrt(jnp.mean(h32 * h32, axis=1, keepdims=True) + EPSILON)
    normed = h32 * scale
    d_normed = fd[...] * par[0:1, :]
    through = scale * (d_normed - normed * jnp.mean(d_normed * normed, axis=1, keepdims=True))
    in_grad[...] = (grd[...].astype(F32) + through).astype(BF16)
    gate_rows.finish()
    cut_rows.finish()
    finish_rows(rows_in, grows_in, inw, vectors, dinw, dvecs)
    for gone in (grads, first_w, gate_w, vecs, lines, cuts, norms, cut_rows, gate_rows, all_small):
        gone.sent()
    for gone in (branches, lowers, sums_x, sums_g, sums_l, sums_s):
        gone.finish()
    small_all_of(zs, sz_s, sz_r).wait_send()
    small_all_of(xs, sx_s, sx_r).wait_send()
    remote(act.at[c], act.at[c], v_s.at[0], v_r.at[0], sibling()).wait_send()
    remote(d_other, d_other, u_s.at[0], u_r.at[0], sibling()).wait_send()

    @pl.when(moves)
    def _():
        swap.wait_send()
        swap_back.wait_send()


def finish_small(small, dvecs):
    me = lax.axis_index("fsdp")
    conv = jnp.zeros((8, 128), F32)
    inner = jnp.zeros((8, 128), F32)
    common = [jnp.zeros((8, 128), F32), jnp.zeros((8, 128), F32)]
    row, col = iota((GW, 128), 0), iota((GW, 128), 1)
    heads = ones(row // 64 == col, F32)
    dvecs[...] = jnp.zeros_like(dvecs)
    for q in range(GROUP):
        part = small[q, :, 0:GW]
        conv = conv + dot(part, ones(row + q * GW == col + 26 * me, F32), HIGHEST)
        inner = inner + dot(part, ones(row + q * GW == col + KOUT * me, F32), HIGHEST)
        common[q % 2] = common[q % 2] + small[q, :, GW:CW]
        span = slice(q * OWN, (q + 1) * OWN)
        dvecs[3:4, span] = small[q, 7:8, 0:OWN]
        dvecs[4:5, span] = small[q, 7:8, 128 : 128 + OWN]
        dvecs[5:6, span] = dot(part, heads, HIGHEST)[6:7, 0:OWN]
    row, col = iota((256, 128), 0), iota((256, 128), 1)
    conv = conv + dot(jnp.concatenate(common, axis=1), ones(row + INNER == col + 26 * me, F32), HIGHEST)
    dvecs[1:2] = conv[4:5]
    dvecs[2:3] = inner[5:6]
    dvecs[8:12] = conv[0:4]


def finish_rows(rows, gate_rows, inw, vectors, dinw, dvecs):
    shared = [jnp.zeros((KIN, 128), F32), jnp.zeros((KIN, 128), F32)]
    for q in range(GROUP):
        own = rows[q].astype(F32)[0:KIN]
        dinw[:, INNER + q * GW : INNER + (q + 1) * GW] = own[:, 0:GW]
        dinw[:, q * GW : (q + 1) * GW] = gate_rows[q].astype(F32)[0:KIN]
        dinw[:, STEP + q * OWN : STEP + (q + 1) * OWN] = own[:, CW : CW + OWN]
        shared[q % 2] = shared[q % 2] + own[:, GW:CW]
    dinw[:, 2 * INNER : 2 * INNER + 128] = shared[0]
    dinw[:, 2 * INNER + 128 : STEP] = shared[1]
    total = jnp.sum(dinw[...] * inw[...].astype(F32), axis=1, keepdims=True)
    spread = jnp.where(iota((KIN, 128), 0) == iota((KIN, 128), 1), total, 0.0)
    gain = jnp.where(iota((1, 128), 1) < KIN, vectors[0:1], 1.0)
    dvecs[0:1] = jnp.sum(spread, axis=0, keepdims=True) / gain


def emit_kernel(mixed, in_grad, dinw, doutw, dvecs, *outs):
    (mixed_out, grad_out, dinw_out, dgain, conv_out, dbias, ddt, da_log, dskip, dinner, doutw_out) = outs
    for given, out in ((mixed, mixed_out), (in_grad, grad_out), (dinw, dinw_out), (doutw, doutw_out)):
        out[...] = given[...]
    for i, line in enumerate((dgain, dbias, dinner, ddt, da_log, dskip)):
        line[...] = dvecs[i, 0 : line.shape[0]]
    conv_out[...] = dvecs[8:12, 0:26]


def emit(*given):
    vmem = pl.BlockSpec(memory_space=pltpu.VMEM)
    shape = jax.ShapeDtypeStruct
    line = [shape((n,), F32) for n in (KIN, 26, HEADS, HEADS, HEADS, KOUT)]
    return pl.pallas_call(
        emit_kernel,
        name="emit",
        out_shape=(*OUT_SHAPES[0:3], line[0], shape((4, 26), F32), *line[1:], OUT_SHAPES[4]),
        in_specs=[vmem] * 5,
        out_specs=(vmem,) * 11,
        compiler_params=pltpu.CompilerParams(vmem_limit_bytes=VMEM_LIMIT),
    )(*given)


def layer(*given):
    vmem, vm = pl.BlockSpec(memory_space=pltpu.VMEM), pltpu.VMEM

    def dma(*dims):
        return pltpu.SemaphoreType.DMA(dims)

    def plane_reduce(halves, rows, cols):
        block = (rows, cols)
        return [
            vm((halves, 3, 4) + block, BF16), vm((halves, 3) + block, BF16), vm((halves, 3) + block, BF16),
            vm((halves,) + block, F32),
        ]

    one, group = [dma(1)] * 2, [dma(2), dma(8)]
    group_reduce = [
        vm((4, SEQ, D), BF16), vm((3, SEQ, D), BF16), vm((2, SEQ // 2, D), BF16), vm((2, SEQ, D), BF16), vm((SEQ, D), F32)
    ]
    gather, two = [dma(2, 2), dma(2, 8)], [dma(2, 2)] * 2
    return pl.pallas_call(
        layer_kernel,
        name="layer",
        out_shape=OUT_SHAPES,
        in_specs=[vmem] * len(given),
        out_specs=(vmem,) * len(OUT_SHAPES),
        scratch_shapes=[
            vm((8, 128), F32), vm((8, 128), F32), vm((8, 128), F32),
            vm((GROUP, 16, COLS), BF16), vm((GROUP, 16, COLS), BF16), vm((2, 48, GA), BF16), vm((2, 48, GW), BF16),
            vm((32, 384), BF16), vm((2, 16, WIDE), BF16), vm((2, 16, WIDE), BF16), vm((SEQ, D), BF16),
            vm((4, 4, 2, 48, GA), BF16), vm((4, 4, 2, 48, GW), BF16), vm((4, 4, 1, 32, 384), BF16),
            vm((4, 4, 2, 16, WIDE), BF16), vm((4, 2, SEQ, D), BF16), vm((4, 2, SEQ, D), BF16),
            vm((ROWS, D), BF16), vm((ROWS, COLS + 128), F32), vm((2, ROWS, 128), F32), vm((128, D), BF16),
            vm((ROWS, GW), F32), vm((ROWS, GW), F32), vm((GW, D), BF16),
            vm((8, D), F32), vm((8, 128), F32), vm((1, GW), F32),
            vm((16, SEQ), F32), vm((GROUP, 16, SEQ), F32), vm((SEQ, SEQ), F32),
            vm((ROWS, GW), BF16), vm((ROWS, COLS), BF16), vm((ROWS, 128), BF16),
            vm((ROWS, 128), F32), vm((ROWS, 128), F32), vm((ROWS, 128), F32), vm((4, 2, SEQ, D), BF16),
            vm((4, 4, 2, 48, GA), BF16), vm((4, 4, 2, 48, GW), BF16), vm((4, 4, 2, 16, WIDE), BF16),
            vm((4, 4, 1, 16, 128), BF16), vm((8, CW), F32),
            *group_reduce, *group_reduce, *plane_reduce(2, 48, GA), *plane_reduce(2, 48, GW),
            *plane_reduce(2, 16, WIDE), *plane_reduce(1, 16, 128),
            vm((2, 16, WIDE), F32), vm((GROUP, 16, CW + 128), BF16), vm((GROUP, 16, CW + 128), BF16),
            vm((GROUP, 16, GW), BF16), vm((GROUP, 16, GW), BF16),
            vm((4, 8, CW), F32), vm((4, 8, CW), F32), vm((8, CW), F32), vm((GROUP, 8, CW), F32),
            *one, *gather, *gather, dma(1, 2), dma(1, 8), *gather, *group, *group, *one, dma(1), dma(4), dma(1), dma(4),
            *group, *group, *two, *two, *two, dma(1, 2), dma(1, 2), *one, *one, *one, *one, *one, dma(2), dma(2),
        ],
        compiler_params=pltpu.CompilerParams(collective_id=0, has_side_effects=True, vmem_limit_bytes=VMEM_LIMIT),
    )(*given)


OUT_SHAPES = (
    jax.ShapeDtypeStruct((SEQ, D), BF16),
    jax.ShapeDtypeStruct((SEQ, D), BF16),
    jax.ShapeDtypeStruct((KIN, STEP + HEADS), F32),
    jax.ShapeDtypeStruct((16, 128), F32),
    jax.ShapeDtypeStruct((KOUT, D), F32),
)


def body(
    hidden, in_weight, norm_gain, conv_weight, conv_bias, dt_bias, a_log, skip, inner_gain, out_weight, out_grad,
    seq_lengths, seq_owner,
):
    mixed, in_grad, dinw, dvecs, doutw = layer(
        hidden, in_weight, norm_gain, conv_weight.T, conv_bias, dt_bias, a_log, skip, inner_gain, out_weight, out_grad,
        seq_lengths, seq_owner,
    )
    outs = list(emit(mixed, in_grad, dinw, doutw, dvecs))
    outs[4] = outs[4].T
    return tuple(outs)


def solution(mesh):
    rows, line, whole = P("fsdp", None), P("fsdp"), P()
    return jax.shard_map(
        body,
        mesh=mesh,
        in_specs=(rows, rows, line, rows, line, whole, whole, whole, line, rows, rows, whole, whole),
        out_specs=(rows, rows, rows, line, rows, line, whole, whole, whole, line, rows),
        check_vma=False,
    )
```

```python
import functools

import jax
import jax.numpy as jnp
from jax import lax
from jax.experimental import pallas as pl
from jax.experimental.pallas import tpu as pltpu
from jax.sharding import PartitionSpec as P

MESH = pl.DeviceIdType.MESH
F32, BF16 = jnp.float32, jnp.bfloat16
HIGHEST = lax.Precision.HIGHEST
EPSILON = 1e-05

D = 1536
INNER = 3072
CONVD = 3328
HEADS = 48
SEQ = 128
GROUP = 8
ROWS = SEQ * GROUP
GW = INNER // GROUP
OWN = HEADS // GROUP
CW = GW + 128
GA, COLS = CW, CW + GW
ST = COLS
KIN = D // 128
KOUT = INNER // 128
STEP = 2 * INNER + 256
FOLD = D + D // 2
WIDE = FOLD // 2
VMEM_LIMIT = 60 * 2**20


def iota(shape, dim):
    return lax.broadcasted_iota(jnp.int32, shape, dim)


def ones(condition, kind=BF16):
    return jnp.where(condition, 1.0, 0.0).astype(kind)


def dot(a, b, precision=None):
    return lax.dot_general(a, b, (((1,), (0,)), ((), ())), precision=precision, preferred_element_type=F32)


def dot_nt(a, b, precision=None):
    return lax.dot_general(a, b, (((1,), (1,)), ((), ())), precision=precision, preferred_element_type=F32)


def dot_tn(a, b, precision=None):
    return lax.dot_general(a, b, (((0,), (0,)), ((), ())), precision=precision, preferred_element_type=F32)


def sigmoid(v):
    return 1.0 / (1.0 + jnp.exp(-v))


def softplus(v):
    return jnp.maximum(v, 0.0) + jnp.log1p(jnp.exp(-jnp.abs(v)))


def later(v, k):
    if k == 0:
        return v
    return jnp.where(iota(v.shape, 0) >= k, pltpu.roll(v, k, 0), 0.0)


def earlier(v, k):
    if k == 0:
        return v
    return jnp.where(iota(v.shape, 0) < v.shape[0] - k, pltpu.roll(v, v.shape[0] - k, 0), 0.0)


def place():
    me = lax.axis_index("fsdp")
    return me // 32, (me // 8) % 4, (me // 2) % 4, me % 2


def index(z, x, y, c):
    return ((z * 4 + x) * 4 + y) * 2 + c


def group_partner(k):
    z, x, y, c = place()
    rank = (y * 2 + c + k) % GROUP
    return index(z, x, rank // 2, rank % 2), rank


def on_z(k):
    z, x, y, c = place()
    return index((z + k) % 4, x, y, c)


def on_x(k):
    z, x, y, c = place()
    return index(z, (x + k) % 4, y, c)


def on_y(k):
    z, x, y, c = place()
    return index(z, x, (y + k) % 4, c)


def sibling():
    z, x, y, c = place()
    return index(z, x, y, 1 - c)


def swap_to():
    z, x, y, c = place()
    return index(y, x % 2 * 2 + c, z, x // 2)


def swap_from():
    z, x, y, c = place()
    return index(y, c * 2 + x // 2, z, x % 2)


def signal(target):
    pl.semaphore_signal(pltpu.get_barrier_semaphore(), inc=1, device_id=(target,), device_id_type=MESH)


def remote(src, dst, send, recv, target):
    return pltpu.make_async_remote_copy(
        src_ref=src, dst_ref=dst, send_sem=send, recv_sem=recv, device_id=(target,), device_id_type=MESH
    )


def plane_partners():
    return [on_z(k) for k in (1, 2, 3)] + [on_x(k) for k in (1, 2, 3)]


def group_partners():
    return [group_partner(k)[0] for k in range(1, GROUP)]


class PlaneGather:
    def __init__(self, buf, own, send, recv, halves):
        self.buf, self.own, self.send, self.recv, self.halves = buf, own, send, recv, halves
        self.z, self.x, _, _ = place()

    def slot(self, half, first, second):
        a, b = (first, second) if half == 0 else (second, first)
        return self.buf.at[(self.z + a) % 4, (self.x + b) % 4, half]

    def along(self, half, stage, k):
        return on_z(k) if (half == 0) == (stage == 0) else on_x(k)

    def came(self, first):
        return 3 if first < 2 else 1

    def mark(self, half, first, second):
        if second == 0:
            return self.recv.at[half, first - 1]
        return self.recv.at[half, 3 + first if second == self.came(first) else 7]

    def copy(self, half, first, stage, k):
        src = self.own(half) if first == 0 else self.slot(half, first, 0)
        at = (4 - k, 0) if stage == 0 else (first, 4 - k)
        return remote(
            src, self.slot(half, first, 0), self.send.at[half, stage], self.mark(half, *at), self.along(half, stage, k)
        )

    def relayed(self, half, first):
        came = self.came(first)
        here = self.slot(half, first, came)
        return remote(here, here, self.send.at[half, 1], self.mark(half, first, 2), self.along(half, 1, 4 - came))

    def arrival(self, half, first, second):
        here = self.slot(half, first, second)
        return remote(here, here, self.send.at[half, 0], self.mark(half, first, second), on_z(1))

    def some(self, rows, count, half):
        return self.buf.at[pl.ds(0, rows), pl.ds(0, count), half]

    def start(self):
        for k in (1, 3, 2):
            for half in range(self.halves):
                self.copy(half, 0, 0, k).start()
        for k in (1, 3):
            for half in range(self.halves):
                self.copy(half, 0, 1, k).start()

    def forward(self):
        for first in (1, 3, 2):
            for half in range(self.halves):
                self.arrival(half, first, 0).wait_recv()
                for k in (1, 3):
                    self.copy(half, first, 1, k).start()

    def relay(self):
        for first in (0, 3, 1, 2):
            for half in range(self.halves):
                self.arrival(half, first, self.came(first)).wait_recv()
                self.relayed(half, first).start()

    def finish(self):
        for half in range(self.halves):
            here = self.some(4, 2, half)
            remote(here, here, self.send.at[half, 0], self.recv.at[half, 7], on_z(1)).wait_recv()

    def sent(self):
        for half in range(self.halves):
            for stage, here in ((0, self.some(1, 3, half)), (1, self.some(4, 3, half))):
                remote(here, here, self.send.at[half, stage], self.recv.at[half, 7], on_z(1)).wait_send()


class GroupGather:
    def __init__(self, buf, own, send, recv):
        self.buf, self.own, self.send, self.recv = buf, own, send, recv
        _, _, self.y, self.c = place()

    def along(self, k):
        return remote(self.own, self.buf.at[self.y, self.c], self.send.at[0], self.recv.at[4 - k], on_y(k))

    def half(self, k):
        return pl.ds(0, SEQ // 2) if k == 3 else pl.ds(SEQ // 2, SEQ // 2)

    def relayed(self, k):
        here = self.buf.at[(self.y + k) % 4, self.c, self.half(k)]
        return remote(here, here, self.send.at[0], self.recv.at[2], on_y(4 - k))

    def across(self, k):
        src = self.own if k == 0 else self.buf.at[(self.y + k) % 4, self.c]
        dst = self.buf.at[(self.y + k) % 4, self.c]
        return remote(src, dst, self.send.at[1], self.recv.at[4 + k], sibling())

    def start(self):
        for k in (1, 3):
            self.along(k).start()
        self.across(0).start()

    def forward(self, k):
        here = self.buf.at[(self.y + k) % 4, self.c]
        remote(here, here, self.send.at[0], self.recv.at[k], sibling()).wait_recv()
        if k != 2:
            self.relayed(k).start()
        self.across(k).start()

    def arrived(self, k):
        here = self.buf.at[(self.y + k) % 4, 1 - self.c]
        remote(here, here, self.send.at[0], self.recv.at[4 + k], sibling()).wait_recv()

    def sent(self):
        for at, here in ((0, self.buf.at[pl.ds(0, 3), 0]), (1, self.buf.at[:, 0])):
            remote(here, here, self.send.at[at], self.recv.at[0], sibling()).wait_send()


def unpack_params(raw, rank, core, par, step_rows):
    row = iota((512, 1), 0)
    device = (row // 4).astype(F32)
    tap = row % 4
    values = raw[...].reshape(512, 384)

    def spots(span, first, count, channel):
        owner = jnp.floor((channel + 0.5) * (1.0 / count))
        lane = channel - owner * count + first
        pick = ones(iota((128, channel.shape[1]), 0).astype(F32) == lane)
        return jnp.where(device == owner, dot(values[:, span], pick), 0.0)

    def only(k, at):
        return jnp.sum(jnp.where(tap == k, at, 0.0), axis=0, keepdims=True)

    def lanes(n):
        return iota((1, n), 1).astype(F32)

    start = rank.astype(F32) * GW
    conv = lanes(CW)
    conv = jnp.where(conv < GW, conv + start, conv - GW + INNER + 128 * core.astype(F32))
    low, high, last = slice(0, 128), slice(128, 256), slice(256, 384)
    par[...] = jnp.zeros_like(par)
    par[0:1, :] = only(0, spots(high, 0, KIN, lanes(D)))
    taps = spots(low, 0, 26, conv)
    for k in range(4):
        par[k + 1 : k + 2, 0:CW] = only(k, taps)
    par[5:6, 0:CW] = only(0, spots(high, KIN, 26, conv))
    par[6:7, 0:GW] = only(0, spots(high, KIN + 26, KOUT, lanes(GW) + start))
    four, two = spots(last, 0, KIN, lanes(D)), spots(last, 16, KIN, lanes(D))
    rows = [only(k, four) for k in range(4)] + [only(k, two) for k in range(2)] + [jnp.zeros((122, D), F32)]
    step_rows[...] = jnp.concatenate(rows, axis=0).astype(BF16)


def own_heads(raw, rank, head, skip):
    row = iota((128, 128), 0)
    col = iota((128, 128), 1)
    given = raw[...]
    mine = dot(given, ones(jnp.logical_and(row == col + OWN * rank, col < OWN), F32), HIGHEST)
    head[...] = jnp.where(iota((8, 128), 0) == 1, -jnp.exp(mine), mine)
    wide = iota((128, GW), 0) == iota((128, GW), 1) // 64 + OWN * rank
    skip[...] = dot(given, ones(wide, F32), HIGHEST)[2:3]


def unfold_out_weight(raw, ow):
    row, col = iota((GW, 256), 0), iota((GW, 256), 1)
    device, line = row // KOUT, row % KOUT
    base = (device % 8 // 2 * 4 + device // 8 * 2 + device % 2) * 16
    top = ones(jnp.logical_and(line < 16, col == base + line))
    low_left = ones(jnp.logical_and(line >= 16, col == base + line - 16))
    low_right = ones(jnp.logical_and(line >= 16, col == base + line - 8))
    first = raw[:, :, 0].reshape(256, WIDE)
    second = raw[:, :, 1].reshape(256, WIDE)
    half, split = D // 2, WIDE - D // 2
    left, right_a = first[:, 0:half], first[:, half:]
    right_b, tail = second[:, 0 : half - split], second[:, half - split :]
    ow[:, 0:half] = (dot(top, left) + dot(low_left, tail)).astype(BF16)
    ow[:, half : half + split] = (dot(top, right_a) + dot(low_right, tail[:, 0:split])).astype(BF16)
    ow[:, half + split :] = (dot(top, right_b) + dot(low_right, tail[:, split:])).astype(BF16)


def convolve(raw, par, at, width):
    out = par[5:6, at : at + width] + raw * par[4:5, at : at + width]
    for k in range(3):
        out = out + later(raw, 3 - k) * par[k + 1 : k + 2, at : at + width]
    return out


def steps_forward(b, proj, head, steps, totals):
    rows = pl.ds(pl.multiple_of(b * SEQ, SEQ), SEQ)
    step = softplus(proj[rows, ST:] + head[0:1, :])
    lower = ones(iota((SEQ, SEQ), 0) >= iota((SEQ, SEQ), 1), F32)
    steps[rows, :] = step
    totals[rows, :] = dot(lower, head[1:2, :] * step, HIGHEST)


def activate(v, out, slope):
    s = sigmoid(v)
    out[...] = v * s
    slope[...] = s * (1.0 + v * (1.0 - s))


def mix_forward(b, proj, act, par, skip, steps, totals, values, slopes, scores, heads_out):
    row, col = iota((SEQ, SEQ), 0), iota((SEQ, SEQ), 1)
    causal = row >= col
    rows = pl.ds(pl.multiple_of(b * SEQ, SEQ), SEQ)
    total = totals[rows, :]
    total_t, step_t = total.T, steps[rows, :].T
    score = dot_nt(act[1, rows, :], act[0, rows, :], HIGHEST)
    scores[b] = score
    for p in range(3):
        span = slice(p * 128, p * 128 + 128)
        activate(convolve(proj[rows, span], par, p * 128, 128), values.at[rows, span], slopes.at[rows, span])
        value = values[rows, span]
        value_low = value.astype(BF16)
        parts = []
        for h in (2 * p, 2 * p + 1):
            decays = jnp.exp(jnp.where(causal, total[:, h : h + 1] - total_t[h : h + 1, :], -1e30))
            mix = (decays * score * step_t[h : h + 1, :]).astype(BF16)
            parts.append(dot(mix, value_low))
        heads_out[rows, span] = jnp.where(col < 64, parts[0], parts[1]) + skip[0:1, span] * value


def weigh(b, proj, par, heads_out, gated):
    rows = pl.ds(pl.multiple_of(b * SEQ, SEQ), SEQ)
    gate = proj[rows, GA:COLS]
    gated[rows, :] = (heads_out[rows, :] * gate * sigmoid(gate) * par[6:7, 0:GW]).astype(BF16)


def column(at, values):
    return jnp.sum(jnp.where(iota((SEQ, SEQ), 1) == at, values, 0.0), axis=1, keepdims=True)


def norm_sums(b, proj, par, heads_out, dgated, acc):
    rows = pl.ds(pl.multiple_of(b * SEQ, SEQ), SEQ)
    gate = proj[rows, GA:COLS]
    product = heads_out[rows, :] * gate * sigmoid(gate)
    squares = jnp.sum(product * product, axis=1, keepdims=True)
    crosses = jnp.sum(product * dgated[rows, :] * par[6:7, 0:GW], axis=1, keepdims=True)
    col = iota((SEQ, SEQ), 1)
    return jnp.where(col == b, squares, jnp.where(col == b + 8, crosses, acc))


def norm_back(b, proj, par, wide, heads_out, dgated, gated, dproj, small):
    rows = pl.ds(pl.multiple_of(b * SEQ, SEQ), SEQ)
    cross = column(b + 8, wide[...])
    inverse = lax.rsqrt(column(b, wide[...]) * (1.0 / INNER) + EPSILON)
    mean = cross * inverse * (1.0 / INNER)
    out = heads_out[rows, :]
    gate = proj[rows, GA:COLS]
    s = sigmoid(gate)
    silu = gate * s
    unit = out * silu * inverse
    dg = dgated[rows, :]
    gain = par[6:7, 0:GW]
    gated[rows, :] = (unit * gain).astype(BF16)
    small[5:6, 0:GW] += jnp.sum(dg * unit, axis=0, keepdims=True)
    d_product = (dg * gain - unit * mean) * inverse
    dproj[rows, GA:COLS] = (d_product * out * (s * (1.0 + gate * (1.0 - s)))).astype(BF16)
    dgated[rows, :] = d_product * silu


def conv_back(d_conv, raw, par, small, at):
    span = slice(at, at + 128)
    back = d_conv * par[4:5, span]
    small[3:4, span] += jnp.sum(d_conv * raw, axis=0, keepdims=True)
    for k in range(3):
        ahead = earlier(d_conv, 3 - k)
        back = back + ahead * par[k + 1 : k + 2, span]
        small[k : k + 1, span] += jnp.sum(ahead * raw, axis=0, keepdims=True)
    small[4:5, span] += jnp.sum(d_conv, axis=0, keepdims=True)
    return back


def mix_back(
    b, core, proj, act, par, head, skip, steps, totals, values, slopes, scores, d_heads, dproj, d_steps, small, d_mine,
    d_other,
):
    row, col = iota((SEQ, SEQ), 0), iota((SEQ, SEQ), 1)
    later_ok = col >= row
    left, right = col < 64, col >= 64
    suffix = ones(row >= col)
    before = row < col
    rows = pl.ds(pl.multiple_of(b * SEQ, SEQ), SEQ)
    step, total = steps[rows, :], totals[rows, :]
    total_t = total.T
    scores_t = scores[b].T
    d_scores = jnp.zeros((SEQ, SEQ), F32)
    direct = jnp.zeros((SEQ, SEQ), F32)
    lines = []
    for p in range(3):
        span = slice(p * 128, p * 128 + 128)
        d_out = d_heads[rows, span]
        value = values[rows, span]
        small[6:7, span] += jnp.sum(d_out * value, axis=0, keepdims=True)
        value_low = value.astype(BF16)
        d_low = d_out.astype(BF16)
        parts = []
        for i, h in enumerate((2 * p, 2 * p + 1)):
            decays = jnp.exp(jnp.where(later_ok, total_t[h : h + 1, :] - total[:, h : h + 1], -1e30))
            size = step[:, h : h + 1]
            own = jnp.where(left if i == 0 else right, d_out, 0.0).astype(BF16)
            d_mix = decays * dot_nt(value_low, own)
            d_scores = d_scores + d_mix * size
            per_step = (d_mix * scores_t).astype(BF16)
            tail = dot(per_step, suffix)
            direct = jnp.where(col == h, tail[:, 0:1], direct)
            lines.append(jnp.sum(jnp.where(before, tail * size, 0.0), axis=0, keepdims=True))
            mix = (decays * scores_t * size).astype(BF16)
            parts.append(dot(mix, d_low))
        d_values = jnp.where(left, parts[0], parts[1]) + skip[0:1, span] * d_out
        d_conv = d_values * slopes[rows, span]
        dproj[rows, span] = conv_back(d_conv, proj[rows, span], par, small, p * 128).astype(BF16)
    d_decay = jnp.concatenate(lines + [jnp.zeros((SEQ - OWN, SEQ), F32)], axis=0).T
    d_step = direct + head[1:2, :] * d_decay
    d_raw = d_step * sigmoid(proj[rows, ST:] + head[0:1, :])
    small[7:8, 0:128] += jnp.sum(d_raw, axis=0, keepdims=True)
    small[7:8, 128:256] += jnp.sum(d_decay * head[1:2, :] * step, axis=0, keepdims=True)
    d_low = d_scores.astype(BF16)
    d_write = dot(d_low, act[1, rows, :].astype(BF16))
    d_read = dot_tn(d_low, act[0, rows, :].astype(BF16))
    d_mine[rows, :] = jnp.where(core == 0, d_write, d_read)
    d_other[rows, :] = jnp.where(core == 0, d_read, d_write)
    d_steps[rows, :] = d_raw.astype(BF16)


def vector_forward(b, core, proj, act, slopes, par):
    rows = pl.ds(pl.multiple_of(b * SEQ, SEQ), SEQ)
    activate(convolve(proj[rows, GW:CW], par, GW, 128), act.at[core, rows, :], slopes.at[rows, GW:CW])


def vector_back(b, proj, par, slopes, d_mine, d_in, dproj, small):
    rows = pl.ds(pl.multiple_of(b * SEQ, SEQ), SEQ)
    d_conv = (d_mine[rows, :] + d_in[rows, :]) * slopes[rows, GW:CW]
    dproj[rows, GW:CW] = conv_back(d_conv, proj[rows, GW:CW], par, small, GW).astype(BF16)


class PlaneReduce:
    def __init__(self, terms, got, mid, last, out, send, recv, halves=2):
        self.terms, self.got, self.mid, self.last, self.out = terms, got, mid, last, out
        self.send, self.recv, self.halves = send, recv, halves
        self.z, self.x, _, _ = place()

    def line(self, half, k):
        return self.terms.at[:, (self.x + k) % 4, 0] if half == 0 else self.terms.at[(self.z + k) % 4, :, 1]

    def first(self, half, k):
        target = on_x(k) if half == 0 else on_z(k)
        return remote(self.line(half, k), self.got.at[half, k - 1], self.send.at[half, 0], self.recv.at[half, 0], target)

    def second(self, half, k):
        target = on_z(k) if half == 0 else on_x(k)
        return remote(self.mid.at[half, k - 1], self.last.at[half, k - 1], self.send.at[half, 1], self.recv.at[half, 1], target)

    def stage(self, half, at, like):
        return remote(like.at[half], like.at[half], self.send.at[half, at], self.recv.at[half, at], on_z(1))

    def start(self):
        for k in (2, 1, 3):
            for half in reversed(range(self.halves)):
                self.first(half, k).start()

    def middle(self):
        for half in reversed(range(self.halves)):
            self.stage(half, 0, self.got).wait_recv()
            for k in (2, 1, 3, 0):
                if half == 0:
                    at = (self.z + k) % 4
                    total = self.terms[at, self.x, 0].astype(F32)
                else:
                    at = (self.x + k) % 4
                    total = self.terms[self.z, at, 1].astype(F32)
                for j in range(3):
                    total = total + self.got[half, j, at].astype(F32)
                if k:
                    self.mid[half, k - 1] = total.astype(BF16)
                    self.second(half, k).start()
                else:
                    self.out[half] = total

    def end(self):
        for half in reversed(range(self.halves)):
            self.stage(half, 1, self.last).wait_recv()
            total = self.out[half]
            for j in range(3):
                total = total + self.last[half, j].astype(F32)
            self.out[half] = total

    def finish(self):
        for half in reversed(range(self.halves)):
            self.stage(half, 0, self.got).wait_send()
            self.stage(half, 1, self.mid).wait_send()


class GroupReduce:
    def __init__(self, terms, got, mid, relay, last, out, send, recv):
        self.terms, self.got, self.mid, self.relay, self.last, self.out = terms, got, mid, relay, last, out
        self.send, self.recv = send, recv
        _, _, self.y, self.c = place()

    def across(self, k):
        src = self.terms.at[(self.y + k) % 4, 1 - self.c]
        return remote(src, self.got.at[k], self.send.at[0], self.recv.at[k], sibling())

    def along(self, k):
        at = (k - 1) // 2
        return remote(self.mid.at[k - 1], self.last.at[at], self.send.at[1], self.recv.at[6], on_y(k))

    def far(self, at):
        src = self.mid.at[1, pl.ds(at * (SEQ // 2), SEQ // 2)]
        return remote(src, self.relay.at[at], self.send.at[1], self.recv.at[4 + at], on_y(3 if at else 1))

    def half(self, k):
        self.across(k).wait_recv()
        return self.terms[(self.y + k) % 4, self.c].astype(F32) + self.got[k].astype(F32)

    def pass_far(self):
        self.mid[1] = self.half(2).astype(BF16)
        for at in range(2):
            self.far(at).start()

    def pass_on(self, k):
        at = (k - 1) // 2
        total = self.half(k)
        self.far(at).wait_recv()
        came = self.relay[at].astype(F32)
        upper, lower = total[0 : SEQ // 2], total[SEQ // 2 :]
        if at == 0:
            upper = upper + came
        else:
            lower = lower + came
        self.mid[k - 1, 0 : SEQ // 2] = upper.astype(BF16)
        self.mid[k - 1, SEQ // 2 :] = lower.astype(BF16)
        self.along(k).start()

    def keep(self):
        self.out[...] = self.half(0)

    def end(self):
        total = self.out[...]
        remote(self.last, self.last, self.send.at[1], self.recv.at[6], sibling()).wait_recv()
        self.out[...] = total + self.last[0].astype(F32) + self.last[1].astype(F32)

    def finish(self):
        for at, here in ((0, self.got), (1, self.mid)):
            remote(here, here, self.send.at[at], self.recv.at[6], sibling()).wait_send()


class Members:
    def __init__(self, src, buf, send, recv):
        self.src, self.buf, self.send, self.recv = src, buf, send.at[0], recv.at[0]
        _, _, y, c = place()
        self.rank = y * 2 + c

    def start(self):
        for k in range(1, GROUP):
            target, q = group_partner(k)
            remote(self.src(q), self.buf.at[self.rank], self.send, self.recv, target).start()

    def others(self):
        here = self.buf.at[pl.ds(0, GROUP - 1)]
        return remote(here, here, self.send, self.recv, sibling())

    def finish(self):
        self.others().wait_recv()

    def sent(self):
        self.others().wait_send()


def layer_kernel(
    hid, inw, gain_in, taps, bias_in, dt_in, a_in, skip_in, inner_in, outw, grd, lengths, owners,
    mixed, in_grad, dinw, dvecs, doutw,
    vectors, heads_in, tap_rows,
    split, joined, block, gblock, params, outl, placed, live_grd,
    wx, wg, praw, plane, hall, gall, low, proj, act, step_rows, steps, totals, values, slopes, scores, heads_out, dgated, ow, par, head, skip, sums, slots, wide,
    gated, dproj, d_steps, d_mine, d_other, d_in, dwx, dwg, dow, dws, small,
    gb, mb, tb, lb, fb, gd, md, td, ld, fd, gx, mx, lx, fx, gg, mg, lg, fg, gl, ml, ll, fl, gs, ms, ls, fs,
    swapped, cut, rows_in, gcut, grows_in, zs, xs, part, small_all,
    a_s, a_r, wx_s, wx_r, wg_s, wg_r, p_s, p_r, l_s, l_r, h_s, h_r, g_s, g_r, n_s, n_r, v_s, v_r, u_s, u_r,
    b_s, b_r, d_s, d_r, rx_s, rx_r, rg_s, rg_r, rl_s, rl_r, rs_s, rs_r, rr_s, rr_r, rq_s, rq_r,
    sz_s, sz_r, sx_s, sx_r, sg_s, sg_r, swap_s, swap_r,
):
    z, x, y, c = place()
    rank = y * 2 + c
    me = lax.axis_index("fsdp")
    partners = plane_partners() + group_partners()
    moves = swap_to() != me
    for p in partners:
        signal(p)

    @pl.when(moves)
    def _():
        signal(swap_to())
        signal(swap_from())

    vectors[...] = jnp.zeros_like(vectors)
    heads_in[...] = jnp.zeros_like(heads_in)
    tap_rows[...] = jnp.zeros_like(tap_rows)
    vectors[0:1, 0:KIN] = gain_in[...].astype(F32)[None, :]
    vectors[0:1, KIN : KIN + 26] = bias_in[...].astype(F32)[None, :]
    vectors[0:1, KIN + 26 : KIN + 26 + KOUT] = inner_in[...].astype(F32)[None, :]
    for i, line in enumerate((dt_in, a_in, skip_in)):
        heads_in[i : i + 1, 0:HEADS] = line[...][None, :]
    tap_rows[0:4, 0:26] = taps[...].astype(F32)
    col_steps = inw[:, STEP : STEP + HEADS]
    steps_low = dot_tn(col_steps, ones(iota((KIN, 128), 0) == iota((KIN, 128), 1)))
    steps_high = dot_tn(col_steps, ones(iota((KIN, 128), 0) + 16 == iota((KIN, 128), 1)))
    rest = jnp.zeros((4, 128), F32)

    def padded(span, extra):
        return jnp.concatenate([inw[:, span].astype(F32), extra], axis=0).astype(BF16)

    vector_cols = [padded(slice(2 * INNER + 128 * i, 2 * INNER + 128 * (i + 1)), rest) for i in range(2)]
    for q in range(GROUP):
        at = q * OWN
        two = jnp.concatenate([steps_high[at + 4 : at + OWN], jnp.zeros((2, 128), F32)], axis=0)
        extra = jnp.concatenate([tap_rows[0:4], vectors[0:4], steps_low[at : at + 4] + two], axis=1)
        split[q, :, 0:GW] = padded(slice(INNER + q * GW, INNER + (q + 1) * GW), extra)
        split[q, :, GW:CW] = vector_cols[q % 2]
        split[q, :, GA:COLS] = padded(slice(q * GW, (q + 1) * GW), jnp.zeros((4, GW), F32))
    end = outw[16:24, :].astype(F32)
    tail = jnp.concatenate([end[:, 0 : D // 2], end[:, D // 2 :]], axis=0).astype(BF16)
    outl[0] = outw[0:16, 0:WIDE]
    outl[1, :, 0 : D - WIDE] = outw[0:16, WIDE:D]
    outl[1, :, D - WIDE :] = tail

    @pl.when(moves)
    def _():
        pl.semaphore_wait(pltpu.get_barrier_semaphore(), len(partners) + 2)

    @pl.when(jnp.logical_not(moves))
    def _():
        pl.semaphore_wait(pltpu.get_barrier_semaphore(), len(partners))

    cuts = Members(lambda q: split.at[q], joined, a_s, a_r)
    cuts.start()
    swap = remote(outl, placed, swap_s.at[0], swap_r.at[0], swap_to())
    swap_back = remote(fl, swapped, swap_s.at[1], swap_r.at[1], swap_from())

    @pl.when(moves)
    def _():
        swap.start()

    joined[rank] = split[rank]
    length = jnp.sum(jnp.where(owners[...][None, :] == me, lengths[...][None, :], 0), axis=1, keepdims=True)
    live = iota((SEQ, 1), 0) < length
    live_grd[...] = jnp.where(live, grd[...].astype(F32), 0.0).astype(BF16)
    own_heads(heads_in, rank, head, skip)

    hidden = GroupGather(hall, hid, h_s, h_r)
    grads = GroupGather(gall, live_grd, g_s, g_r)
    first_w = PlaneGather(wx, lambda h: block.at[h], wx_s, wx_r, 2)
    gate_w = PlaneGather(wg, lambda h: gblock.at[h], wg_s, wg_r, 2)
    vecs = PlaneGather(praw, lambda h: params, p_s, p_r, 1)
    lines = PlaneGather(plane, lambda h: placed.at[h], l_s, l_r, 2)

    hidden.start()
    cuts.finish()
    row, col = iota((128, 128), 0), iota((128, 128), 1)
    member, line = col // 16, col % 16
    spot = jnp.where(line < KIN, member * KIN + line, 96 + member * 4 + line - KIN)
    both = dot(ones(spot == row), joined[...].reshape(128, COLS)).astype(BF16)
    for h in range(2):
        block[h] = both[48 * h : 48 * h + 48, 0:GA]
        gblock[h] = both[48 * h : 48 * h + 48, GA:COLS]
    params[...] = both[96:128, 0:384]
    vecs.start()
    first_w.start()
    grads.start()
    wx[z, x] = block[...]
    wg[z, x] = gblock[...]
    praw[z, x, 0] = params[...]
    hall[y, c] = hid[...]
    gall[y, c] = live_grd[...]
    vecs.forward()
    first_w.forward()
    gate_w.start()

    @pl.when(moves)
    def _():
        swap.wait_recv()

    @pl.when(jnp.logical_not(moves))
    def _():
        placed[...] = outl[...]

    lines.start()
    plane[z, x] = placed[...]
    hidden.forward(1)
    hidden.forward(3)
    vecs.relay()
    first_w.relay()
    vecs.finish()
    unpack_params(praw, rank, c, par, step_rows)
    gate_w.forward()
    lines.forward()

    def chunk(i):
        return pl.ds(pl.multiple_of(i * 256, 256), 256)

    def turn(i):
        return i + i // 2 * (5 - 2 * i)

    def in_turn(i):
        return (y + turn(i)) % 4

    def vector_copy(i):
        here = act.at[c, chunk(in_turn(i))]
        return remote(here, here, v_s.at[0], v_r.at[i], sibling())

    def vector_arrival(i):
        here = act.at[1 - c, chunk(in_turn(i))]
        return remote(here, here, v_s.at[0], v_r.at[i], sibling())

    def prepare(at):
        for core in range(2):
            h = hall[at, core].astype(F32)
            scale = lax.rsqrt(jnp.mean(h * h, axis=1, keepdims=True) + EPSILON)
            rows = pl.ds(pl.multiple_of(at * 256 + core * SEQ, SEQ), SEQ)
            low[rows, :] = (h * scale * par[0:1, :]).astype(BF16)
        proj[chunk(at), ST:] = dot_nt(low[chunk(at), :], step_rows[...])
        for core in range(2):
            steps_forward(at * 2 + core, proj, head, steps, totals)

    def forward(i, carry):
        @pl.when(i == 1)
        def _():
            hidden.arrived(1)
            hidden.forward(2)

        @pl.when(i == 2)
        def _():
            hidden.arrived(3)
            gate_w.relay()

        @pl.when(i == 3)
        def _():
            hidden.arrived(2)
            lines.relay()
            grads.forward(1)
            grads.forward(3)

        @pl.when(jnp.logical_and(i > 0, i < 4))
        def _():
            prepare(in_turn(i))

        @pl.when(i < 4)
        def _():
            at = in_turn(i)
            rows = chunk(at)
            proj[rows, 0:GA] = dot(low[rows, :], wx[...].reshape(D, GA))
            for core in range(2):
                vector_forward(at * 2 + core, c, proj, act, slopes, par)
            vector_copy(i).start()

        @pl.when(i > 0)
        def _():
            vector_arrival(i - 1).wait_recv()
            at = in_turn(i - 1)
            for core in range(2):
                mix_forward(at * 2 + core, proj, act, par, skip, steps, totals, values, slopes, scores, heads_out)

        return carry

    hidden.arrived(0)
    prepare(y)
    first_w.finish()
    lax.fori_loop(0, 5, forward, 0)
    gate_w.finish()

    def project_gate(i, carry):
        proj[chunk(i), GA:COLS] = dot(low[chunk(i), :], wg[...].reshape(D, GW))
        return carry

    lax.fori_loop(0, ROWS // 256, project_gate, 0)

    def weighed(b, carry):
        weigh(b, proj, par, heads_out, gated)
        return carry

    lax.fori_loop(0, GROUP, weighed, 0)
    lines.finish()
    unfold_out_weight(plane, ow)
    grads.forward(2)
    grads.arrived(0)

    def pull(i, carry):
        @pl.when(i == 1)
        def _():
            grads.arrived(1)

        @pl.when(i == 2)
        def _():
            grads.arrived(3)

        @pl.when(i == 3)
        def _():
            grads.arrived(2)

        at = in_turn(i)
        dgated[chunk(at), :] = dot_nt(gall[at].reshape(256, D), ow[...])
        return carry

    lax.fori_loop(0, 4, pull, 0)
    acc = lax.fori_loop(
        0, GROUP, lambda b, acc: norm_sums(b, proj, par, heads_out, dgated, acc), jnp.zeros((SEQ, SEQ), F32)
    )
    sums[...] = acc.T[0:16, :]
    norms = Members(lambda q: sums, slots, n_s, n_r)
    norms.start()
    slots[rank] = sums[...]
    small[...] = jnp.zeros_like(small)
    hidden.sent()
    branch = hall
    branches = GroupReduce(branch, gb, mb, tb, lb, fb, b_s, b_r)

    def out_term(i, carry):
        at = in_turn(3 - i)
        branch[at] = dot(gated[chunk(at), :], ow[...]).astype(BF16).reshape(2, SEQ, D)
        branches.across(turn(3 - i)).start()
        return carry

    lax.fori_loop(0, 4, out_term, 0)
    norms.finish()
    total = slots[0]
    for q in range(1, GROUP):
        total = total + slots[q]
    wide[...] = jnp.concatenate([total, jnp.zeros((SEQ - 16, SEQ), F32)], axis=0).T

    def norms_back(b, carry):
        norm_back(b, proj, par, wide, heads_out, dgated, gated, dproj, small)
        return carry

    lax.fori_loop(0, GROUP, norms_back, 0)
    branches.pass_far()

    d_low = gall
    lowers = GroupReduce(d_low, gd, md, td, ld, fd, d_s, d_r)
    sums_x = PlaneReduce(dwx, gx, mx, lx, fx, rx_s, rx_r)
    sums_g = PlaneReduce(dwg, gg, mg, lg, fg, rg_s, rg_r)
    sums_l = PlaneReduce(dow, gl, ml, ll, fl, rl_s, rl_r)
    sums_s = PlaneReduce(dws, gs, ms, ls, fs, rs_s, rs_r, 1)
    cut_rows = Members(lambda q: cut.at[q], rows_in, rr_s, rr_r)
    gate_rows = Members(lambda q: gcut.at[q], grows_in, rq_s, rq_r)
    all_small = Members(lambda q: small_all.at[rank], small_all, sg_s, sg_r)

    def small_z(k):
        return remote(small, zs.at[z], sz_s.at[0], sz_r.at[0], on_z(k))

    def small_x(k):
        return remote(part, xs.at[x], sx_s.at[0], sx_r.at[0], on_x(k))

    def small_all_of(buf, send, recv):
        here = buf.at[pl.ds(0, 3)]
        return remote(here, here, send.at[0], recv.at[0], on_z(1))

    def slab(k, span):
        at = (z + k) % 4
        own = low[:, pl.ds(pl.multiple_of(at * GW, GW), GW)]
        return at, dot_tn(own, dproj[:, span]).astype(BF16).reshape(4, 2, 48, span.stop - span.start)

    for k in (2, 1, 3, 0):
        at, rows = slab(k, slice(GA, COLS))
        dwg[at] = rows
        if k:
            sums_g.first(1, k).start()
    for k in (2, 1, 3):
        sums_g.first(0, k).start()
    out = dot_tn(gated[...], gall[...].reshape(ROWS, D))
    for j in range(16):
        piece = out[j * KOUT : (j + 1) * KOUT]
        tail = jnp.concatenate([piece[16:24, 0 : D // 2], piece[16:24, D // 2 :]], axis=0)
        fold = jnp.concatenate([piece[0:16], tail], axis=1).astype(BF16)
        for h in range(2):
            dow[j % 8 // 2, j // 8 * 2 + j % 2, h] = fold[:, h * WIDE : (h + 1) * WIDE]
    sums_l.start()
    grads.sent()

    def other_copy(i):
        rows = chunk(in_turn(3 - i))
        return remote(d_other.at[rows], d_in.at[rows], u_s.at[0], u_r.at[i], sibling())

    def lower_back(k):
        at = (y + k) % 4
        rows = chunk(at)
        back = dot_nt(dproj[rows, 0:GA], wx[...].reshape(D, GA))
        back = back + dot_nt(dproj[rows, GA:COLS], wg[...].reshape(D, GW))
        back = back + dot(d_steps[rows, :], step_rows[...])
        d_low[at] = back.astype(BF16).reshape(2, SEQ, D)
        lowers.across(k).start()

    def backward(i, carry):
        @pl.when(i < 4)
        def _():
            at = in_turn(3 - i)
            for core in range(2):
                mix_back(
                    at * 2 + core, c, proj, act, par, head, skip, steps, totals, values, slopes, scores, dgated, dproj,
                    d_steps, small, d_mine, d_other,
                )
            other_copy(i).start()

        @pl.when(i == 0)
        def _():
            branches.pass_on(3)
            branches.pass_on(1)
            branches.keep()

        @pl.when(i > 0)
        def _():
            other_copy(i - 1).wait_recv()
            at = in_turn(4 - i)
            for core in range(2):
                vector_back(at * 2 + core, proj, par, slopes, d_mine, d_in, dproj, small)

        @pl.when(i == 1)
        def _():
            lower_back(2)

        @pl.when(i == 3)
        def _():
            lowers.pass_far()

        return carry

    lax.fori_loop(0, 5, backward, 0)
    for k in (1, 2, 3):
        small_z(k).start()
    zs[z] = small[...]
    for k in (2, 1, 3, 0):
        at, rows = slab(k, slice(0, GA))
        dwx[at] = rows
        if k:
            sums_x.first(1, k).start()
    for k in (2, 1, 3):
        sums_x.first(0, k).start()
    sums_g.middle()
    sums_l.middle()
    steps_back = dot_tn(d_steps[...], low[...])
    for r in range(16):
        own = jnp.concatenate([steps_back[0:16, r * 96 : (r + 1) * 96], jnp.zeros((16, 32), F32)], axis=1)
        dws[r // 4, r % 4, 0] = own.astype(BF16)
    sums_s.start()

    def lower_backs(i, carry):
        lower_back(turn(2 - i))
        return carry

    lax.fori_loop(0, 3, lower_backs, 0)
    lowers.pass_on(3)
    lowers.pass_on(1)
    small_all_of(zs, sz_s, sz_r).wait_recv()
    part[...] = ((zs[0] + zs[1]) + zs[2]) + zs[3]
    xs[x] = part[...]
    for k in (1, 2, 3):
        small_x(k).start()
    sums_x.middle()
    sums_s.middle()
    lowers.keep()
    sums_g.end()
    for q in range(GROUP):
        gcut[q] = jnp.zeros((16, GW), BF16)
        gcut[q, 0:KIN, :] = fg[q // 4, q % 4 * KIN : (q % 4 + 1) * KIN, :].astype(BF16)
    gate_rows.start()
    grows_in[rank] = gcut[rank]
    sums_l.end()

    @pl.when(moves)
    def _():
        swap_back.start()

    small_all_of(xs, sx_s, sx_r).wait_recv()
    small_all[rank] = ((xs[0] + xs[1]) + xs[2]) + xs[3]
    all_small.start()
    branches.end()
    h32 = hid[...].astype(F32)
    inverse = lax.rsqrt(column(rank, wide[...]) * (1.0 / INNER) + EPSILON)
    mixed[...] = (h32 + jnp.where(live, inverse * fb[...], 0.0)).astype(BF16)
    sums_s.end()
    sums_x.end()
    step_cols = dot_tn(fs[0, 0:8], ones(iota((8, 128), 0) == iota((8, 128), 1), F32), HIGHEST)
    for q in range(GROUP):
        at = q % 4 * KIN
        cut[q] = jnp.zeros((16, CW + 128), BF16)
        cut[q, 0:KIN, 0:CW] = fx[q // 4, at : at + KIN, :].astype(BF16)
        cut[q, 0:KIN, CW:] = step_cols[q * KIN : (q + 1) * KIN].astype(BF16)
    cut_rows.start()
    rows_in[rank] = cut[rank]
    all_small.finish()
    finish_small(small_all, dvecs)

    @pl.when(moves)
    def _():
        swap_back.wait_recv()

    @pl.when(jnp.logical_not(moves))
    def _():
        swapped[...] = fl[...]

    doutw[0:16, 0:WIDE] = swapped[0]
    doutw[0:16, WIDE:D] = swapped[1, :, 0 : D - WIDE]
    doutw[16:24, 0 : D // 2] = swapped[1, 0:8, D - WIDE :]
    doutw[16:24, D // 2 : D] = swapped[1, 8:16, D - WIDE :]
    lowers.end()
    scale = lax.rsqrt(jnp.mean(h32 * h32, axis=1, keepdims=True) + EPSILON)
    normed = h32 * scale
    d_normed = fd[...] * par[0:1, :]
    through = scale * (d_normed - normed * jnp.mean(d_normed * normed, axis=1, keepdims=True))
    in_grad[...] = (grd[...].astype(F32) + through).astype(BF16)
    gate_rows.finish()
    gate_total = finish_gate(grows_in, inw, dinw)
    cut_rows.finish()
    finish_rows(rows_in, gate_total, inw, vectors, dinw, dvecs)
    for gone in (first_w, gate_w, vecs, lines, cuts, norms, cut_rows, gate_rows, all_small):
        gone.sent()
    for gone in (branches, lowers, sums_x, sums_g, sums_l, sums_s):
        gone.finish()
    small_all_of(zs, sz_s, sz_r).wait_send()
    small_all_of(xs, sx_s, sx_r).wait_send()
    remote(act.at[c], act.at[c], v_s.at[0], v_r.at[0], sibling()).wait_send()
    remote(d_other, d_other, u_s.at[0], u_r.at[0], sibling()).wait_send()

    @pl.when(moves)
    def _():
        swap.wait_send()
        swap_back.wait_send()


def finish_small(small, dvecs):
    me = lax.axis_index("fsdp")
    conv = jnp.zeros((8, 128), F32)
    inner = jnp.zeros((8, 128), F32)
    common = [jnp.zeros((8, 128), F32), jnp.zeros((8, 128), F32)]
    row, col = iota((GW, 128), 0), iota((GW, 128), 1)
    heads = ones(row // 64 == col, F32)
    dvecs[...] = jnp.zeros_like(dvecs)
    for q in range(GROUP):
        part = small[q, :, 0:GW]
        conv = conv + dot(part, ones(row + q * GW == col + 26 * me, F32), HIGHEST)
        inner = inner + dot(part, ones(row + q * GW == col + KOUT * me, F32), HIGHEST)
        common[q % 2] = common[q % 2] + small[q, :, GW:CW]
        span = slice(q * OWN, (q + 1) * OWN)
        dvecs[3:4, span] = small[q, 7:8, 0:OWN]
        dvecs[4:5, span] = small[q, 7:8, 128 : 128 + OWN]
        dvecs[5:6, span] = dot(part, heads, HIGHEST)[6:7, 0:OWN]
    row, col = iota((256, 128), 0), iota((256, 128), 1)
    conv = conv + dot(jnp.concatenate(common, axis=1), ones(row + INNER == col + 26 * me, F32), HIGHEST)
    dvecs[1:2] = conv[4:5]
    dvecs[2:3] = inner[5:6]
    dvecs[8:12] = conv[0:4]


def finish_gate(gate_rows, inw, dinw):
    for q in range(GROUP):
        dinw[:, q * GW : (q + 1) * GW] = gate_rows[q].astype(F32)[0:KIN]
    return jnp.sum(dinw[:, 0:INNER] * inw[:, 0:INNER].astype(F32), axis=1, keepdims=True)


def finish_rows(rows, gate_total, inw, vectors, dinw, dvecs):
    shared = [jnp.zeros((KIN, 128), F32), jnp.zeros((KIN, 128), F32)]
    for q in range(GROUP):
        own = rows[q].astype(F32)[0:KIN]
        dinw[:, INNER + q * GW : INNER + (q + 1) * GW] = own[:, 0:GW]
        dinw[:, STEP + q * OWN : STEP + (q + 1) * OWN] = own[:, CW : CW + OWN]
        shared[q % 2] = shared[q % 2] + own[:, GW:CW]
    dinw[:, 2 * INNER : 2 * INNER + 128] = shared[0]
    dinw[:, 2 * INNER + 128 : STEP] = shared[1]
    total = gate_total + jnp.sum(dinw[:, INNER:] * inw[:, INNER:].astype(F32), axis=1, keepdims=True)
    spread = jnp.where(iota((KIN, 128), 0) == iota((KIN, 128), 1), total, 0.0)
    gain = jnp.where(iota((1, 128), 1) < KIN, vectors[0:1], 1.0)
    dvecs[0:1] = jnp.sum(spread, axis=0, keepdims=True) / gain


def emit_kernel(mixed, in_grad, dinw, doutw, dvecs, *outs):
    (mixed_out, grad_out, dinw_out, dgain, conv_out, dbias, ddt, da_log, dskip, dinner, doutw_out) = outs
    for given, out in ((mixed, mixed_out), (in_grad, grad_out), (dinw, dinw_out), (doutw, doutw_out)):
        out[...] = given[...]
    for i, line in enumerate((dgain, dbias, dinner, ddt, da_log, dskip)):
        line[...] = dvecs[i, 0 : line.shape[0]]
    conv_out[...] = dvecs[8:12, 0:26]


def emit(*given):
    vmem = pl.BlockSpec(memory_space=pltpu.VMEM)
    shape = jax.ShapeDtypeStruct
    line = [shape((n,), F32) for n in (KIN, 26, HEADS, HEADS, HEADS, KOUT)]
    return pl.pallas_call(
        emit_kernel,
        name="emit",
        out_shape=(*OUT_SHAPES[0:3], line[0], shape((4, 26), F32), *line[1:], OUT_SHAPES[4]),
        in_specs=[vmem] * 5,
        out_specs=(vmem,) * 11,
        compiler_params=pltpu.CompilerParams(vmem_limit_bytes=VMEM_LIMIT),
    )(*given)


def layer(*given):
    vmem, vm = pl.BlockSpec(memory_space=pltpu.VMEM), pltpu.VMEM

    def dma(*dims):
        return pltpu.SemaphoreType.DMA(dims)

    def plane_reduce(halves, rows, cols):
        block = (rows, cols)
        return [
            vm((halves, 3, 4) + block, BF16), vm((halves, 3) + block, BF16), vm((halves, 3) + block, BF16),
            vm((halves,) + block, F32),
        ]

    one, group = [dma(1)] * 2, [dma(2), dma(8)]
    group_reduce = [
        vm((4, SEQ, D), BF16), vm((3, SEQ, D), BF16), vm((2, SEQ // 2, D), BF16), vm((2, SEQ, D), BF16), vm((SEQ, D), F32)
    ]
    gather, two = [dma(2, 2), dma(2, 8)], [dma(2, 2)] * 2
    return pl.pallas_call(
        layer_kernel,
        name="layer",
        out_shape=OUT_SHAPES,
        in_specs=[vmem] * len(given),
        out_specs=(vmem,) * len(OUT_SHAPES),
        scratch_shapes=[
            vm((8, 128), F32), vm((8, 128), F32), vm((8, 128), F32),
            vm((GROUP, 16, COLS), BF16), vm((GROUP, 16, COLS), BF16), vm((2, 48, GA), BF16), vm((2, 48, GW), BF16),
            vm((32, 384), BF16), vm((2, 16, WIDE), BF16), vm((2, 16, WIDE), BF16), vm((SEQ, D), BF16),
            vm((4, 4, 2, 48, GA), BF16), vm((4, 4, 2, 48, GW), BF16), vm((4, 4, 1, 32, 384), BF16),
            vm((4, 4, 2, 16, WIDE), BF16), vm((4, 2, SEQ, D), BF16), vm((4, 2, SEQ, D), BF16),
            vm((ROWS, D), BF16), vm((ROWS, COLS + 128), F32), vm((2, ROWS, 128), F32), vm((128, D), BF16),
            vm((ROWS, 128), F32), vm((ROWS, 128), F32), vm((ROWS, GW), F32), vm((ROWS, CW), F32), vm((GROUP, SEQ, SEQ), F32),
            vm((ROWS, GW), F32), vm((ROWS, GW), F32), vm((GW, D), BF16),
            vm((8, D), F32), vm((8, 128), F32), vm((1, GW), F32),
            vm((16, SEQ), F32), vm((GROUP, 16, SEQ), F32), vm((SEQ, SEQ), F32),
            vm((ROWS, GW), BF16), vm((ROWS, COLS), BF16), vm((ROWS, 128), BF16),
            vm((ROWS, 128), F32), vm((ROWS, 128), F32), vm((ROWS, 128), F32),
            vm((4, 4, 2, 48, GA), BF16), vm((4, 4, 2, 48, GW), BF16), vm((4, 4, 2, 16, WIDE), BF16),
            vm((4, 4, 1, 16, 128), BF16), vm((8, CW), F32),
            *group_reduce, *group_reduce, *plane_reduce(2, 48, GA), *plane_reduce(2, 48, GW),
            *plane_reduce(2, 16, WIDE), *plane_reduce(1, 16, 128),
            vm((2, 16, WIDE), F32), vm((GROUP, 16, CW + 128), BF16), vm((GROUP, 16, CW + 128), BF16),
            vm((GROUP, 16, GW), BF16), vm((GROUP, 16, GW), BF16),
            vm((4, 8, CW), F32), vm((4, 8, CW), F32), vm((8, CW), F32), vm((GROUP, 8, CW), F32),
            *one, *gather, *gather, dma(1, 2), dma(1, 8), *gather, *group, *group, *one, dma(1), dma(4), dma(1), dma(4),
            *group, *group, *two, *two, *two, dma(1, 2), dma(1, 2), *one, *one, *one, *one, *one, dma(2), dma(2),
        ],
        compiler_params=pltpu.CompilerParams(collective_id=0, has_side_effects=True, vmem_limit_bytes=VMEM_LIMIT),
    )(*given)


OUT_SHAPES = (
    jax.ShapeDtypeStruct((SEQ, D), BF16),
    jax.ShapeDtypeStruct((SEQ, D), BF16),
    jax.ShapeDtypeStruct((KIN, STEP + HEADS), F32),
    jax.ShapeDtypeStruct((16, 128), F32),
    jax.ShapeDtypeStruct((KOUT, D), F32),
)


def body(
    hidden, in_weight, norm_gain, conv_weight, conv_bias, dt_bias, a_log, skip, inner_gain, out_weight, out_grad,
    seq_lengths, seq_owner,
):
    mixed, in_grad, dinw, dvecs, doutw = layer(
        hidden, in_weight, norm_gain, conv_weight.T, conv_bias, dt_bias, a_log, skip, inner_gain, out_weight, out_grad,
        seq_lengths, seq_owner,
    )
    outs = list(emit(mixed, in_grad, dinw, doutw, dvecs))
    outs[4] = outs[4].T
    return tuple(outs)


def solution(mesh):
    rows, line, whole = P("fsdp", None), P("fsdp"), P()
    return jax.shard_map(
        body,
        mesh=mesh,
        in_specs=(rows, rows, line, rows, line, whole, whole, whole, line, rows, rows, whole, whole),
        out_specs=(rows, rows, rows, line, rows, line, whole, whole, whole, line, rows),
        check_vma=False,
    )
```

```python
import functools

import jax
import jax.numpy as jnp
from jax import lax
from jax.experimental import pallas as pl
from jax.experimental.pallas import tpu as pltpu
from jax.sharding import PartitionSpec as P

MESH = pl.DeviceIdType.MESH
F32, BF16 = jnp.float32, jnp.bfloat16
HIGHEST = lax.Precision.HIGHEST
EPSILON = 1e-05

D = 1536
INNER = 3072
CONVD = 3328
HEADS = 48
SEQ = 128
GROUP = 8
ROWS = SEQ * GROUP
GW = INNER // GROUP
OWN = HEADS // GROUP
CW = GW + 128
GA, COLS = CW, CW + GW
ST = COLS
KIN = D // 128
KOUT = INNER // 128
STEP = 2 * INNER + 256
FOLD = D + D // 2
WIDE = FOLD // 2
VMEM_LIMIT = 60 * 2**20


def iota(shape, dim):
    return lax.broadcasted_iota(jnp.int32, shape, dim)


def ones(condition, kind=BF16):
    return jnp.where(condition, 1.0, 0.0).astype(kind)


def dot(a, b, precision=None):
    return lax.dot_general(a, b, (((1,), (0,)), ((), ())), precision=precision, preferred_element_type=F32)


def dot_nt(a, b, precision=None):
    return lax.dot_general(a, b, (((1,), (1,)), ((), ())), precision=precision, preferred_element_type=F32)


def dot_tn(a, b, precision=None):
    return lax.dot_general(a, b, (((0,), (0,)), ((), ())), precision=precision, preferred_element_type=F32)


def sigmoid(v):
    return 1.0 / (1.0 + jnp.exp(-v))


def softplus(v):
    return jnp.maximum(v, 0.0) + jnp.log1p(jnp.exp(-jnp.abs(v)))


def later(v, k):
    if k == 0:
        return v
    return jnp.where(iota(v.shape, 0) >= k, pltpu.roll(v, k, 0), 0.0)


def earlier(v, k):
    if k == 0:
        return v
    return jnp.where(iota(v.shape, 0) < v.shape[0] - k, pltpu.roll(v, v.shape[0] - k, 0), 0.0)


def place():
    me = lax.axis_index("fsdp")
    return me // 32, (me // 8) % 4, (me // 2) % 4, me % 2


def index(z, x, y, c):
    return ((z * 4 + x) * 4 + y) * 2 + c


def group_partner(k):
    z, x, y, c = place()
    rank = (y * 2 + c + k) % GROUP
    return index(z, x, rank // 2, rank % 2), rank


def on_z(k):
    z, x, y, c = place()
    return index((z + k) % 4, x, y, c)


def on_x(k):
    z, x, y, c = place()
    return index(z, (x + k) % 4, y, c)


def on_y(k):
    z, x, y, c = place()
    return index(z, x, (y + k) % 4, c)


def sibling():
    z, x, y, c = place()
    return index(z, x, y, 1 - c)


def swap_to():
    z, x, y, c = place()
    return index(y, x % 2 * 2 + c, z, x // 2)


def swap_from():
    z, x, y, c = place()
    return index(y, c * 2 + x // 2, z, x % 2)


def signal(target):
    pl.semaphore_signal(pltpu.get_barrier_semaphore(), inc=1, device_id=(target,), device_id_type=MESH)


def remote(src, dst, send, recv, target):
    return pltpu.make_async_remote_copy(
        src_ref=src, dst_ref=dst, send_sem=send, recv_sem=recv, device_id=(target,), device_id_type=MESH
    )


def plane_partners():
    return [on_z(k) for k in (1, 2, 3)] + [on_x(k) for k in (1, 2, 3)]


def group_partners():
    return [group_partner(k)[0] for k in range(1, GROUP)]


class PlaneGather:
    def __init__(self, buf, own, send, recv, halves):
        self.buf, self.own, self.send, self.recv, self.halves = buf, own, send, recv, halves
        self.z, self.x, _, _ = place()

    def slot(self, half, first, second):
        a, b = (first, second) if half == 0 else (second, first)
        return self.buf.at[(self.z + a) % 4, (self.x + b) % 4, half]

    def along(self, half, stage, k):
        return on_z(k) if (half == 0) == (stage == 0) else on_x(k)

    def came(self, first):
        return 3 if first < 2 else 1

    def mark(self, half, first, second):
        if second == 0:
            return self.recv.at[half, first - 1]
        return self.recv.at[half, 3 + first if second == self.came(first) else 7]

    def copy(self, half, first, stage, k):
        src = self.own(half) if first == 0 else self.slot(half, first, 0)
        at = (4 - k, 0) if stage == 0 else (first, 4 - k)
        return remote(
            src, self.slot(half, first, 0), self.send.at[half, stage], self.mark(half, *at), self.along(half, stage, k)
        )

    def relayed(self, half, first):
        came = self.came(first)
        here = self.slot(half, first, came)
        return remote(here, here, self.send.at[half, 1], self.mark(half, first, 2), self.along(half, 1, 4 - came))

    def arrival(self, half, first, second):
        here = self.slot(half, first, second)
        return remote(here, here, self.send.at[half, 0], self.mark(half, first, second), on_z(1))

    def some(self, rows, count, half):
        return self.buf.at[pl.ds(0, rows), pl.ds(0, count), half]

    def start(self):
        for k in (1, 3, 2):
            for half in range(self.halves):
                self.copy(half, 0, 0, k).start()
        for k in (1, 3):
            for half in range(self.halves):
                self.copy(half, 0, 1, k).start()

    def forward(self):
        for first in (1, 3, 2):
            for half in range(self.halves):
                self.arrival(half, first, 0).wait_recv()
                for k in (1, 3):
                    self.copy(half, first, 1, k).start()

    def relay(self):
        for first in (0, 3, 1, 2):
            for half in range(self.halves):
                self.arrival(half, first, self.came(first)).wait_recv()
                self.relayed(half, first).start()

    def finish(self):
        for half in range(self.halves):
            here = self.some(4, 2, half)
            remote(here, here, self.send.at[half, 0], self.recv.at[half, 7], on_z(1)).wait_recv()

    def sent(self):
        for half in range(self.halves):
            for stage, here in ((0, self.some(1, 3, half)), (1, self.some(4, 3, half))):
                remote(here, here, self.send.at[half, stage], self.recv.at[half, 7], on_z(1)).wait_send()


class GroupGather:
    def __init__(self, buf, own, send, recv):
        self.buf, self.own, self.send, self.recv = buf, own, send, recv
        _, _, self.y, self.c = place()

    def along(self, k):
        return remote(self.own, self.buf.at[self.y, self.c], self.send.at[0], self.recv.at[4 - k], on_y(k))

    def half(self, k):
        return pl.ds(0, SEQ // 2) if k == 3 else pl.ds(SEQ // 2, SEQ // 2)

    def relayed(self, k):
        here = self.buf.at[(self.y + k) % 4, self.c, self.half(k)]
        return remote(here, here, self.send.at[0], self.recv.at[2], on_y(4 - k))

    def across(self, k):
        src = self.own if k == 0 else self.buf.at[(self.y + k) % 4, self.c]
        dst = self.buf.at[(self.y + k) % 4, self.c]
        return remote(src, dst, self.send.at[1], self.recv.at[4 + k], sibling())

    def start(self):
        for k in (1, 3):
            self.along(k).start()
        self.across(0).start()

    def forward(self, k):
        here = self.buf.at[(self.y + k) % 4, self.c]
        remote(here, here, self.send.at[0], self.recv.at[k], sibling()).wait_recv()
        if k != 2:
            self.relayed(k).start()
        self.across(k).start()

    def arrived(self, k):
        here = self.buf.at[(self.y + k) % 4, 1 - self.c]
        remote(here, here, self.send.at[0], self.recv.at[4 + k], sibling()).wait_recv()

    def sent(self):
        for at, here in ((0, self.buf.at[pl.ds(0, 3), 0]), (1, self.buf.at[:, 0])):
            remote(here, here, self.send.at[at], self.recv.at[0], sibling()).wait_send()


def unpack_params(raw, rank, core, par, step_rows):
    row = iota((512, 1), 0)
    device = (row // 4).astype(F32)
    tap = row % 4
    values = raw[...].reshape(512, 384)

    def spots(span, first, count, channel):
        owner = jnp.floor((channel + 0.5) * (1.0 / count))
        lane = channel - owner * count + first
        pick = ones(iota((128, channel.shape[1]), 0).astype(F32) == lane)
        return jnp.where(device == owner, dot(values[:, span], pick), 0.0)

    def only(k, at):
        return jnp.sum(jnp.where(tap == k, at, 0.0), axis=0, keepdims=True)

    def lanes(n):
        return iota((1, n), 1).astype(F32)

    start = rank.astype(F32) * GW
    conv = lanes(CW)
    conv = jnp.where(conv < GW, conv + start, conv - GW + INNER + 128 * core.astype(F32))
    low, high, last = slice(0, 128), slice(128, 256), slice(256, 384)
    par[...] = jnp.zeros_like(par)
    par[0:1, :] = only(0, spots(high, 0, KIN, lanes(D)))
    taps = spots(low, 0, 26, conv)
    for k in range(4):
        par[k + 1 : k + 2, 0:CW] = only(k, taps)
    par[5:6, 0:CW] = only(0, spots(high, KIN, 26, conv))
    par[6:7, 0:GW] = only(0, spots(high, KIN + 26, KOUT, lanes(GW) + start))
    four, two = spots(last, 0, KIN, lanes(D)), spots(last, 16, KIN, lanes(D))
    rows = [only(k, four) for k in range(4)] + [only(k, two) for k in range(2)] + [jnp.zeros((122, D), F32)]
    step_rows[...] = jnp.concatenate(rows, axis=0).astype(BF16)


def own_heads(raw, rank, head, skip):
    row = iota((128, 128), 0)
    col = iota((128, 128), 1)
    given = raw[...]
    mine = dot(given, ones(jnp.logical_and(row == col + OWN * rank, col < OWN), F32), HIGHEST)
    head[...] = jnp.where(iota((8, 128), 0) == 1, -jnp.exp(mine), mine)
    wide = iota((128, GW), 0) == iota((128, GW), 1) // 64 + OWN * rank
    skip[...] = dot(given, ones(wide, F32), HIGHEST)[2:3]


def unfold_out_weight(raw, ow):
    row, col = iota((GW, 256), 0), iota((GW, 256), 1)
    device, line = row // KOUT, row % KOUT
    base = (device % 8 // 2 * 4 + device // 8 * 2 + device % 2) * 16
    top = ones(jnp.logical_and(line < 16, col == base + line))
    low_left = ones(jnp.logical_and(line >= 16, col == base + line - 16))
    low_right = ones(jnp.logical_and(line >= 16, col == base + line - 8))
    first = raw[:, :, 0].reshape(256, WIDE)
    second = raw[:, :, 1].reshape(256, WIDE)
    half, split = D // 2, WIDE - D // 2
    left, right_a = first[:, 0:half], first[:, half:]
    right_b, tail = second[:, 0 : half - split], second[:, half - split :]
    ow[:, 0:half] = (dot(top, left) + dot(low_left, tail)).astype(BF16)
    ow[:, half : half + split] = (dot(top, right_a) + dot(low_right, tail[:, 0:split])).astype(BF16)
    ow[:, half + split :] = (dot(top, right_b) + dot(low_right, tail[:, split:])).astype(BF16)


def convolve(raw, par, at, width):
    out = par[5:6, at : at + width] + raw * par[4:5, at : at + width]
    for k in range(3):
        out = out + later(raw, 3 - k) * par[k + 1 : k + 2, at : at + width]
    return out


def steps_forward(b, proj, head, steps, totals):
    rows = pl.ds(pl.multiple_of(b * SEQ, SEQ), SEQ)
    step = softplus(proj[rows, ST:] + head[0:1, :])
    lower = ones(iota((SEQ, SEQ), 0) >= iota((SEQ, SEQ), 1), F32)
    steps[rows, :] = step
    totals[rows, :] = dot(lower, head[1:2, :] * step, HIGHEST)


def activate(v, out, slope):
    s = sigmoid(v)
    out[...] = v * s
    slope[...] = s * (1.0 + v * (1.0 - s))


def mix_forward(b, proj, act, par, skip, steps, totals, values, slopes, scores, heads_out):
    row, col = iota((SEQ, SEQ), 0), iota((SEQ, SEQ), 1)
    causal = row >= col
    rows = pl.ds(pl.multiple_of(b * SEQ, SEQ), SEQ)
    total = totals[rows, :]
    total_t, step_t = total.T, steps[rows, :].T
    score = dot_nt(act[1, rows, :], act[0, rows, :], HIGHEST)
    scores[b] = score
    for p in range(3):
        span = slice(p * 128, p * 128 + 128)
        activate(convolve(proj[rows, span], par, p * 128, 128), values.at[rows, span], slopes.at[rows, span])
        value = values[rows, span]
        value_low = value.astype(BF16)
        parts = []
        for h in (2 * p, 2 * p + 1):
            decays = jnp.exp(jnp.where(causal, total[:, h : h + 1] - total_t[h : h + 1, :], -1e30))
            mix = (decays * score * step_t[h : h + 1, :]).astype(BF16)
            parts.append(dot(mix, value_low))
        heads_out[rows, span] = jnp.where(col < 64, parts[0], parts[1]) + skip[0:1, span] * value


def weigh(b, proj, par, heads_out, gated, acc):
    rows = pl.ds(pl.multiple_of(b * SEQ, SEQ), SEQ)
    gate = proj[rows, GA:COLS]
    product = heads_out[rows, :] * gate * sigmoid(gate)
    gated[rows, :] = (product * par[6:7, 0:GW]).astype(BF16)
    squares = jnp.sum(product * product, axis=1, keepdims=True)
    return jnp.where(iota((SEQ, SEQ), 1) == b, squares, acc)


def column(at, values):
    return jnp.sum(jnp.where(iota((SEQ, SEQ), 1) == at, values, 0.0), axis=1, keepdims=True)


def norm_sums(b, gated, dgated, acc):
    rows = pl.ds(pl.multiple_of(b * SEQ, SEQ), SEQ)
    crosses = jnp.sum(gated[rows, :].astype(F32) * dgated[rows, :], axis=1, keepdims=True)
    return jnp.where(iota((SEQ, SEQ), 1) == b + 8, crosses, acc)


def norm_back(b, proj, par, wide, heads_out, dgated, gated, dproj, small):
    rows = pl.ds(pl.multiple_of(b * SEQ, SEQ), SEQ)
    cross = column(b + 8, wide[...])
    inverse = lax.rsqrt(column(b, wide[...]) * (1.0 / INNER) + EPSILON)
    mean = cross * inverse * (1.0 / INNER)
    out = heads_out[rows, :]
    gate = proj[rows, GA:COLS]
    s = sigmoid(gate)
    silu = gate * s
    unit = out * silu * inverse
    dg = dgated[rows, :]
    gain = par[6:7, 0:GW]
    gated[rows, :] = (unit * gain).astype(BF16)
    small[5:6, 0:GW] += jnp.sum(dg * unit, axis=0, keepdims=True)
    d_product = (dg * gain - unit * mean) * inverse
    dproj[rows, GA:COLS] = (d_product * out * (s * (1.0 + gate * (1.0 - s)))).astype(BF16)
    dgated[rows, :] = d_product * silu


def conv_back(d_conv, raw, par, small, at):
    span = slice(at, at + 128)
    back = d_conv * par[4:5, span]
    small[3:4, span] += jnp.sum(d_conv * raw, axis=0, keepdims=True)
    for k in range(3):
        ahead = earlier(d_conv, 3 - k)
        back = back + ahead * par[k + 1 : k + 2, span]
        small[k : k + 1, span] += jnp.sum(ahead * raw, axis=0, keepdims=True)
    small[4:5, span] += jnp.sum(d_conv, axis=0, keepdims=True)
    return back


def mix_back(
    b, core, proj, act, par, head, skip, steps, totals, values, slopes, scores, d_heads, dproj, d_steps, small, d_mine,
    d_other,
):
    row, col = iota((SEQ, SEQ), 0), iota((SEQ, SEQ), 1)
    later_ok = col >= row
    left, right = col < 64, col >= 64
    suffix = ones(row >= col)
    before = row < col
    rows = pl.ds(pl.multiple_of(b * SEQ, SEQ), SEQ)
    step, total = steps[rows, :], totals[rows, :]
    total_t = total.T
    scores_t = scores[b].T
    d_scores = jnp.zeros((SEQ, SEQ), F32)
    direct = jnp.zeros((SEQ, SEQ), F32)
    lines = []
    for p in range(3):
        span = slice(p * 128, p * 128 + 128)
        d_out = d_heads[rows, span]
        value = values[rows, span]
        small[6:7, span] += jnp.sum(d_out * value, axis=0, keepdims=True)
        value_low = value.astype(BF16)
        d_low = d_out.astype(BF16)
        parts = []
        for i, h in enumerate((2 * p, 2 * p + 1)):
            decays = jnp.exp(jnp.where(later_ok, total_t[h : h + 1, :] - total[:, h : h + 1], -1e30))
            size = step[:, h : h + 1]
            own = jnp.where(left if i == 0 else right, d_out, 0.0).astype(BF16)
            d_mix = decays * dot_nt(value_low, own)
            d_scores = d_scores + d_mix * size
            per_step = (d_mix * scores_t).astype(BF16)
            tail = dot(per_step, suffix)
            direct = jnp.where(col == h, tail[:, 0:1], direct)
            lines.append(jnp.sum(jnp.where(before, tail * size, 0.0), axis=0, keepdims=True))
            mix = (decays * scores_t * size).astype(BF16)
            parts.append(dot(mix, d_low))
        d_values = jnp.where(left, parts[0], parts[1]) + skip[0:1, span] * d_out
        d_conv = d_values * slopes[rows, span]
        dproj[rows, span] = conv_back(d_conv, proj[rows, span], par, small, p * 128).astype(BF16)
    d_decay = jnp.concatenate(lines + [jnp.zeros((SEQ - OWN, SEQ), F32)], axis=0).T
    d_step = direct + head[1:2, :] * d_decay
    d_raw = d_step * sigmoid(proj[rows, ST:] + head[0:1, :])
    small[7:8, 0:128] += jnp.sum(d_raw, axis=0, keepdims=True)
    small[7:8, 128:256] += jnp.sum(d_decay * head[1:2, :] * step, axis=0, keepdims=True)
    d_low = d_scores.astype(BF16)
    d_write = dot(d_low, act[1, rows, :].astype(BF16))
    d_read = dot_tn(d_low, act[0, rows, :].astype(BF16))
    d_mine[rows, :] = jnp.where(core == 0, d_write, d_read)
    d_other[rows, :] = jnp.where(core == 0, d_read, d_write)
    d_steps[rows, :] = d_raw.astype(BF16)


def vector_forward(b, core, proj, act, slopes, par):
    rows = pl.ds(pl.multiple_of(b * SEQ, SEQ), SEQ)
    activate(convolve(proj[rows, GW:CW], par, GW, 128), act.at[core, rows, :], slopes.at[rows, GW:CW])


def vector_back(b, proj, par, slopes, d_mine, d_in, dproj, small):
    rows = pl.ds(pl.multiple_of(b * SEQ, SEQ), SEQ)
    d_conv = (d_mine[rows, :] + d_in[rows, :]) * slopes[rows, GW:CW]
    dproj[rows, GW:CW] = conv_back(d_conv, proj[rows, GW:CW], par, small, GW).astype(BF16)


class PlaneReduce:
    def __init__(self, terms, got, mid, last, out, send, recv, halves=2):
        self.terms, self.got, self.mid, self.last, self.out = terms, got, mid, last, out
        self.send, self.recv, self.halves = send, recv, halves
        self.z, self.x, _, _ = place()

    def line(self, half, k):
        return self.terms.at[:, (self.x + k) % 4, 0] if half == 0 else self.terms.at[(self.z + k) % 4, :, 1]

    def first(self, half, k):
        target = on_x(k) if half == 0 else on_z(k)
        return remote(self.line(half, k), self.got.at[half, k - 1], self.send.at[half, 0], self.recv.at[half, 0], target)

    def second(self, half, k):
        target = on_z(k) if half == 0 else on_x(k)
        return remote(self.mid.at[half, k - 1], self.last.at[half, k - 1], self.send.at[half, 1], self.recv.at[half, 1], target)

    def stage(self, half, at, like):
        return remote(like.at[half], like.at[half], self.send.at[half, at], self.recv.at[half, at], on_z(1))

    def start(self):
        for k in (2, 1, 3):
            for half in reversed(range(self.halves)):
                self.first(half, k).start()

    def middle(self):
        for half in reversed(range(self.halves)):
            self.stage(half, 0, self.got).wait_recv()
            for k in (2, 1, 3, 0):
                if half == 0:
                    at = (self.z + k) % 4
                    total = self.terms[at, self.x, 0].astype(F32)
                else:
                    at = (self.x + k) % 4
                    total = self.terms[self.z, at, 1].astype(F32)
                for j in range(3):
                    total = total + self.got[half, j, at].astype(F32)
                if k:
                    self.mid[half, k - 1] = total.astype(BF16)
                    self.second(half, k).start()
                else:
                    self.out[half] = total

    def end(self):
        for half in reversed(range(self.halves)):
            self.stage(half, 1, self.last).wait_recv()
            total = self.out[half]
            for j in range(3):
                total = total + self.last[half, j].astype(F32)
            self.out[half] = total

    def finish(self):
        for half in reversed(range(self.halves)):
            self.stage(half, 0, self.got).wait_send()
            self.stage(half, 1, self.mid).wait_send()


class GroupReduce:
    def __init__(self, terms, got, mid, relay, last, out, send, recv):
        self.terms, self.got, self.mid, self.relay, self.last, self.out = terms, got, mid, relay, last, out
        self.send, self.recv = send, recv
        _, _, self.y, self.c = place()

    def across(self, k):
        src = self.terms.at[(self.y + k) % 4, 1 - self.c]
        return remote(src, self.got.at[k], self.send.at[0], self.recv.at[k], sibling())

    def along(self, k):
        at = (k - 1) // 2
        return remote(self.mid.at[k - 1], self.last.at[at], self.send.at[1], self.recv.at[6], on_y(k))

    def far(self, at):
        src = self.mid.at[1, pl.ds(at * (SEQ // 2), SEQ // 2)]
        return remote(src, self.relay.at[at], self.send.at[1], self.recv.at[4 + at], on_y(3 if at else 1))

    def half(self, k):
        self.across(k).wait_recv()
        return self.terms[(self.y + k) % 4, self.c].astype(F32) + self.got[k].astype(F32)

    def pass_far(self):
        self.mid[1] = self.half(2).astype(BF16)
        for at in range(2):
            self.far(at).start()

    def pass_on(self, k):
        at = (k - 1) // 2
        total = self.half(k)
        self.far(at).wait_recv()
        came = self.relay[at].astype(F32)
        upper, lower = total[0 : SEQ // 2], total[SEQ // 2 :]
        if at == 0:
            upper = upper + came
        else:
            lower = lower + came
        self.mid[k - 1, 0 : SEQ // 2] = upper.astype(BF16)
        self.mid[k - 1, SEQ // 2 :] = lower.astype(BF16)
        self.along(k).start()

    def keep(self):
        self.out[...] = self.half(0)

    def end(self):
        total = self.out[...]
        remote(self.last, self.last, self.send.at[1], self.recv.at[6], sibling()).wait_recv()
        self.out[...] = total + self.last[0].astype(F32) + self.last[1].astype(F32)

    def finish(self):
        for at, here in ((0, self.got), (1, self.mid)):
            remote(here, here, self.send.at[at], self.recv.at[6], sibling()).wait_send()


class Members:
    def __init__(self, src, buf, send, recv):
        self.src, self.buf, self.send, self.recv = src, buf, send.at[0], recv.at[0]
        _, _, y, c = place()
        self.rank = y * 2 + c

    def start(self):
        for k in range(1, GROUP):
            target, q = group_partner(k)
            remote(self.src(q), self.buf.at[self.rank], self.send, self.recv, target).start()

    def others(self):
        here = self.buf.at[pl.ds(0, GROUP - 1)]
        return remote(here, here, self.send, self.recv, sibling())

    def finish(self):
        self.others().wait_recv()

    def sent(self):
        self.others().wait_send()


def layer_kernel(
    hid, inw, gain_in, taps, bias_in, dt_in, a_in, skip_in, inner_in, outw, grd, lengths, owners,
    mixed, in_grad, dinw, dvecs, doutw,
    vectors, heads_in, tap_rows,
    split, joined, block, gblock, params, outl, placed, live_grd,
    wx, wg, praw, plane, hall, gall, low, proj, act, step_rows, steps, totals, values, slopes, scores, heads_out, dgated, ow, par, head, skip, sums, slots, wide,
    gated, dproj, d_steps, d_mine, d_other, d_in, dwx, dwg, dow, dws, small,
    gb, mb, tb, lb, fb, gd, md, td, ld, fd, gx, mx, lx, fx, gg, mg, lg, fg, gl, ml, ll, fl, gs, ms, ls, fs,
    swapped, cut, rows_in, gcut, grows_in, zs, xs, part, small_all,
    a_s, a_r, wx_s, wx_r, wg_s, wg_r, p_s, p_r, l_s, l_r, h_s, h_r, g_s, g_r, n_s, n_r, v_s, v_r, u_s, u_r,
    b_s, b_r, d_s, d_r, rx_s, rx_r, rg_s, rg_r, rl_s, rl_r, rs_s, rs_r, rr_s, rr_r, rq_s, rq_r,
    sz_s, sz_r, sx_s, sx_r, sg_s, sg_r, swap_s, swap_r,
):
    z, x, y, c = place()
    rank = y * 2 + c
    me = lax.axis_index("fsdp")
    partners = plane_partners() + group_partners()
    moves = swap_to() != me
    for p in partners:
        signal(p)

    @pl.when(moves)
    def _():
        signal(swap_to())
        signal(swap_from())

    vectors[...] = jnp.zeros_like(vectors)
    heads_in[...] = jnp.zeros_like(heads_in)
    tap_rows[...] = jnp.zeros_like(tap_rows)
    vectors[0:1, 0:KIN] = gain_in[...].astype(F32)[None, :]
    vectors[0:1, KIN : KIN + 26] = bias_in[...].astype(F32)[None, :]
    vectors[0:1, KIN + 26 : KIN + 26 + KOUT] = inner_in[...].astype(F32)[None, :]
    for i, line in enumerate((dt_in, a_in, skip_in)):
        heads_in[i : i + 1, 0:HEADS] = line[...][None, :]
    tap_rows[0:4, 0:26] = taps[...].astype(F32)
    col_steps = inw[:, STEP : STEP + HEADS]
    steps_low = dot_tn(col_steps, ones(iota((KIN, 128), 0) == iota((KIN, 128), 1)))
    steps_high = dot_tn(col_steps, ones(iota((KIN, 128), 0) + 16 == iota((KIN, 128), 1)))
    rest = jnp.zeros((4, 128), F32)

    def padded(span, extra):
        return jnp.concatenate([inw[:, span].astype(F32), extra], axis=0).astype(BF16)

    vector_cols = [padded(slice(2 * INNER + 128 * i, 2 * INNER + 128 * (i + 1)), rest) for i in range(2)]
    for q in range(GROUP):
        at = q * OWN
        two = jnp.concatenate([steps_high[at + 4 : at + OWN], jnp.zeros((2, 128), F32)], axis=0)
        extra = jnp.concatenate([tap_rows[0:4], vectors[0:4], steps_low[at : at + 4] + two], axis=1)
        split[q, :, 0:GW] = padded(slice(INNER + q * GW, INNER + (q + 1) * GW), extra)
        split[q, :, GW:CW] = vector_cols[q % 2]
        split[q, :, GA:COLS] = padded(slice(q * GW, (q + 1) * GW), jnp.zeros((4, GW), F32))
    end = outw[16:24, :].astype(F32)
    tail = jnp.concatenate([end[:, 0 : D // 2], end[:, D // 2 :]], axis=0).astype(BF16)
    outl[0] = outw[0:16, 0:WIDE]
    outl[1, :, 0 : D - WIDE] = outw[0:16, WIDE:D]
    outl[1, :, D - WIDE :] = tail

    @pl.when(moves)
    def _():
        pl.semaphore_wait(pltpu.get_barrier_semaphore(), len(partners) + 2)

    @pl.when(jnp.logical_not(moves))
    def _():
        pl.semaphore_wait(pltpu.get_barrier_semaphore(), len(partners))

    cuts = Members(lambda q: split.at[q], joined, a_s, a_r)
    cuts.start()
    swap = remote(outl, placed, swap_s.at[0], swap_r.at[0], swap_to())
    swap_back = remote(fl, swapped, swap_s.at[1], swap_r.at[1], swap_from())

    @pl.when(moves)
    def _():
        swap.start()

    joined[rank] = split[rank]
    length = jnp.sum(jnp.where(owners[...][None, :] == me, lengths[...][None, :], 0), axis=1, keepdims=True)
    live = iota((SEQ, 1), 0) < length
    live_grd[...] = jnp.where(live, grd[...].astype(F32), 0.0).astype(BF16)
    own_heads(heads_in, rank, head, skip)

    hidden = GroupGather(hall, hid, h_s, h_r)
    grads = GroupGather(gall, live_grd, g_s, g_r)
    first_w = PlaneGather(wx, lambda h: block.at[h], wx_s, wx_r, 2)
    gate_w = PlaneGather(wg, lambda h: gblock.at[h], wg_s, wg_r, 2)
    vecs = PlaneGather(praw, lambda h: params, p_s, p_r, 1)
    lines = PlaneGather(plane, lambda h: placed.at[h], l_s, l_r, 2)

    hidden.start()
    cuts.finish()
    row, col = iota((128, 128), 0), iota((128, 128), 1)
    member, line = col // 16, col % 16
    spot = jnp.where(line < KIN, member * KIN + line, 96 + member * 4 + line - KIN)
    both = dot(ones(spot == row), joined[...].reshape(128, COLS)).astype(BF16)
    for h in range(2):
        block[h] = both[48 * h : 48 * h + 48, 0:GA]
        gblock[h] = both[48 * h : 48 * h + 48, GA:COLS]
    params[...] = both[96:128, 0:384]
    vecs.start()
    first_w.start()
    grads.start()
    wx[z, x] = block[...]
    wg[z, x] = gblock[...]
    praw[z, x, 0] = params[...]
    hall[y, c] = hid[...]
    gall[y, c] = live_grd[...]
    vecs.forward()
    first_w.forward()
    gate_w.start()

    @pl.when(moves)
    def _():
        swap.wait_recv()

    @pl.when(jnp.logical_not(moves))
    def _():
        placed[...] = outl[...]

    lines.start()
    plane[z, x] = placed[...]
    hidden.forward(1)
    hidden.forward(3)
    vecs.relay()
    first_w.relay()
    vecs.finish()
    unpack_params(praw, rank, c, par, step_rows)
    gate_w.forward()
    lines.forward()

    def chunk(i):
        return pl.ds(pl.multiple_of(i * 256, 256), 256)

    def turn(i):
        return i + i // 2 * (5 - 2 * i)

    def in_turn(i):
        return (y + turn(i)) % 4

    def vector_copy(i):
        here = act.at[c, chunk(in_turn(i))]
        return remote(here, here, v_s.at[0], v_r.at[i], sibling())

    def vector_arrival(i):
        here = act.at[1 - c, chunk(in_turn(i))]
        return remote(here, here, v_s.at[0], v_r.at[i], sibling())

    def prepare(at):
        for core in range(2):
            h = hall[at, core].astype(F32)
            scale = lax.rsqrt(jnp.mean(h * h, axis=1, keepdims=True) + EPSILON)
            rows = pl.ds(pl.multiple_of(at * 256 + core * SEQ, SEQ), SEQ)
            low[rows, :] = (h * scale * par[0:1, :]).astype(BF16)
        proj[chunk(at), ST:] = dot_nt(low[chunk(at), :], step_rows[...])
        for core in range(2):
            steps_forward(at * 2 + core, proj, head, steps, totals)

    def forward(i, carry):
        @pl.when(i == 1)
        def _():
            hidden.arrived(1)
            hidden.forward(2)

        @pl.when(i == 2)
        def _():
            hidden.arrived(3)
            gate_w.relay()

        @pl.when(i == 3)
        def _():
            hidden.arrived(2)
            lines.relay()
            grads.forward(1)
            grads.forward(3)

        @pl.when(jnp.logical_and(i > 0, i < 4))
        def _():
            prepare(in_turn(i))

        @pl.when(i < 4)
        def _():
            at = in_turn(i)
            rows = chunk(at)
            proj[rows, 0:GA] = dot(low[rows, :], wx[...].reshape(D, GA))
            for core in range(2):
                vector_forward(at * 2 + core, c, proj, act, slopes, par)
            vector_copy(i).start()

        @pl.when(i > 0)
        def _():
            vector_arrival(i - 1).wait_recv()
            at = in_turn(i - 1)
            for core in range(2):
                mix_forward(at * 2 + core, proj, act, par, skip, steps, totals, values, slopes, scores, heads_out)

        return carry

    hidden.arrived(0)
    prepare(y)
    first_w.finish()
    lax.fori_loop(0, 5, forward, 0)
    gate_w.finish()

    def project_gate(i, carry):
        proj[chunk(i), GA:COLS] = dot(low[chunk(i), :], wg[...].reshape(D, GW))
        return carry

    lax.fori_loop(0, ROWS // 256, project_gate, 0)

    def weighed(b, acc):
        return weigh(b, proj, par, heads_out, gated, acc)

    wide[...] = lax.fori_loop(0, GROUP, weighed, jnp.zeros((SEQ, SEQ), F32))
    lines.finish()
    unfold_out_weight(plane, ow)
    grads.forward(2)
    grads.arrived(0)

    def pull(i, carry):
        @pl.when(i == 1)
        def _():
            grads.arrived(1)

        @pl.when(i == 2)
        def _():
            grads.arrived(3)

        @pl.when(i == 3)
        def _():
            grads.arrived(2)

        at = in_turn(i)
        dgated[chunk(at), :] = dot_nt(gall[at].reshape(256, D), ow[...])
        return carry

    lax.fori_loop(0, 4, pull, 0)
    acc = lax.fori_loop(0, GROUP, lambda b, acc: norm_sums(b, gated, dgated, acc), wide[...])
    sums[...] = acc.T[0:16, :]
    norms = Members(lambda q: sums, slots, n_s, n_r)
    norms.start()
    slots[rank] = sums[...]
    small[...] = jnp.zeros_like(small)
    hidden.sent()
    branch = hall
    branches = GroupReduce(branch, gb, mb, tb, lb, fb, b_s, b_r)

    def out_term(i, carry):
        at = in_turn(3 - i)
        branch[at] = dot(gated[chunk(at), :], ow[...]).astype(BF16).reshape(2, SEQ, D)
        branches.across(turn(3 - i)).start()
        return carry

    lax.fori_loop(0, 4, out_term, 0)
    norms.finish()
    total = slots[0]
    for q in range(1, GROUP):
        total = total + slots[q]
    wide[...] = jnp.concatenate([total, jnp.zeros((SEQ - 16, SEQ), F32)], axis=0).T

    def norms_back(b, carry):
        norm_back(b, proj, par, wide, heads_out, dgated, gated, dproj, small)
        return carry

    branches.pass_far()
    lax.fori_loop(0, GROUP, norms_back, 0)

    d_low = gall
    lowers = GroupReduce(d_low, gd, md, td, ld, fd, d_s, d_r)
    sums_x = PlaneReduce(dwx, gx, mx, lx, fx, rx_s, rx_r)
    sums_g = PlaneReduce(dwg, gg, mg, lg, fg, rg_s, rg_r)
    sums_l = PlaneReduce(dow, gl, ml, ll, fl, rl_s, rl_r)
    sums_s = PlaneReduce(dws, gs, ms, ls, fs, rs_s, rs_r, 1)
    cut_rows = Members(lambda q: cut.at[q], rows_in, rr_s, rr_r)
    gate_rows = Members(lambda q: gcut.at[q], grows_in, rq_s, rq_r)
    all_small = Members(lambda q: small_all.at[rank], small_all, sg_s, sg_r)

    def small_z(k):
        return remote(small, zs.at[z], sz_s.at[0], sz_r.at[0], on_z(k))

    def small_x(k):
        return remote(part, xs.at[x], sx_s.at[0], sx_r.at[0], on_x(k))

    def small_all_of(buf, send, recv):
        here = buf.at[pl.ds(0, 3)]
        return remote(here, here, send.at[0], recv.at[0], on_z(1))

    def slab(k, span):
        at = (z + k) % 4
        own = low[:, pl.ds(pl.multiple_of(at * GW, GW), GW)]
        return at, dot_tn(own, dproj[:, span]).astype(BF16).reshape(4, 2, 48, span.stop - span.start)

    out = dot_tn(gated[...], gall[...].reshape(ROWS, D))
    for j in range(16):
        piece = out[j * KOUT : (j + 1) * KOUT]
        tail = jnp.concatenate([piece[16:24, 0 : D // 2], piece[16:24, D // 2 :]], axis=0)
        fold = jnp.concatenate([piece[0:16], tail], axis=1).astype(BF16)
        for h in range(2):
            dow[j % 8 // 2, j // 8 * 2 + j % 2, h] = fold[:, h * WIDE : (h + 1) * WIDE]
    sums_l.start()
    for k in (2, 1, 3, 0):
        at, rows = slab(k, slice(GA, COLS))
        dwg[at] = rows
        if k:
            sums_g.first(1, k).start()
    for k in (2, 1, 3):
        sums_g.first(0, k).start()
    grads.sent()

    def other_copy(i):
        rows = chunk(in_turn(3 - i))
        return remote(d_other.at[rows], d_in.at[rows], u_s.at[0], u_r.at[i], sibling())

    def lower_back(k):
        at = (y + k) % 4
        rows = chunk(at)
        back = dot_nt(dproj[rows, 0:GA], wx[...].reshape(D, GA))
        back = back + dot_nt(dproj[rows, GA:COLS], wg[...].reshape(D, GW))
        back = back + dot(d_steps[rows, :], step_rows[...])
        d_low[at] = back.astype(BF16).reshape(2, SEQ, D)
        lowers.across(k).start()

    def backward(i, carry):
        @pl.when(i < 4)
        def _():
            at = in_turn(3 - i)
            for core in range(2):
                mix_back(
                    at * 2 + core, c, proj, act, par, head, skip, steps, totals, values, slopes, scores, dgated, dproj,
                    d_steps, small, d_mine, d_other,
                )
            other_copy(i).start()

        @pl.when(i == 0)
        def _():
            branches.pass_on(3)
            branches.pass_on(1)
            branches.keep()

        @pl.when(i > 0)
        def _():
            other_copy(i - 1).wait_recv()
            at = in_turn(4 - i)
            for core in range(2):
                vector_back(at * 2 + core, proj, par, slopes, d_mine, d_in, dproj, small)

        @pl.when(i == 4)
        def _():
            sums_l.middle()

        @pl.when(i == 1)
        def _():
            lower_back(2)

        @pl.when(i == 3)
        def _():
            lowers.pass_far()

        return carry

    lax.fori_loop(0, 5, backward, 0)
    for k in (1, 2, 3):
        small_z(k).start()
    zs[z] = small[...]
    for k in (2, 1, 3, 0):
        at, rows = slab(k, slice(0, GA))
        dwx[at] = rows
        if k:
            sums_x.first(1, k).start()
    for k in (2, 1, 3):
        sums_x.first(0, k).start()
    sums_g.middle()
    steps_back = dot_tn(d_steps[...], low[...])
    for r in range(16):
        own = jnp.concatenate([steps_back[0:16, r * 96 : (r + 1) * 96], jnp.zeros((16, 32), F32)], axis=1)
        dws[r // 4, r % 4, 0] = own.astype(BF16)
    sums_s.start()

    def lower_backs(i, carry):
        lower_back(turn(2 - i))
        return carry

    lax.fori_loop(0, 3, lower_backs, 0)
    lowers.pass_on(3)
    lowers.pass_on(1)
    small_all_of(zs, sz_s, sz_r).wait_recv()
    part[...] = ((zs[0] + zs[1]) + zs[2]) + zs[3]
    xs[x] = part[...]
    for k in (1, 2, 3):
        small_x(k).start()
    sums_x.middle()
    sums_s.middle()
    lowers.keep()
    sums_g.end()
    for q in range(GROUP):
        gcut[q] = jnp.zeros((16, GW), BF16)
        gcut[q, 0:KIN, :] = fg[q // 4, q % 4 * KIN : (q % 4 + 1) * KIN, :].astype(BF16)
    gate_rows.start()
    grows_in[rank] = gcut[rank]
    sums_l.end()

    @pl.when(moves)
    def _():
        swap_back.start()

    small_all_of(xs, sx_s, sx_r).wait_recv()
    small_all[rank] = ((xs[0] + xs[1]) + xs[2]) + xs[3]
    all_small.start()
    branches.end()
    h32 = hid[...].astype(F32)
    inverse = lax.rsqrt(column(rank, wide[...]) * (1.0 / INNER) + EPSILON)
    mixed[...] = (h32 + jnp.where(live, inverse * fb[...], 0.0)).astype(BF16)
    sums_s.end()
    sums_x.end()
    step_cols = dot_tn(fs[0, 0:8], ones(iota((8, 128), 0) == iota((8, 128), 1), F32), HIGHEST)
    for q in range(GROUP):
        at = q % 4 * KIN
        cut[q] = jnp.zeros((16, CW + 128), BF16)
        cut[q, 0:KIN, 0:CW] = fx[q // 4, at : at + KIN, :].astype(BF16)
        cut[q, 0:KIN, CW:] = step_cols[q * KIN : (q + 1) * KIN].astype(BF16)
    cut_rows.start()
    rows_in[rank] = cut[rank]
    all_small.finish()
    finish_small(small_all, dvecs)

    @pl.when(moves)
    def _():
        swap_back.wait_recv()

    @pl.when(jnp.logical_not(moves))
    def _():
        swapped[...] = fl[...]

    doutw[0:16, 0:WIDE] = swapped[0]
    doutw[0:16, WIDE:D] = swapped[1, :, 0 : D - WIDE]
    doutw[16:24, 0 : D // 2] = swapped[1, 0:8, D - WIDE :]
    doutw[16:24, D // 2 : D] = swapped[1, 8:16, D - WIDE :]
    lowers.end()
    scale = lax.rsqrt(jnp.mean(h32 * h32, axis=1, keepdims=True) + EPSILON)
    normed = h32 * scale
    d_normed = fd[...] * par[0:1, :]
    through = scale * (d_normed - normed * jnp.mean(d_normed * normed, axis=1, keepdims=True))
    in_grad[...] = (grd[...].astype(F32) + through).astype(BF16)
    gate_rows.finish()
    gate_total = finish_gate(grows_in, inw, dinw)
    cut_rows.finish()
    finish_rows(rows_in, gate_total, inw, vectors, dinw, dvecs)
    for gone in (first_w, gate_w, vecs, lines, cuts, norms, cut_rows, gate_rows, all_small):
        gone.sent()
    for gone in (branches, lowers, sums_x, sums_g, sums_l, sums_s):
        gone.finish()
    small_all_of(zs, sz_s, sz_r).wait_send()
    small_all_of(xs, sx_s, sx_r).wait_send()
    remote(act.at[c], act.at[c], v_s.at[0], v_r.at[0], sibling()).wait_send()
    remote(d_other, d_other, u_s.at[0], u_r.at[0], sibling()).wait_send()

    @pl.when(moves)
    def _():
        swap.wait_send()
        swap_back.wait_send()


def finish_small(small, dvecs):
    me = lax.axis_index("fsdp")
    conv = jnp.zeros((8, 128), F32)
    inner = jnp.zeros((8, 128), F32)
    common = [jnp.zeros((8, 128), F32), jnp.zeros((8, 128), F32)]
    row, col = iota((GW, 128), 0), iota((GW, 128), 1)
    heads = ones(row // 64 == col, F32)
    dvecs[...] = jnp.zeros_like(dvecs)
    for q in range(GROUP):
        part = small[q, :, 0:GW]
        conv = conv + dot(part, ones(row + q * GW == col + 26 * me, F32), HIGHEST)
        inner = inner + dot(part, ones(row + q * GW == col + KOUT * me, F32), HIGHEST)
        common[q % 2] = common[q % 2] + small[q, :, GW:CW]
        span = slice(q * OWN, (q + 1) * OWN)
        dvecs[3:4, span] = small[q, 7:8, 0:OWN]
        dvecs[4:5, span] = small[q, 7:8, 128 : 128 + OWN]
        dvecs[5:6, span] = dot(part, heads, HIGHEST)[6:7, 0:OWN]
    row, col = iota((256, 128), 0), iota((256, 128), 1)
    conv = conv + dot(jnp.concatenate(common, axis=1), ones(row + INNER == col + 26 * me, F32), HIGHEST)
    dvecs[1:2] = conv[4:5]
    dvecs[2:3] = inner[5:6]
    dvecs[8:12] = conv[0:4]


def finish_gate(gate_rows, inw, dinw):
    for q in range(GROUP):
        dinw[:, q * GW : (q + 1) * GW] = gate_rows[q].astype(F32)[0:KIN]
    return jnp.sum(dinw[:, 0:INNER] * inw[:, 0:INNER].astype(F32), axis=1, keepdims=True)


def finish_rows(rows, gate_total, inw, vectors, dinw, dvecs):
    shared = [jnp.zeros((KIN, 128), F32), jnp.zeros((KIN, 128), F32)]
    for q in range(GROUP):
        own = rows[q].astype(F32)[0:KIN]
        dinw[:, INNER + q * GW : INNER + (q + 1) * GW] = own[:, 0:GW]
        dinw[:, STEP + q * OWN : STEP + (q + 1) * OWN] = own[:, CW : CW + OWN]
        shared[q % 2] = shared[q % 2] + own[:, GW:CW]
    dinw[:, 2 * INNER : 2 * INNER + 128] = shared[0]
    dinw[:, 2 * INNER + 128 : STEP] = shared[1]
    total = gate_total + jnp.sum(dinw[:, INNER:] * inw[:, INNER:].astype(F32), axis=1, keepdims=True)
    spread = jnp.where(iota((KIN, 128), 0) == iota((KIN, 128), 1), total, 0.0)
    gain = jnp.where(iota((1, 128), 1) < KIN, vectors[0:1], 1.0)
    dvecs[0:1] = jnp.sum(spread, axis=0, keepdims=True) / gain


def emit_kernel(mixed, in_grad, dinw, doutw, dvecs, *outs):
    (mixed_out, grad_out, dinw_out, dgain, conv_out, dbias, ddt, da_log, dskip, dinner, doutw_out) = outs
    for given, out in ((mixed, mixed_out), (in_grad, grad_out), (dinw, dinw_out), (doutw, doutw_out)):
        out[...] = given[...]
    for i, line in enumerate((dgain, dbias, dinner, ddt, da_log, dskip)):
        line[...] = dvecs[i, 0 : line.shape[0]]
    conv_out[...] = dvecs[8:12, 0:26]


def emit(*given):
    vmem = pl.BlockSpec(memory_space=pltpu.VMEM)
    shape = jax.ShapeDtypeStruct
    line = [shape((n,), F32) for n in (KIN, 26, HEADS, HEADS, HEADS, KOUT)]
    return pl.pallas_call(
        emit_kernel,
        name="emit",
        out_shape=(*OUT_SHAPES[0:3], line[0], shape((4, 26), F32), *line[1:], OUT_SHAPES[4]),
        in_specs=[vmem] * 5,
        out_specs=(vmem,) * 11,
        compiler_params=pltpu.CompilerParams(vmem_limit_bytes=VMEM_LIMIT),
    )(*given)


def layer(*given):
    vmem, vm = pl.BlockSpec(memory_space=pltpu.VMEM), pltpu.VMEM

    def dma(*dims):
        return pltpu.SemaphoreType.DMA(dims)

    def plane_reduce(halves, rows, cols):
        block = (rows, cols)
        return [
            vm((halves, 3, 4) + block, BF16), vm((halves, 3) + block, BF16), vm((halves, 3) + block, BF16),
            vm((halves,) + block, F32),
        ]

    one, group = [dma(1)] * 2, [dma(2), dma(8)]
    group_reduce = [
        vm((4, SEQ, D), BF16), vm((3, SEQ, D), BF16), vm((2, SEQ // 2, D), BF16), vm((2, SEQ, D), BF16), vm((SEQ, D), F32)
    ]
    gather, two = [dma(2, 2), dma(2, 8)], [dma(2, 2)] * 2
    return pl.pallas_call(
        layer_kernel,
        name="layer",
        out_shape=OUT_SHAPES,
        in_specs=[vmem] * len(given),
        out_specs=(vmem,) * len(OUT_SHAPES),
        scratch_shapes=[
            vm((8, 128), F32), vm((8, 128), F32), vm((8, 128), F32),
            vm((GROUP, 16, COLS), BF16), vm((GROUP, 16, COLS), BF16), vm((2, 48, GA), BF16), vm((2, 48, GW), BF16),
            vm((32, 384), BF16), vm((2, 16, WIDE), BF16), vm((2, 16, WIDE), BF16), vm((SEQ, D), BF16),
            vm((4, 4, 2, 48, GA), BF16), vm((4, 4, 2, 48, GW), BF16), vm((4, 4, 1, 32, 384), BF16),
            vm((4, 4, 2, 16, WIDE), BF16), vm((4, 2, SEQ, D), BF16), vm((4, 2, SEQ, D), BF16),
            vm((ROWS, D), BF16), vm((ROWS, COLS + 128), F32), vm((2, ROWS, 128), F32), vm((128, D), BF16),
            vm((ROWS, 128), F32), vm((ROWS, 128), F32), vm((ROWS, GW), F32), vm((ROWS, CW), F32), vm((GROUP, SEQ, SEQ), F32),
            vm((ROWS, GW), F32), vm((ROWS, GW), F32), vm((GW, D), BF16),
            vm((8, D), F32), vm((8, 128), F32), vm((1, GW), F32),
            vm((16, SEQ), F32), vm((GROUP, 16, SEQ), F32), vm((SEQ, SEQ), F32),
            vm((ROWS, GW), BF16), vm((ROWS, COLS), BF16), vm((ROWS, 128), BF16),
            vm((ROWS, 128), F32), vm((ROWS, 128), F32), vm((ROWS, 128), F32),
            vm((4, 4, 2, 48, GA), BF16), vm((4, 4, 2, 48, GW), BF16), vm((4, 4, 2, 16, WIDE), BF16),
            vm((4, 4, 1, 16, 128), BF16), vm((8, CW), F32),
            *group_reduce, *group_reduce, *plane_reduce(2, 48, GA), *plane_reduce(2, 48, GW),
            *plane_reduce(2, 16, WIDE), *plane_reduce(1, 16, 128),
            vm((2, 16, WIDE), F32), vm((GROUP, 16, CW + 128), BF16), vm((GROUP, 16, CW + 128), BF16),
            vm((GROUP, 16, GW), BF16), vm((GROUP, 16, GW), BF16),
            vm((4, 8, CW), F32), vm((4, 8, CW), F32), vm((8, CW), F32), vm((GROUP, 8, CW), F32),
            *one, *gather, *gather, dma(1, 2), dma(1, 8), *gather, *group, *group, *one, dma(1), dma(4), dma(1), dma(4),
            *group, *group, *two, *two, *two, dma(1, 2), dma(1, 2), *one, *one, *one, *one, *one, dma(2), dma(2),
        ],
        compiler_params=pltpu.CompilerParams(collective_id=0, has_side_effects=True, vmem_limit_bytes=VMEM_LIMIT),
    )(*given)


OUT_SHAPES = (
    jax.ShapeDtypeStruct((SEQ, D), BF16),
    jax.ShapeDtypeStruct((SEQ, D), BF16),
    jax.ShapeDtypeStruct((KIN, STEP + HEADS), F32),
    jax.ShapeDtypeStruct((16, 128), F32),
    jax.ShapeDtypeStruct((KOUT, D), F32),
)


def body(
    hidden, in_weight, norm_gain, conv_weight, conv_bias, dt_bias, a_log, skip, inner_gain, out_weight, out_grad,
    seq_lengths, seq_owner,
):
    mixed, in_grad, dinw, dvecs, doutw = layer(
        hidden, in_weight, norm_gain, conv_weight.T, conv_bias, dt_bias, a_log, skip, inner_gain, out_weight, out_grad,
        seq_lengths, seq_owner,
    )
    outs = list(emit(mixed, in_grad, dinw, doutw, dvecs))
    outs[4] = outs[4].T
    return tuple(outs)


def solution(mesh):
    rows, line, whole = P("fsdp", None), P("fsdp"), P()
    return jax.shard_map(
        body,
        mesh=mesh,
        in_specs=(rows, rows, line, rows, line, whole, whole, whole, line, rows, rows, whole, whole),
        out_specs=(rows, rows, rows, line, rows, line, whole, whole, whole, line, rows),
        check_vma=False,
    )
```

```python
import functools

import jax
import jax.numpy as jnp
from jax import lax
from jax.experimental import pallas as pl
from jax.experimental.pallas import tpu as pltpu
from jax.sharding import PartitionSpec as P

MESH = pl.DeviceIdType.MESH
F32, BF16 = jnp.float32, jnp.bfloat16
HIGHEST = lax.Precision.HIGHEST
EPSILON = 1e-05

D = 1536
INNER = 3072
CONVD = 3328
HEADS = 48
SEQ = 128
GROUP = 8
ROWS = SEQ * GROUP
GW = INNER // GROUP
OWN = HEADS // GROUP
CW = GW + 128
GA, COLS = CW, CW + GW
ST = COLS
KIN = D // 128
KOUT = INNER // 128
STEP = 2 * INNER + 256
FOLD = D + D // 2
WIDE = FOLD // 2
VMEM_LIMIT = 60 * 2**20


def iota(shape, dim):
    return lax.broadcasted_iota(jnp.int32, shape, dim)


def ones(condition, kind=BF16):
    return jnp.where(condition, 1.0, 0.0).astype(kind)


def dot(a, b, precision=None):
    return lax.dot_general(a, b, (((1,), (0,)), ((), ())), precision=precision, preferred_element_type=F32)


def dot_nt(a, b, precision=None):
    return lax.dot_general(a, b, (((1,), (1,)), ((), ())), precision=precision, preferred_element_type=F32)


def dot_tn(a, b, precision=None):
    return lax.dot_general(a, b, (((0,), (0,)), ((), ())), precision=precision, preferred_element_type=F32)


def sigmoid(v):
    return 1.0 / (1.0 + jnp.exp(-v))


def softplus(v):
    return jnp.maximum(v, 0.0) + jnp.log1p(jnp.exp(-jnp.abs(v)))


def later(v, k):
    if k == 0:
        return v
    return jnp.where(iota(v.shape, 0) >= k, pltpu.roll(v, k, 0), 0.0)


def earlier(v, k):
    if k == 0:
        return v
    return jnp.where(iota(v.shape, 0) < v.shape[0] - k, pltpu.roll(v, v.shape[0] - k, 0), 0.0)


def place():
    me = lax.axis_index("fsdp")
    return me // 32, (me // 8) % 4, (me // 2) % 4, me % 2


def index(z, x, y, c):
    return ((z * 4 + x) * 4 + y) * 2 + c


def group_partner(k):
    z, x, y, c = place()
    rank = (y * 2 + c + k) % GROUP
    return index(z, x, rank // 2, rank % 2), rank


def on_z(k):
    z, x, y, c = place()
    return index((z + k) % 4, x, y, c)


def on_x(k):
    z, x, y, c = place()
    return index(z, (x + k) % 4, y, c)


def on_y(k):
    z, x, y, c = place()
    return index(z, x, (y + k) % 4, c)


def sibling():
    z, x, y, c = place()
    return index(z, x, y, 1 - c)


def swap_to():
    z, x, y, c = place()
    return index(y, x % 2 * 2 + c, z, x // 2)


def swap_from():
    z, x, y, c = place()
    return index(y, c * 2 + x // 2, z, x % 2)


def signal(target):
    pl.semaphore_signal(pltpu.get_barrier_semaphore(), inc=1, device_id=(target,), device_id_type=MESH)


def remote(src, dst, send, recv, target):
    return pltpu.make_async_remote_copy(
        src_ref=src, dst_ref=dst, send_sem=send, recv_sem=recv, device_id=(target,), device_id_type=MESH
    )


def plane_partners():
    return [on_z(k) for k in (1, 2, 3)] + [on_x(k) for k in (1, 2, 3)]


def group_partners():
    return [group_partner(k)[0] for k in range(1, GROUP)]


class PlaneGather:
    def __init__(self, buf, own, send, recv, halves):
        self.buf, self.own, self.send, self.recv, self.halves = buf, own, send, recv, halves
        self.z, self.x, _, _ = place()

    def slot(self, half, first, second):
        a, b = (first, second) if half == 0 else (second, first)
        return self.buf.at[(self.z + a) % 4, (self.x + b) % 4, half]

    def along(self, half, stage, k):
        return on_z(k) if (half == 0) == (stage == 0) else on_x(k)

    def came(self, first):
        return 3 if first < 2 else 1

    def mark(self, half, first, second):
        if second == 0:
            return self.recv.at[half, first - 1]
        return self.recv.at[half, 3 + first if second == self.came(first) else 7]

    def copy(self, half, first, stage, k):
        src = self.own(half) if first == 0 else self.slot(half, first, 0)
        at = (4 - k, 0) if stage == 0 else (first, 4 - k)
        return remote(
            src, self.slot(half, first, 0), self.send.at[half, stage], self.mark(half, *at), self.along(half, stage, k)
        )

    def relayed(self, half, first):
        came = self.came(first)
        here = self.slot(half, first, came)
        return remote(here, here, self.send.at[half, 1], self.mark(half, first, 2), self.along(half, 1, 4 - came))

    def arrival(self, half, first, second):
        here = self.slot(half, first, second)
        return remote(here, here, self.send.at[half, 0], self.mark(half, first, second), on_z(1))

    def some(self, rows, count, half):
        return self.buf.at[pl.ds(0, rows), pl.ds(0, count), half]

    def start(self):
        for k in (1, 3, 2):
            for half in range(self.halves):
                self.copy(half, 0, 0, k).start()
        for k in (1, 3):
            for half in range(self.halves):
                self.copy(half, 0, 1, k).start()

    def forward(self):
        for first in (1, 3, 2):
            for half in range(self.halves):
                self.arrival(half, first, 0).wait_recv()
                for k in (1, 3):
                    self.copy(half, first, 1, k).start()

    def relay(self):
        for first in (0, 3, 1, 2):
            for half in range(self.halves):
                self.arrival(half, first, self.came(first)).wait_recv()
                self.relayed(half, first).start()

    def finish(self):
        for half in range(self.halves):
            here = self.some(4, 2, half)
            remote(here, here, self.send.at[half, 0], self.recv.at[half, 7], on_z(1)).wait_recv()

    def sent(self):
        for half in range(self.halves):
            for stage, here in ((0, self.some(1, 3, half)), (1, self.some(4, 3, half))):
                remote(here, here, self.send.at[half, stage], self.recv.at[half, 7], on_z(1)).wait_send()


class GroupGather:
    def __init__(self, buf, own, send, recv):
        self.buf, self.own, self.send, self.recv = buf, own, send, recv
        _, _, self.y, self.c = place()

    def along(self, k):
        return remote(self.own, self.buf.at[self.y, self.c], self.send.at[0], self.recv.at[4 - k], on_y(k))

    def half(self, k):
        return pl.ds(0, SEQ // 2) if k == 3 else pl.ds(SEQ // 2, SEQ // 2)

    def relayed(self, k):
        here = self.buf.at[(self.y + k) % 4, self.c, self.half(k)]
        return remote(here, here, self.send.at[0], self.recv.at[2], on_y(4 - k))

    def across(self, k):
        src = self.own if k == 0 else self.buf.at[(self.y + k) % 4, self.c]
        dst = self.buf.at[(self.y + k) % 4, self.c]
        return remote(src, dst, self.send.at[1], self.recv.at[4 + k], sibling())

    def start(self):
        for k in (1, 3):
            self.along(k).start()
        self.across(0).start()

    def forward(self, k):
        here = self.buf.at[(self.y + k) % 4, self.c]
        remote(here, here, self.send.at[0], self.recv.at[k], sibling()).wait_recv()
        if k != 2:
            self.relayed(k).start()
        self.across(k).start()

    def arrived(self, k):
        here = self.buf.at[(self.y + k) % 4, 1 - self.c]
        remote(here, here, self.send.at[0], self.recv.at[4 + k], sibling()).wait_recv()

    def sent(self):
        for at, here in ((0, self.buf.at[pl.ds(0, 3), 0]), (1, self.buf.at[:, 0])):
            remote(here, here, self.send.at[at], self.recv.at[0], sibling()).wait_send()


def unpack_params(raw, rank, core, par, step_rows):
    row = iota((512, 1), 0)
    device = (row // 4).astype(F32)
    tap = row % 4
    values = raw[...].reshape(512, 384)

    def spots(span, first, count, channel):
        owner = jnp.floor((channel + 0.5) * (1.0 / count))
        lane = channel - owner * count + first
        pick = ones(iota((128, channel.shape[1]), 0).astype(F32) == lane)
        return jnp.where(device == owner, dot(values[:, span], pick), 0.0)

    def only(k, at):
        return jnp.sum(jnp.where(tap == k, at, 0.0), axis=0, keepdims=True)

    def lanes(n):
        return iota((1, n), 1).astype(F32)

    start = rank.astype(F32) * GW
    conv = lanes(CW)
    conv = jnp.where(conv < GW, conv + start, conv - GW + INNER + 128 * core.astype(F32))
    low, high, last = slice(0, 128), slice(128, 256), slice(256, 384)
    par[...] = jnp.zeros_like(par)
    par[0:1, :] = only(0, spots(high, 0, KIN, lanes(D)))
    taps = spots(low, 0, 26, conv)
    for k in range(4):
        par[k + 1 : k + 2, 0:CW] = only(k, taps)
    par[5:6, 0:CW] = only(0, spots(high, KIN, 26, conv))
    par[6:7, 0:GW] = only(0, spots(high, KIN + 26, KOUT, lanes(GW) + start))
    four, two = spots(last, 0, KIN, lanes(D)), spots(last, 16, KIN, lanes(D))
    rows = [only(k, four) for k in range(4)] + [only(k, two) for k in range(2)] + [jnp.zeros((122, D), F32)]
    step_rows[...] = jnp.concatenate(rows, axis=0).astype(BF16)


def own_heads(raw, rank, head, skip):
    row = iota((128, 128), 0)
    col = iota((128, 128), 1)
    given = raw[...]
    mine = dot(given, ones(jnp.logical_and(row == col + OWN * rank, col < OWN), F32), HIGHEST)
    head[...] = jnp.where(iota((8, 128), 0) == 1, -jnp.exp(mine), mine)
    wide = iota((128, GW), 0) == iota((128, GW), 1) // 64 + OWN * rank
    skip[...] = dot(given, ones(wide, F32), HIGHEST)[2:3]


def unfold_out_weight(raw, ow):
    row, col = iota((GW, 256), 0), iota((GW, 256), 1)
    device, line = row // KOUT, row % KOUT
    base = (device % 8 // 2 * 4 + device // 8 * 2 + device % 2) * 16
    top = ones(jnp.logical_and(line < 16, col == base + line))
    low_left = ones(jnp.logical_and(line >= 16, col == base + line - 16))
    low_right = ones(jnp.logical_and(line >= 16, col == base + line - 8))
    first = raw[:, :, 0].reshape(256, WIDE)
    second = raw[:, :, 1].reshape(256, WIDE)
    half, split = D // 2, WIDE - D // 2
    left, right_a = first[:, 0:half], first[:, half:]
    right_b, tail = second[:, 0 : half - split], second[:, half - split :]
    ow[:, 0:half] = (dot(top, left) + dot(low_left, tail)).astype(BF16)
    ow[:, half : half + split] = (dot(top, right_a) + dot(low_right, tail[:, 0:split])).astype(BF16)
    ow[:, half + split :] = (dot(top, right_b) + dot(low_right, tail[:, split:])).astype(BF16)


def convolve(raw, par, at, width):
    out = par[5:6, at : at + width] + raw * par[4:5, at : at + width]
    for k in range(3):
        out = out + later(raw, 3 - k) * par[k + 1 : k + 2, at : at + width]
    return out


def steps_forward(b, proj, head, steps, totals):
    rows = pl.ds(pl.multiple_of(b * SEQ, SEQ), SEQ)
    step = softplus(proj[rows, ST:] + head[0:1, :])
    lower = ones(iota((SEQ, SEQ), 0) >= iota((SEQ, SEQ), 1), F32)
    steps[rows, :] = step
    totals[rows, :] = dot(lower, head[1:2, :] * step, HIGHEST)


def activate(v, out, slope):
    s = sigmoid(v)
    out[...] = v * s
    slope[...] = s * (1.0 + v * (1.0 - s))


def mix_forward(b, proj, act, par, skip, steps, totals, values, slopes, scores, heads_out):
    row, col = iota((SEQ, SEQ), 0), iota((SEQ, SEQ), 1)
    causal = row >= col
    rows = pl.ds(pl.multiple_of(b * SEQ, SEQ), SEQ)
    total = totals[rows, :]
    total_t, step_t = total.T, steps[rows, :].T
    score = dot_nt(act[1, rows, :], act[0, rows, :], HIGHEST)
    scores[b] = score
    for p in range(3):
        span = slice(p * 128, p * 128 + 128)
        activate(convolve(proj[rows, span], par, p * 128, 128), values.at[rows, span], slopes.at[rows, span])
        value = values[rows, span]
        value_low = value.astype(BF16)
        parts = []
        for h in (2 * p, 2 * p + 1):
            decays = jnp.exp(jnp.where(causal, total[:, h : h + 1] - total_t[h : h + 1, :], -1e30))
            mix = (decays * score * step_t[h : h + 1, :]).astype(BF16)
            parts.append(dot(mix, value_low))
        heads_out[rows, span] = jnp.where(col < 64, parts[0], parts[1]) + skip[0:1, span] * value


def weigh(b, proj, par, heads_out, gated, acc):
    rows = pl.ds(pl.multiple_of(b * SEQ, SEQ), SEQ)
    gate = proj[rows, GA:COLS]
    product = heads_out[rows, :] * gate * sigmoid(gate)
    gated[rows, :] = (product * par[6:7, 0:GW]).astype(BF16)
    squares = jnp.sum(product * product, axis=1, keepdims=True)
    return jnp.where(iota((SEQ, SEQ), 1) == b, squares, acc)


def column(at, values):
    return jnp.sum(jnp.where(iota((SEQ, SEQ), 1) == at, values, 0.0), axis=1, keepdims=True)


def norm_sums(b, gated, dgated, acc):
    rows = pl.ds(pl.multiple_of(b * SEQ, SEQ), SEQ)
    crosses = jnp.sum(gated[rows, :].astype(F32) * dgated[rows, :], axis=1, keepdims=True)
    return jnp.where(iota((SEQ, SEQ), 1) == b + 8, crosses, acc)


def norm_back(b, proj, par, wide, heads_out, dgated, gated, dproj, small):
    rows = pl.ds(pl.multiple_of(b * SEQ, SEQ), SEQ)
    cross = column(b + 8, wide[...])
    inverse = lax.rsqrt(column(b, wide[...]) * (1.0 / INNER) + EPSILON)
    mean = cross * inverse * (1.0 / INNER)
    out = heads_out[rows, :]
    gate = proj[rows, GA:COLS]
    s = sigmoid(gate)
    silu = gate * s
    unit = out * silu * inverse
    dg = dgated[rows, :]
    gain = par[6:7, 0:GW]
    gated[rows, :] = (unit * gain).astype(BF16)
    small[5:6, 0:GW] += jnp.sum(dg * unit, axis=0, keepdims=True)
    d_product = (dg * gain - unit * mean) * inverse
    dproj[rows, GA:COLS] = (d_product * out * (s * (1.0 + gate * (1.0 - s)))).astype(BF16)
    dgated[rows, :] = d_product * silu


def conv_back(d_conv, raw, par, small, at):
    span = slice(at, at + 128)
    back = d_conv * par[4:5, span]
    small[3:4, span] += jnp.sum(d_conv * raw, axis=0, keepdims=True)
    for k in range(3):
        ahead = earlier(d_conv, 3 - k)
        back = back + ahead * par[k + 1 : k + 2, span]
        small[k : k + 1, span] += jnp.sum(ahead * raw, axis=0, keepdims=True)
    small[4:5, span] += jnp.sum(d_conv, axis=0, keepdims=True)
    return back


def mix_back(
    b, core, proj, act, par, head, skip, steps, totals, values, slopes, scores, d_heads, dproj, d_steps, small, d_mine,
    d_other,
):
    row, col = iota((SEQ, SEQ), 0), iota((SEQ, SEQ), 1)
    later_ok = col >= row
    left, right = col < 64, col >= 64
    suffix = ones(row >= col)
    before = row < col
    rows = pl.ds(pl.multiple_of(b * SEQ, SEQ), SEQ)
    step, total = steps[rows, :], totals[rows, :]
    total_t = total.T
    scores_t = scores[b].T
    d_scores = jnp.zeros((SEQ, SEQ), F32)
    direct = jnp.zeros((SEQ, SEQ), F32)
    lines = []
    for p in range(3):
        span = slice(p * 128, p * 128 + 128)
        d_out = d_heads[rows, span]
        value = values[rows, span]
        small[6:7, span] += jnp.sum(d_out * value, axis=0, keepdims=True)
        value_low = value.astype(BF16)
        d_low = d_out.astype(BF16)
        parts = []
        for i, h in enumerate((2 * p, 2 * p + 1)):
            decays = jnp.exp(jnp.where(later_ok, total_t[h : h + 1, :] - total[:, h : h + 1], -1e30))
            size = step[:, h : h + 1]
            own = jnp.where(left if i == 0 else right, d_out, 0.0).astype(BF16)
            d_mix = decays * dot_nt(value_low, own)
            d_scores = d_scores + d_mix * size
            per_step = (d_mix * scores_t).astype(BF16)
            tail = dot(per_step, suffix)
            direct = jnp.where(col == h, tail[:, 0:1], direct)
            lines.append(jnp.sum(jnp.where(before, tail * size, 0.0), axis=0, keepdims=True))
            mix = (decays * scores_t * size).astype(BF16)
            parts.append(dot(mix, d_low))
        d_values = jnp.where(left, parts[0], parts[1]) + skip[0:1, span] * d_out
        d_conv = d_values * slopes[rows, span]
        dproj[rows, span] = conv_back(d_conv, proj[rows, span], par, small, p * 128).astype(BF16)
    d_decay = jnp.concatenate(lines + [jnp.zeros((SEQ - OWN, SEQ), F32)], axis=0).T
    d_step = direct + head[1:2, :] * d_decay
    d_raw = d_step * sigmoid(proj[rows, ST:] + head[0:1, :])
    small[7:8, 0:128] += jnp.sum(d_raw, axis=0, keepdims=True)
    small[7:8, 128:256] += jnp.sum(d_decay * head[1:2, :] * step, axis=0, keepdims=True)
    d_low = d_scores.astype(BF16)
    d_write = dot(d_low, act[1, rows, :].astype(BF16))
    d_read = dot_tn(d_low, act[0, rows, :].astype(BF16))
    d_mine[rows, :] = jnp.where(core == 0, d_write, d_read)
    d_other[rows, :] = jnp.where(core == 0, d_read, d_write)
    d_steps[rows, :] = d_raw.astype(BF16)


def vector_forward(b, core, proj, act, slopes, par):
    rows = pl.ds(pl.multiple_of(b * SEQ, SEQ), SEQ)
    activate(convolve(proj[rows, GW:CW], par, GW, 128), act.at[core, rows, :], slopes.at[rows, GW:CW])


def vector_back(b, proj, par, slopes, d_mine, d_in, dproj, small):
    rows = pl.ds(pl.multiple_of(b * SEQ, SEQ), SEQ)
    d_conv = (d_mine[rows, :] + d_in[rows, :]) * slopes[rows, GW:CW]
    dproj[rows, GW:CW] = conv_back(d_conv, proj[rows, GW:CW], par, small, GW).astype(BF16)


class PlaneReduce:
    def __init__(self, terms, got, mid, last, out, send, recv, halves=2):
        self.terms, self.got, self.mid, self.last, self.out = terms, got, mid, last, out
        self.send, self.recv, self.halves = send, recv, halves
        self.z, self.x, _, _ = place()

    def line(self, half, k):
        return self.terms.at[:, (self.x + k) % 4, 0] if half == 0 else self.terms.at[(self.z + k) % 4, :, 1]

    def first(self, half, k):
        target = on_x(k) if half == 0 else on_z(k)
        return remote(self.line(half, k), self.got.at[half, k - 1], self.send.at[half, 0], self.recv.at[half, 0], target)

    def second(self, half, k):
        target = on_z(k) if half == 0 else on_x(k)
        return remote(self.mid.at[half, k - 1], self.last.at[half, k - 1], self.send.at[half, 1], self.recv.at[half, 1], target)

    def stage(self, half, at, like):
        return remote(like.at[half], like.at[half], self.send.at[half, at], self.recv.at[half, at], on_z(1))

    def start(self):
        for k in (2, 1, 3):
            for half in reversed(range(self.halves)):
                self.first(half, k).start()

    def middle(self):
        for half in reversed(range(self.halves)):
            self.stage(half, 0, self.got).wait_recv()
            for k in (2, 1, 3, 0):
                if half == 0:
                    at = (self.z + k) % 4
                    total = self.terms[at, self.x, 0].astype(F32)
                else:
                    at = (self.x + k) % 4
                    total = self.terms[self.z, at, 1].astype(F32)
                for j in range(3):
                    total = total + self.got[half, j, at].astype(F32)
                if k:
                    self.mid[half, k - 1] = total.astype(BF16)
                    self.second(half, k).start()
                else:
                    self.out[half] = total

    def end(self):
        for half in reversed(range(self.halves)):
            self.stage(half, 1, self.last).wait_recv()
            total = self.out[half]
            for j in range(3):
                total = total + self.last[half, j].astype(F32)
            self.out[half] = total

    def finish(self):
        for half in reversed(range(self.halves)):
            self.stage(half, 0, self.got).wait_send()
            self.stage(half, 1, self.mid).wait_send()


class GroupReduce:
    def __init__(self, terms, got, mid, relay, last, out, send, recv):
        self.terms, self.got, self.mid, self.relay, self.last, self.out = terms, got, mid, relay, last, out
        self.send, self.recv = send, recv
        _, _, self.y, self.c = place()

    def across(self, k):
        src = self.terms.at[(self.y + k) % 4, 1 - self.c]
        return remote(src, self.got.at[k], self.send.at[0], self.recv.at[k], sibling())

    def along(self, k):
        at = (k - 1) // 2
        return remote(self.mid.at[k - 1], self.last.at[at], self.send.at[1], self.recv.at[6], on_y(k))

    def far(self, at):
        src = self.mid.at[1, pl.ds(at * (SEQ // 2), SEQ // 2)]
        return remote(src, self.relay.at[at], self.send.at[1], self.recv.at[4 + at], on_y(3 if at else 1))

    def half(self, k):
        self.across(k).wait_recv()
        return self.terms[(self.y + k) % 4, self.c].astype(F32) + self.got[k].astype(F32)

    def pass_far(self):
        self.mid[1] = self.half(2).astype(BF16)
        for at in range(2):
            self.far(at).start()

    def pass_on(self, k):
        at = (k - 1) // 2
        total = self.half(k)
        self.far(at).wait_recv()
        came = self.relay[at].astype(F32)
        upper, lower = total[0 : SEQ // 2], total[SEQ // 2 :]
        if at == 0:
            upper = upper + came
        else:
            lower = lower + came
        self.mid[k - 1, 0 : SEQ // 2] = upper.astype(BF16)
        self.mid[k - 1, SEQ // 2 :] = lower.astype(BF16)
        self.along(k).start()

    def keep(self):
        self.out[...] = self.half(0)

    def end(self):
        total = self.out[...]
        remote(self.last, self.last, self.send.at[1], self.recv.at[6], sibling()).wait_recv()
        self.out[...] = total + self.last[0].astype(F32) + self.last[1].astype(F32)

    def finish(self):
        for at, here in ((0, self.got), (1, self.mid)):
            remote(here, here, self.send.at[at], self.recv.at[6], sibling()).wait_send()


class Members:
    def __init__(self, src, buf, send, recv):
        self.src, self.buf, self.send, self.recv = src, buf, send.at[0], recv.at[0]
        _, _, y, c = place()
        self.rank = y * 2 + c

    def start(self):
        for k in range(1, GROUP):
            target, q = group_partner(k)
            remote(self.src(q), self.buf.at[self.rank], self.send, self.recv, target).start()

    def others(self):
        here = self.buf.at[pl.ds(0, GROUP - 1)]
        return remote(here, here, self.send, self.recv, sibling())

    def finish(self):
        self.others().wait_recv()

    def sent(self):
        self.others().wait_send()


def layer_kernel(
    hid, inw, gain_in, taps, bias_in, dt_in, a_in, skip_in, inner_in, outw, grd, lengths, owners,
    mixed, in_grad, dinw, dvecs, doutw,
    vectors, heads_in, tap_rows,
    split, joined, block, gblock, params, outl, placed, live_grd,
    wx, wg, praw, plane, hall, gall, low, proj, act, step_rows, steps, totals, values, slopes, scores, heads_out, dgated, ow, par, head, skip, sums, slots, wide,
    gated, dproj, d_steps, d_mine, d_other, d_in, dwx, dwg, dow, dws, small,
    gb, mb, tb, lb, fb, gd, md, td, ld, fd, gx, mx, lx, fx, gg, mg, lg, fg, gl, ml, ll, fl, gs, ms, ls, fs,
    swapped, cut, rows_in, gcut, grows_in, zs, xs, part, small_all,
    a_s, a_r, wx_s, wx_r, wg_s, wg_r, p_s, p_r, l_s, l_r, h_s, h_r, g_s, g_r, n_s, n_r, v_s, v_r, u_s, u_r,
    b_s, b_r, d_s, d_r, rx_s, rx_r, rg_s, rg_r, rl_s, rl_r, rs_s, rs_r, rr_s, rr_r, rq_s, rq_r,
    sz_s, sz_r, sx_s, sx_r, sg_s, sg_r, swap_s, swap_r,
):
    z, x, y, c = place()
    rank = y * 2 + c
    me = lax.axis_index("fsdp")
    partners = plane_partners() + group_partners()
    moves = swap_to() != me
    for p in partners:
        signal(p)

    @pl.when(moves)
    def _():
        signal(swap_to())
        signal(swap_from())

    vectors[...] = jnp.zeros_like(vectors)
    heads_in[...] = jnp.zeros_like(heads_in)
    tap_rows[...] = jnp.zeros_like(tap_rows)
    vectors[0:1, 0:KIN] = gain_in[...].astype(F32)[None, :]
    vectors[0:1, KIN : KIN + 26] = bias_in[...].astype(F32)[None, :]
    vectors[0:1, KIN + 26 : KIN + 26 + KOUT] = inner_in[...].astype(F32)[None, :]
    for i, line in enumerate((dt_in, a_in, skip_in)):
        heads_in[i : i + 1, 0:HEADS] = line[...][None, :]
    tap_rows[0:4, 0:26] = taps[...].astype(F32)
    col_steps = inw[:, STEP : STEP + HEADS]
    steps_low = dot_tn(col_steps, ones(iota((KIN, 128), 0) == iota((KIN, 128), 1)))
    steps_high = dot_tn(col_steps, ones(iota((KIN, 128), 0) + 16 == iota((KIN, 128), 1)))
    rest = jnp.zeros((4, 128), F32)

    def padded(span, extra):
        return jnp.concatenate([inw[:, span].astype(F32), extra], axis=0).astype(BF16)

    vector_cols = [padded(slice(2 * INNER + 128 * i, 2 * INNER + 128 * (i + 1)), rest) for i in range(2)]
    for q in range(GROUP):
        at = q * OWN
        two = jnp.concatenate([steps_high[at + 4 : at + OWN], jnp.zeros((2, 128), F32)], axis=0)
        extra = jnp.concatenate([tap_rows[0:4], vectors[0:4], steps_low[at : at + 4] + two], axis=1)
        split[q, :, 0:GW] = padded(slice(INNER + q * GW, INNER + (q + 1) * GW), extra)
        split[q, :, GW:CW] = vector_cols[q % 2]
        split[q, :, GA:COLS] = padded(slice(q * GW, (q + 1) * GW), jnp.zeros((4, GW), F32))
    end = outw[16:24, :].astype(F32)
    tail = jnp.concatenate([end[:, 0 : D // 2], end[:, D // 2 :]], axis=0).astype(BF16)
    outl[0] = outw[0:16, 0:WIDE]
    outl[1, :, 0 : D - WIDE] = outw[0:16, WIDE:D]
    outl[1, :, D - WIDE :] = tail

    @pl.when(moves)
    def _():
        pl.semaphore_wait(pltpu.get_barrier_semaphore(), len(partners) + 2)

    @pl.when(jnp.logical_not(moves))
    def _():
        pl.semaphore_wait(pltpu.get_barrier_semaphore(), len(partners))

    cuts = Members(lambda q: split.at[q], joined, a_s, a_r)
    cuts.start()
    swap = remote(outl, placed, swap_s.at[0], swap_r.at[0], swap_to())
    swap_back = remote(fl, swapped, swap_s.at[1], swap_r.at[1], swap_from())

    @pl.when(moves)
    def _():
        swap.start()

    joined[rank] = split[rank]
    length = jnp.sum(jnp.where(owners[...][None, :] == me, lengths[...][None, :], 0), axis=1, keepdims=True)
    live = iota((SEQ, 1), 0) < length
    live_grd[...] = jnp.where(live, grd[...].astype(F32), 0.0).astype(BF16)
    own_heads(heads_in, rank, head, skip)

    hidden = GroupGather(hall, hid, h_s, h_r)
    grads = GroupGather(gall, live_grd, g_s, g_r)
    first_w = PlaneGather(wx, lambda h: block.at[h], wx_s, wx_r, 2)
    gate_w = PlaneGather(wg, lambda h: gblock.at[h], wg_s, wg_r, 2)
    vecs = PlaneGather(praw, lambda h: params, p_s, p_r, 1)
    lines = PlaneGather(plane, lambda h: placed.at[h], l_s, l_r, 2)

    hidden.start()
    cuts.finish()
    row, col = iota((128, 128), 0), iota((128, 128), 1)
    member, line = col // 16, col % 16
    spot = jnp.where(line < KIN, member * KIN + line, 96 + member * 4 + line - KIN)
    both = dot(ones(spot == row), joined[...].reshape(128, COLS)).astype(BF16)
    for h in range(2):
        block[h] = both[48 * h : 48 * h + 48, 0:GA]
        gblock[h] = both[48 * h : 48 * h + 48, GA:COLS]
    params[...] = both[96:128, 0:384]
    vecs.start()
    first_w.start()
    grads.start()
    wx[z, x] = block[...]
    wg[z, x] = gblock[...]
    praw[z, x, 0] = params[...]
    hall[y, c] = hid[...]
    gall[y, c] = live_grd[...]
    vecs.forward()
    first_w.forward()
    gate_w.start()

    @pl.when(moves)
    def _():
        swap.wait_recv()

    @pl.when(jnp.logical_not(moves))
    def _():
        placed[...] = outl[...]

    lines.start()
    plane[z, x] = placed[...]
    hidden.forward(1)
    hidden.forward(3)
    vecs.relay()
    first_w.relay()
    vecs.finish()
    unpack_params(praw, rank, c, par, step_rows)
    gate_w.forward()
    lines.forward()

    def chunk(i):
        return pl.ds(pl.multiple_of(i * 256, 256), 256)

    def turn(i):
        return i + i // 2 * (5 - 2 * i)

    def in_turn(i):
        return (y + turn(i)) % 4

    def vector_copy(i):
        here = act.at[c, chunk(in_turn(i))]
        return remote(here, here, v_s.at[0], v_r.at[i], sibling())

    def vector_arrival(i):
        here = act.at[1 - c, chunk(in_turn(i))]
        return remote(here, here, v_s.at[0], v_r.at[i], sibling())

    def prepare(at):
        for core in range(2):
            h = hall[at, core].astype(F32)
            scale = lax.rsqrt(jnp.mean(h * h, axis=1, keepdims=True) + EPSILON)
            rows = pl.ds(pl.multiple_of(at * 256 + core * SEQ, SEQ), SEQ)
            low[rows, :] = (h * scale * par[0:1, :]).astype(BF16)
        proj[chunk(at), ST:] = dot_nt(low[chunk(at), :], step_rows[...])
        for core in range(2):
            steps_forward(at * 2 + core, proj, head, steps, totals)

    def forward(i, carry):
        @pl.when(i == 1)
        def _():
            hidden.arrived(1)
            hidden.forward(2)

        @pl.when(i == 2)
        def _():
            hidden.arrived(3)
            gate_w.relay()

        @pl.when(i == 3)
        def _():
            hidden.arrived(2)
            lines.relay()
            grads.forward(1)
            grads.forward(3)

        @pl.when(jnp.logical_and(i > 0, i < 4))
        def _():
            prepare(in_turn(i))

        @pl.when(i < 4)
        def _():
            at = in_turn(i)
            rows = chunk(at)
            proj[rows, 0:GA] = dot(low[rows, :], wx[...].reshape(D, GA))
            for core in range(2):
                vector_forward(at * 2 + core, c, proj, act, slopes, par)
            vector_copy(i).start()

        @pl.when(i > 0)
        def _():
            vector_arrival(i - 1).wait_recv()
            at = in_turn(i - 1)
            for core in range(2):
                mix_forward(at * 2 + core, proj, act, par, skip, steps, totals, values, slopes, scores, heads_out)

        return carry

    hidden.arrived(0)
    prepare(y)
    first_w.finish()
    lax.fori_loop(0, 5, forward, 0)
    gate_w.finish()

    def project_gate(i, carry):
        proj[chunk(i), GA:COLS] = dot(low[chunk(i), :], wg[...].reshape(D, GW))
        return carry

    lax.fori_loop(0, ROWS // 256, project_gate, 0)

    def weighed(b, acc):
        return weigh(b, proj, par, heads_out, gated, acc)

    wide[...] = lax.fori_loop(0, GROUP, weighed, jnp.zeros((SEQ, SEQ), F32))
    lines.finish()
    unfold_out_weight(plane, ow)
    grads.forward(2)
    grads.arrived(0)

    def pull(i, carry):
        @pl.when(i == 1)
        def _():
            grads.arrived(1)

        @pl.when(i == 2)
        def _():
            grads.arrived(3)

        @pl.when(i == 3)
        def _():
            grads.arrived(2)

        at = in_turn(i)
        dgated[chunk(at), :] = dot_nt(gall[at].reshape(256, D), ow[...])
        return carry

    lax.fori_loop(0, 4, pull, 0)
    acc = lax.fori_loop(0, GROUP, lambda b, acc: norm_sums(b, gated, dgated, acc), wide[...])
    sums[...] = acc.T[0:16, :]
    norms = Members(lambda q: sums, slots, n_s, n_r)
    norms.start()
    slots[rank] = sums[...]
    small[...] = jnp.zeros_like(small)
    hidden.sent()
    branch = hall
    branches = GroupReduce(branch, gb, mb, tb, lb, fb, b_s, b_r)

    def out_term(i, carry):
        at = in_turn(3 - i)
        branch[at] = dot(gated[chunk(at), :], ow[...]).astype(BF16).reshape(2, SEQ, D)
        branches.across(turn(3 - i)).start()
        return carry

    lax.fori_loop(0, 4, out_term, 0)
    norms.finish()
    total = slots[0]
    for q in range(1, GROUP):
        total = total + slots[q]
    wide[...] = jnp.concatenate([total, jnp.zeros((SEQ - 16, SEQ), F32)], axis=0).T

    def norms_back(b, carry):
        norm_back(b, proj, par, wide, heads_out, dgated, gated, dproj, small)
        return carry

    branches.pass_far()
    lax.fori_loop(0, GROUP, norms_back, 0)

    d_low = gall
    lowers = GroupReduce(d_low, gd, md, td, ld, fd, d_s, d_r)
    sums_x = PlaneReduce(dwx, gx, mx, lx, fx, rx_s, rx_r)
    sums_g = PlaneReduce(dwg, gg, mg, lg, fg, rg_s, rg_r)
    sums_l = PlaneReduce(dow, gl, ml, ll, fl, rl_s, rl_r)
    sums_s = PlaneReduce(dws, gs, ms, ls, fs, rs_s, rs_r, 1)
    cut_rows = Members(lambda q: cut.at[q], rows_in, rr_s, rr_r)
    gate_rows = Members(lambda q: gcut.at[q], grows_in, rq_s, rq_r)
    all_small = Members(lambda q: small_all.at[rank], small_all, sg_s, sg_r)

    def small_z(k):
        return remote(small, zs.at[z], sz_s.at[0], sz_r.at[0], on_z(k))

    def small_x(k):
        return remote(part, xs.at[x], sx_s.at[0], sx_r.at[0], on_x(k))

    def small_all_of(buf, send, recv):
        here = buf.at[pl.ds(0, 3)]
        return remote(here, here, send.at[0], recv.at[0], on_z(1))

    def slab(k, span):
        at = (z + k) % 4
        own = low[:, pl.ds(pl.multiple_of(at * GW, GW), GW)]
        return at, dot_tn(own, dproj[:, span]).astype(BF16).reshape(4, 2, 48, span.stop - span.start)

    out = dot_tn(gated[...], gall[...].reshape(ROWS, D))
    for j in range(16):
        piece = out[j * KOUT : (j + 1) * KOUT]
        tail = jnp.concatenate([piece[16:24, 0 : D // 2], piece[16:24, D // 2 :]], axis=0)
        fold = jnp.concatenate([piece[0:16], tail], axis=1).astype(BF16)
        for h in range(2):
            dow[j % 8 // 2, j // 8 * 2 + j % 2, h] = fold[:, h * WIDE : (h + 1) * WIDE]
    sums_l.start()
    for k in (2, 1, 3, 0):
        at, rows = slab(k, slice(GA, COLS))
        dwg[at] = rows
        if k:
            sums_g.first(1, k).start()
    for k in (2, 1, 3):
        sums_g.first(0, k).start()
    grads.sent()

    def other_copy(i):
        rows = chunk(in_turn(3 - i))
        return remote(d_other.at[rows], d_in.at[rows], u_s.at[0], u_r.at[i], sibling())

    def lower_back(k):
        at = (y + k) % 4
        rows = chunk(at)
        back = dot_nt(dproj[rows, 0:GA], wx[...].reshape(D, GA))
        back = back + dot_nt(dproj[rows, GA:COLS], wg[...].reshape(D, GW))
        back = back + dot(d_steps[rows, :], step_rows[...])
        d_low[at] = back.astype(BF16).reshape(2, SEQ, D)
        lowers.across(k).start()

    def backward(i, carry):
        @pl.when(i < 4)
        def _():
            at = in_turn(3 - i)
            for core in range(2):
                mix_back(
                    at * 2 + core, c, proj, act, par, head, skip, steps, totals, values, slopes, scores, dgated, dproj,
                    d_steps, small, d_mine, d_other,
                )
            other_copy(i).start()

        @pl.when(i == 0)
        def _():
            branches.pass_on(3)
            branches.pass_on(1)
            branches.keep()

        @pl.when(i > 0)
        def _():
            other_copy(i - 1).wait_recv()
            at = in_turn(4 - i)
            for core in range(2):
                vector_back(at * 2 + core, proj, par, slopes, d_mine, d_in, dproj, small)

        @pl.when(i == 4)
        def _():
            sums_l.middle()

        return carry

    lax.fori_loop(0, 5, backward, 0)
    for k in (1, 2, 3):
        small_z(k).start()
    zs[z] = small[...]
    for k in (2, 1, 3, 0):
        at, rows = slab(k, slice(0, GA))
        dwx[at] = rows
        if k:
            sums_x.first(1, k).start()
    for k in (2, 1, 3):
        sums_x.first(0, k).start()
    sums_g.middle()
    steps_back = dot_tn(d_steps[...], low[...])
    for r in range(16):
        own = jnp.concatenate([steps_back[0:16, r * 96 : (r + 1) * 96], jnp.zeros((16, 32), F32)], axis=1)
        dws[r // 4, r % 4, 0] = own.astype(BF16)
    sums_s.start()

    def lower_backs(i, carry):
        lower_back(turn(3 - i))

        @pl.when(i == 1)
        def _():
            lowers.pass_far()

        return carry

    lax.fori_loop(0, 4, lower_backs, 0)
    lowers.pass_on(3)
    lowers.pass_on(1)
    small_all_of(zs, sz_s, sz_r).wait_recv()
    part[...] = ((zs[0] + zs[1]) + zs[2]) + zs[3]
    xs[x] = part[...]
    for k in (1, 2, 3):
        small_x(k).start()
    sums_x.middle()
    sums_s.middle()
    lowers.keep()
    sums_g.end()
    for q in range(GROUP):
        gcut[q] = jnp.zeros((16, GW), BF16)
        gcut[q, 0:KIN, :] = fg[q // 4, q % 4 * KIN : (q % 4 + 1) * KIN, :].astype(BF16)
    gate_rows.start()
    grows_in[rank] = gcut[rank]
    sums_l.end()

    @pl.when(moves)
    def _():
        swap_back.start()

    small_all_of(xs, sx_s, sx_r).wait_recv()
    small_all[rank] = ((xs[0] + xs[1]) + xs[2]) + xs[3]
    all_small.start()
    branches.end()
    h32 = hid[...].astype(F32)
    inverse = lax.rsqrt(column(rank, wide[...]) * (1.0 / INNER) + EPSILON)
    mixed[...] = (h32 + jnp.where(live, inverse * fb[...], 0.0)).astype(BF16)
    sums_s.end()
    sums_x.end()
    step_cols = dot_tn(fs[0, 0:8], ones(iota((8, 128), 0) == iota((8, 128), 1), F32), HIGHEST)
    for q in range(GROUP):
        at = q % 4 * KIN
        cut[q] = jnp.zeros((16, CW + 128), BF16)
        cut[q, 0:KIN, 0:CW] = fx[q // 4, at : at + KIN, :].astype(BF16)
        cut[q, 0:KIN, CW:] = step_cols[q * KIN : (q + 1) * KIN].astype(BF16)
    cut_rows.start()
    rows_in[rank] = cut[rank]
    all_small.finish()
    finish_small(small_all, dvecs)

    @pl.when(moves)
    def _():
        swap_back.wait_recv()

    @pl.when(jnp.logical_not(moves))
    def _():
        swapped[...] = fl[...]

    doutw[0:16, 0:WIDE] = swapped[0]
    doutw[0:16, WIDE:D] = swapped[1, :, 0 : D - WIDE]
    doutw[16:24, 0 : D // 2] = swapped[1, 0:8, D - WIDE :]
    doutw[16:24, D // 2 : D] = swapped[1, 8:16, D - WIDE :]
    lowers.end()
    scale = lax.rsqrt(jnp.mean(h32 * h32, axis=1, keepdims=True) + EPSILON)
    normed = h32 * scale
    d_normed = fd[...] * par[0:1, :]
    through = scale * (d_normed - normed * jnp.mean(d_normed * normed, axis=1, keepdims=True))
    in_grad[...] = (grd[...].astype(F32) + through).astype(BF16)
    gate_rows.finish()
    gate_total = finish_gate(grows_in, inw, dinw)
    cut_rows.finish()
    finish_rows(rows_in, gate_total, inw, vectors, dinw, dvecs)
    for gone in (first_w, gate_w, vecs, lines, cuts, norms, cut_rows, gate_rows, all_small):
        gone.sent()
    for gone in (branches, lowers, sums_x, sums_g, sums_l, sums_s):
        gone.finish()
    small_all_of(zs, sz_s, sz_r).wait_send()
    small_all_of(xs, sx_s, sx_r).wait_send()
    remote(act.at[c], act.at[c], v_s.at[0], v_r.at[0], sibling()).wait_send()
    remote(d_other, d_other, u_s.at[0], u_r.at[0], sibling()).wait_send()

    @pl.when(moves)
    def _():
        swap.wait_send()
        swap_back.wait_send()


def finish_small(small, dvecs):
    me = lax.axis_index("fsdp")
    conv = jnp.zeros((8, 128), F32)
    inner = jnp.zeros((8, 128), F32)
    common = [jnp.zeros((8, 128), F32), jnp.zeros((8, 128), F32)]
    row, col = iota((GW, 128), 0), iota((GW, 128), 1)
    heads = ones(row // 64 == col, F32)
    dvecs[...] = jnp.zeros_like(dvecs)
    for q in range(GROUP):
        part = small[q, :, 0:GW]
        conv = conv + dot(part, ones(row + q * GW == col + 26 * me, F32), HIGHEST)
        inner = inner + dot(part, ones(row + q * GW == col + KOUT * me, F32), HIGHEST)
        common[q % 2] = common[q % 2] + small[q, :, GW:CW]
        span = slice(q * OWN, (q + 1) * OWN)
        dvecs[3:4, span] = small[q, 7:8, 0:OWN]
        dvecs[4:5, span] = small[q, 7:8, 128 : 128 + OWN]
        dvecs[5:6, span] = dot(part, heads, HIGHEST)[6:7, 0:OWN]
    row, col = iota((256, 128), 0), iota((256, 128), 1)
    conv = conv + dot(jnp.concatenate(common, axis=1), ones(row + INNER == col + 26 * me, F32), HIGHEST)
    dvecs[1:2] = conv[4:5]
    dvecs[2:3] = inner[5:6]
    dvecs[8:12] = conv[0:4]


def finish_gate(gate_rows, inw, dinw):
    for q in range(GROUP):
        dinw[:, q * GW : (q + 1) * GW] = gate_rows[q].astype(F32)[0:KIN]
    return jnp.sum(dinw[:, 0:INNER] * inw[:, 0:INNER].astype(F32), axis=1, keepdims=True)


def finish_rows(rows, gate_total, inw, vectors, dinw, dvecs):
    shared = [jnp.zeros((KIN, 128), F32), jnp.zeros((KIN, 128), F32)]
    for q in range(GROUP):
        own = rows[q].astype(F32)[0:KIN]
        dinw[:, INNER + q * GW : INNER + (q + 1) * GW] = own[:, 0:GW]
        dinw[:, STEP + q * OWN : STEP + (q + 1) * OWN] = own[:, CW : CW + OWN]
        shared[q % 2] = shared[q % 2] + own[:, GW:CW]
    dinw[:, 2 * INNER : 2 * INNER + 128] = shared[0]
    dinw[:, 2 * INNER + 128 : STEP] = shared[1]
    total = gate_total + jnp.sum(dinw[:, INNER:] * inw[:, INNER:].astype(F32), axis=1, keepdims=True)
    spread = jnp.where(iota((KIN, 128), 0) == iota((KIN, 128), 1), total, 0.0)
    gain = jnp.where(iota((1, 128), 1) < KIN, vectors[0:1], 1.0)
    dvecs[0:1] = jnp.sum(spread, axis=0, keepdims=True) / gain


def emit_kernel(mixed, in_grad, dinw, doutw, dvecs, *outs):
    (mixed_out, grad_out, dinw_out, dgain, conv_out, dbias, ddt, da_log, dskip, dinner, doutw_out) = outs
    for given, out in ((mixed, mixed_out), (in_grad, grad_out), (dinw, dinw_out), (doutw, doutw_out)):
        out[...] = given[...]
    for i, line in enumerate((dgain, dbias, dinner, ddt, da_log, dskip)):
        line[...] = dvecs[i, 0 : line.shape[0]]
    conv_out[...] = dvecs[8:12, 0:26]


def emit(*given):
    vmem = pl.BlockSpec(memory_space=pltpu.VMEM)
    shape = jax.ShapeDtypeStruct
    line = [shape((n,), F32) for n in (KIN, 26, HEADS, HEADS, HEADS, KOUT)]
    return pl.pallas_call(
        emit_kernel,
        name="emit",
        out_shape=(*OUT_SHAPES[0:3], line[0], shape((4, 26), F32), *line[1:], OUT_SHAPES[4]),
        in_specs=[vmem] * 5,
        out_specs=(vmem,) * 11,
        compiler_params=pltpu.CompilerParams(vmem_limit_bytes=VMEM_LIMIT),
    )(*given)


def layer(*given):
    vmem, vm = pl.BlockSpec(memory_space=pltpu.VMEM), pltpu.VMEM

    def dma(*dims):
        return pltpu.SemaphoreType.DMA(dims)

    def plane_reduce(halves, rows, cols):
        block = (rows, cols)
        return [
            vm((halves, 3, 4) + block, BF16), vm((halves, 3) + block, BF16), vm((halves, 3) + block, BF16),
            vm((halves,) + block, F32),
        ]

    one, group = [dma(1)] * 2, [dma(2), dma(8)]
    group_reduce = [
        vm((4, SEQ, D), BF16), vm((3, SEQ, D), BF16), vm((2, SEQ // 2, D), BF16), vm((2, SEQ, D), BF16), vm((SEQ, D), F32)
    ]
    gather, two = [dma(2, 2), dma(2, 8)], [dma(2, 2)] * 2
    return pl.pallas_call(
        layer_kernel,
        name="layer",
        out_shape=OUT_SHAPES,
        in_specs=[vmem] * len(given),
        out_specs=(vmem,) * len(OUT_SHAPES),
        scratch_shapes=[
            vm((8, 128), F32), vm((8, 128), F32), vm((8, 128), F32),
            vm((GROUP, 16, COLS), BF16), vm((GROUP, 16, COLS), BF16), vm((2, 48, GA), BF16), vm((2, 48, GW), BF16),
            vm((32, 384), BF16), vm((2, 16, WIDE), BF16), vm((2, 16, WIDE), BF16), vm((SEQ, D), BF16),
            vm((4, 4, 2, 48, GA), BF16), vm((4, 4, 2, 48, GW), BF16), vm((4, 4, 1, 32, 384), BF16),
            vm((4, 4, 2, 16, WIDE), BF16), vm((4, 2, SEQ, D), BF16), vm((4, 2, SEQ, D), BF16),
            vm((ROWS, D), BF16), vm((ROWS, COLS + 128), F32), vm((2, ROWS, 128), F32), vm((128, D), BF16),
            vm((ROWS, 128), F32), vm((ROWS, 128), F32), vm((ROWS, GW), F32), vm((ROWS, CW), F32), vm((GROUP, SEQ, SEQ), F32),
            vm((ROWS, GW), F32), vm((ROWS, GW), F32), vm((GW, D), BF16),
            vm((8, D), F32), vm((8, 128), F32), vm((1, GW), F32),
            vm((16, SEQ), F32), vm((GROUP, 16, SEQ), F32), vm((SEQ, SEQ), F32),
            vm((ROWS, GW), BF16), vm((ROWS, COLS), BF16), vm((ROWS, 128), BF16),
            vm((ROWS, 128), F32), vm((ROWS, 128), F32), vm((ROWS, 128), F32),
            vm((4, 4, 2, 48, GA), BF16), vm((4, 4, 2, 48, GW), BF16), vm((4, 4, 2, 16, WIDE), BF16),
            vm((4, 4, 1, 16, 128), BF16), vm((8, CW), F32),
            *group_reduce, *group_reduce, *plane_reduce(2, 48, GA), *plane_reduce(2, 48, GW),
            *plane_reduce(2, 16, WIDE), *plane_reduce(1, 16, 128),
            vm((2, 16, WIDE), F32), vm((GROUP, 16, CW + 128), BF16), vm((GROUP, 16, CW + 128), BF16),
            vm((GROUP, 16, GW), BF16), vm((GROUP, 16, GW), BF16),
            vm((4, 8, CW), F32), vm((4, 8, CW), F32), vm((8, CW), F32), vm((GROUP, 8, CW), F32),
            *one, *gather, *gather, dma(1, 2), dma(1, 8), *gather, *group, *group, *one, dma(1), dma(4), dma(1), dma(4),
            *group, *group, *two, *two, *two, dma(1, 2), dma(1, 2), *one, *one, *one, *one, *one, dma(2), dma(2),
        ],
        compiler_params=pltpu.CompilerParams(collective_id=0, has_side_effects=True, vmem_limit_bytes=VMEM_LIMIT),
    )(*given)


OUT_SHAPES = (
    jax.ShapeDtypeStruct((SEQ, D), BF16),
    jax.ShapeDtypeStruct((SEQ, D), BF16),
    jax.ShapeDtypeStruct((KIN, STEP + HEADS), F32),
    jax.ShapeDtypeStruct((16, 128), F32),
    jax.ShapeDtypeStruct((KOUT, D), F32),
)


def body(
    hidden, in_weight, norm_gain, conv_weight, conv_bias, dt_bias, a_log, skip, inner_gain, out_weight, out_grad,
    seq_lengths, seq_owner,
):
    mixed, in_grad, dinw, dvecs, doutw = layer(
        hidden, in_weight, norm_gain, conv_weight.T, conv_bias, dt_bias, a_log, skip, inner_gain, out_weight, out_grad,
        seq_lengths, seq_owner,
    )
    outs = list(emit(mixed, in_grad, dinw, doutw, dvecs))
    outs[4] = outs[4].T
    return tuple(outs)


def solution(mesh):
    rows, line, whole = P("fsdp", None), P("fsdp"), P()
    return jax.shard_map(
        body,
        mesh=mesh,
        in_specs=(rows, rows, line, rows, line, whole, whole, whole, line, rows, rows, whole, whole),
        out_specs=(rows, rows, rows, line, rows, line, whole, whole, whole, line, rows),
        check_vma=False,
    )
```
